32 devices in a mesh: dir: 2 (over x), group: 4 (over y, core), dp: 4 (over z).
Axes of the slice: x: 2, y: 2, z: 4, core: 2. Of those that a mesh axis runs over, the one named last changes fastest.
Arguments:
- chars: int32 [2, 384, 24], P('dir', ('group', 'dp')), may hold values from 0 to 274
- targets: int32 [2, 384, 24], P('dir', ('group', 'dp')), may hold values from 0 to 274
- resets: int32 [2, 384, 24], P('dir', ('group', 'dp')), may hold values 0 or 1
- word_pos: int32 [2, 384, 8], P('dir', ('group', 'dp')), may hold values from -1 to 23, as said below
- h_init: float32 [2, 384, 2048], P('dir', ('group', 'dp')), may hold values from -0.9 to 0.9
- c_init: float32 [2, 384, 2048], P('dir', ('group', 'dp')), may hold values from -5 to 5
- word_grad: bfloat16 [384, 8, 4096], P(('group', 'dp'), None, 'dir'), may hold values from -0.119628906 to 0.119628906
- w_emb: float32 [2, 275, 100], P('dir'), may hold values from -5 to 5
- w_in: float32 [2, 100, 8192], P('dir', None, 'group'), may hold values from -0.625 to 0.625
- w_rec: float32 [2, 2048, 8192], P('dir', 'group'), may hold values from -0.125 to 0.125
- b_rec: float32 [2, 8192], P('dir', 'group'), may hold values from -3 to 3
- w_dec: float32 [2, 2048, 275], P('dir', 'group'), may hold values from -0.5 to 0.5
- b_dec: float32 [2, 275], P('dir'), may hold values from -4 to 4
- mom_emb: float32 [2, 275, 100], P('dir'), may hold values from -0.00048828125 to 0.00048828125
- mom_in: float32 [2, 100, 8192], P('dir', None, 'group'), may hold values from -0.00048828125 to 0.00048828125
- mom_rec: float32 [2, 2048, 8192], P('dir', 'group'), may hold values from -0.00048828125 to 0.00048828125
- mom_bias: float32 [2, 8192], P('dir', 'group'), may hold values from -0.00048828125 to 0.00048828125
- mom_dec: float32 [2, 2048, 275], P('dir', 'group'), may hold values from -0.00048828125 to 0.00048828125
- mom_dbias: float32 [2, 275], P('dir'), may hold values from -0.00048828125 to 0.00048828125
Outputs:
- losses: float32 [2], P('dir')
- word_vectors: bfloat16 [384, 8, 4096], P(('group', 'dp'), 'dir')
- grad_h: float32 [2, 384, 2048], P('dir', ('group', 'dp'))
- grad_c: float32 [2, 384, 2048], P('dir', ('group', 'dp'))
- grad_emb: float32 [2, 275, 100], P('dir')
- grad_in: float32 [2, 100, 8192], P('dir', None, 'group')
- grad_rec: float32 [2, 2048, 8192], P('dir', 'group')
- grad_bias: float32 [2, 8192], P('dir', 'group')
- grad_dec: float32 [2, 2048, 275], P('dir', 'group')
- grad_dbias: float32 [2, 275], P('dir')
- next_mom_emb: float32 [2, 275, 100], P('dir')
- next_mom_in: float32 [2, 100, 8192], P('dir', None, 'group')
- next_mom_rec: float32 [2, 2048, 8192], P('dir', 'group')
- next_mom_bias: float32 [2, 8192], P('dir', 'group')
- next_mom_dec: float32 [2, 2048, 275], P('dir', 'group')
- next_mom_dbias: float32 [2, 275], P('dir')
The draws below stay inside these ranges and needn't reach their ends.
Inputs may be any that keep to these rules, and one draw needn't show every extreme that they name: `word_pos`: for each model and segment the used slots come first and name distinct positions in increasing order; the other slots hold -1. Both models use the same number of slots in a segment; the first segment of each aligned block of 24 segments uses all 8.
All inputs are finite; a program needn't handle non-finite values. No bound on the sum of `resets` on one device may be relied on, other than what follows from the above.
Results may differ from the reference program's by a relative error of at most 0.012.
Values may be sent and summed in bfloat16 or wider, within the bound.
A program may use at most 256 MiB of HBM per device.

```python
import math
import jax
import jax.numpy as jnp
import numpy as np
from jax import lax

H = 2048
E = 100
V = 275
SEG_DEV = 24
SEG_LEN = 24
WPS = 8
SEGS = 384


def draw_word_pos(key, part):
    count_key = jax.random.fold_in(key, 101)
    counts = jax.random.randint(count_key, (SEGS,), 2, WPS + 1)
    segment_ids = jnp.arange(SEGS, dtype=jnp.int32)
    counts = jnp.where(segment_ids % SEG_DEV == 0, WPS, counts)
    slot_ids = jnp.arange(WPS, dtype=jnp.int32)
    blocks = []
    for direction in range(2):
        scores = jax.random.randint(jax.random.fold_in(key, 200 + direction), (SEGS, SEG_LEN), 0, 4096)
        scores = scores * SEG_LEN + jnp.arange(SEG_LEN, dtype=jnp.int32)[None, :]
        ranking = jnp.argsort(scores, axis=1, stable=True).astype(jnp.int32)
        chosen = jnp.sort(ranking[:, :WPS], axis=1)
        blocks.append(jnp.where(slot_ids[None, :] < counts[:, None], chosen, -1))
    return jnp.stack(blocks).astype(jnp.int32)


def draw_b_rec(key, part):
    key = jax.random.fold_in(key, 7)
    base = 0.5 * jax.random.normal(jax.random.fold_in(key, 1), (2, 4 * H), jnp.float32)
    base = jnp.clip(base, -3.0, 3.0)
    forget = jax.random.uniform(jax.random.fold_in(key, 2), (2, 4 * H), jnp.float32, 2.5, 3.0)
    column = jnp.arange(4 * H, dtype=jnp.int32)
    in_forget = (column >= H) & (column < 2 * H)
    return jnp.where(in_forget[None, :], forget, base).astype(jnp.float32)


def place_ends(drawn, key, low, largest):
    longest = drawn.shape.index(max(drawn.shape))
    spots = []
    for shift in (0, 1):
        where = [jax.random.randint(jax.random.fold_in(key, axis), (), 0, length) for axis, length in enumerate(drawn.shape)]
        where[longest] = (where[longest] + shift) % drawn.shape[longest]
        spots.append(tuple(where))
    return drawn.at[spots[0]].set(low).at[spots[1]].set(largest)


def block_scale(rng, dims, pieces, least, largest):
    factor_of = 1.0
    for dim, parts in pieces:
        steps = jax.random.uniform(jax.random.fold_in(jax.random.fold_in(rng, 6), dim), (parts,), jnp.float32, least / len(pieces), largest / len(pieces))
        factor_of = factor_of * jnp.repeat(jnp.exp(steps), dims[dim] // parts).reshape((-1,) + (1,) * (len(dims) - 1 - dim))
    return factor_of


def rank_bounds(count, lean):
    weights = [(1 << 20) // math.isqrt(grade ** lean) + 1 for grade in range(1, count + 1)]
    spread = 1 + sum(weights) // (1 << 30)
    return np.cumsum(np.array([max(1, weight // spread) for weight in weights]))


def skewed_ids(key, extent, count, slope):
    grid = rank_bounds(count, slope)
    ticket = jax.random.randint(jax.random.fold_in(key, 1), extent, 0, int(grid[count - 1]))
    rank = jnp.searchsorted(jnp.asarray(grid, jnp.int32), ticket, side="right")
    return jax.random.permutation(jax.random.fold_in(key, 2), count)[rank].astype(jnp.int32)


def gaussian(key, extent, width, reach, split=(), kind=jnp.bfloat16):
    array = width * jax.random.normal(key, extent, jnp.float32)
    if split:
        array = array * block_scale(key, extent, split, -0.22, 0.18)
    return jnp.clip(array, -reach, reach).astype(kind)


def setup_inputs(seed: int = 0) -> dict:
    streams_of = jax.random.split(jax.random.key(seed), 20)
    chars = place_ends(skewed_ids(streams_of[0], (2, SEGS, SEG_LEN), V, 2), jax.random.fold_in(streams_of[0], 3), 0, V - 1).astype(jnp.int32)
    targets = place_ends(skewed_ids(streams_of[1], (2, SEGS, SEG_LEN), V, 2), jax.random.fold_in(streams_of[1], 3), 0, V - 1).astype(jnp.int32)
    resets = place_ends((jax.random.randint(streams_of[2], (2, SEGS, SEG_LEN), 0, 64) < 1).astype(jnp.int32), jax.random.fold_in(streams_of[2], 1), 0, 1)
    word_pos = draw_word_pos(jax.random.fold_in(streams_of[19], 71), 0)
    h_init = jnp.clip(jax.random.uniform(streams_of[4], (2, SEGS, H), jnp.float32, -0.9, 0.9) * block_scale(streams_of[4], (2, SEGS, H), ((0, 2), (1, 16)), -0.4, 0.0), -0.9, 0.9)
    c_init = gaussian(streams_of[5], (2, SEGS, H), 1.0, 5.0, ((0, 2), (1, 16)), jnp.float32)
    word_grad = gaussian(streams_of[6], (SEGS, WPS, 2 * H), 0.02, 0.119628906, ((0, 16), (2, 2)))
    w_emb = gaussian(streams_of[7], (2, V, E), 1.0, 5.0, ((0, 2),), jnp.float32)
    w_in = gaussian(streams_of[8], (2, E, 4 * H), E ** -0.5, 0.625, ((0, 2), (2, 4)), jnp.float32)
    w_rec = gaussian(streams_of[9], (2, H, 4 * H), H ** -0.5, 0.125, ((0, 2), (1, 4)), jnp.float32)
    b_rec = draw_b_rec(jax.random.fold_in(streams_of[19], 71), 0)
    w_dec = gaussian(streams_of[11], (2, H, V), (H // 16) ** -0.5, 0.5, ((0, 2), (1, 4)), jnp.float32)
    b_dec = gaussian(streams_of[12], (2, V), 1.0, 4.0, ((0, 2),), jnp.float32)
    mom_emb = gaussian(streams_of[13], (2, V, E), (0.25 / (4 * H)), 0.00048828125, ((0, 2),), jnp.float32)
    mom_in = gaussian(streams_of[14], (2, E, 4 * H), (0.25 / (4 * H)), 0.00048828125, ((0, 2), (2, 4)), jnp.float32)
    mom_rec = gaussian(streams_of[15], (2, H, 4 * H), (0.25 / (4 * H)), 0.00048828125, ((0, 2), (1, 4)), jnp.float32)
    mom_bias = gaussian(streams_of[16], (2, 4 * H), (0.25 / (4 * H)), 0.00048828125, ((0, 2), (1, 4)), jnp.float32)
    mom_dec = gaussian(streams_of[17], (2, H, V), (0.25 / (4 * H)), 0.00048828125, ((0, 2), (1, 4)), jnp.float32)
    mom_dbias = gaussian(streams_of[18], (2, V), (0.25 / (4 * H)), 0.00048828125, ((0, 2),), jnp.float32)
    return dict(chars=chars, targets=targets, resets=resets, word_pos=word_pos, h_init=h_init, c_init=c_init, word_grad=word_grad, w_emb=w_emb, w_in=w_in, w_rec=w_rec, b_rec=b_rec, w_dec=w_dec, b_dec=b_dec, mom_emb=mom_emb, mom_in=mom_in, mom_rec=mom_rec, mom_bias=mom_bias, mom_dec=mom_dec, mom_dbias=mom_dbias)


highest = lax.Precision.HIGHEST

@jax.custom_vjp
def low(v):
    return lax.optimization_barrier(v.astype(jnp.bfloat16)).astype(jnp.float32)

@jax.custom_vjp
def low_back(v):
    return v

def low_keep(v):
    return (low(v), None)

def low_pass(kept, grad):
    return (grad,)

def back_keep(v):
    return (v, None)

def back_low(kept, grad):
    return (low(grad),)
low.defvjp(low_keep, low_pass)
low_back.defvjp(back_keep, back_low)

def lstm_forward(emb_table, w_input, w_hidden, gate_bias, w_decode, decode_bias, start_hidden, start_cell, char_ids, target_ids, keep_mask, positions, cotangent):
    char_onehot = (char_ids[:, :, None] == jnp.arange(V, dtype=jnp.int32)).astype(jnp.float32)
    embedded = jnp.einsum('slv,ve->lse', char_onehot, low(emb_table), precision=highest)
    projected = jnp.einsum('lse,eg->lsg', embedded, low(w_input), precision=highest) + low(gate_bias)
    recurrent = low(w_hidden)
    keep_major = jnp.transpose(keep_mask)

    def advance(state_pair, step_feed):
        hidden_prev, cell_prev = state_pair
        proj_step, keep_step = step_feed
        hidden_kept = hidden_prev * keep_step[:, None]
        cell_kept = cell_prev * keep_step[:, None]
        preact = low_back(proj_step + jnp.dot(hidden_kept, recurrent, precision=highest))
        gate_in = jax.nn.sigmoid(preact[:, :H])
        gate_forget = jax.nn.sigmoid(preact[:, H:2 * H])
        gate_cell = jnp.tanh(preact[:, 2 * H:3 * H])
        gate_out = jax.nn.sigmoid(preact[:, 3 * H:])
        cell_next = gate_forget * cell_kept + gate_in * gate_cell
        hidden_next = low(gate_out * jnp.tanh(cell_next))
        return ((hidden_next, cell_next), hidden_next)
    final_pair, hiddens = lax.scan(advance, (low(start_hidden), start_cell), (projected, keep_major))
    logits = low_back(jnp.einsum('lsh,hv->lsv', hiddens, low(w_decode), precision=highest) + decode_bias)
    target_onehot = (jnp.transpose(target_ids)[:, :, None] == jnp.arange(V, dtype=jnp.int32)).astype(jnp.float32)
    token_loss = jax.nn.logsumexp(logits, axis=-1) - lax.optimization_barrier(jnp.sum(logits * target_onehot, axis=-1))
    loss_total = jnp.sum(token_loss)
    pos_onehot = (positions[:, :, None] == jnp.arange(SEG_LEN, dtype=jnp.int32)).astype(jnp.float32)
    picked = jnp.einsum('skl,lsh->skh', pos_onehot, hiddens, precision=highest)
    objective = loss_total / SEG_LEN + jnp.sum(picked * cotangent)
    return (objective, (loss_total, picked))

def reference(chars, targets, resets, word_pos, h_init, c_init, word_grad, w_emb, w_in, w_rec, b_rec, w_dec, b_dec, mom_emb, mom_in, mom_rec, mom_bias, mom_dec, mom_dbias):
    weights_all = (w_emb, w_in, w_rec, b_rec, w_dec, b_dec)
    moments_all = (mom_emb, mom_in, mom_rec, mom_bias, mom_dec, mom_dbias)
    loss_list, picked_list, hgrad_list, cgrad_list = ([], [], [], [])
    grad_lists = [[] for index_w in range(6)]
    mom_lists = [[] for index_w in range(6)]
    for direction in range(2):
        keep_mask = (1 - resets[direction]).astype(jnp.float32)
        cotangent = word_grad[:, :, direction * H:(direction + 1) * H].astype(jnp.float32)
        char_ids = chars[direction]
        target_ids = targets[direction]
        positions = word_pos[direction]

        def objective_fn(emb_table, w_input, w_hidden, gate_bias, w_decode, decode_bias, start_hidden, start_cell):
            return lstm_forward(emb_table, w_input, w_hidden, gate_bias, w_decode, decode_bias, start_hidden, start_cell, char_ids, target_ids, keep_mask, positions, cotangent)
        primals = tuple((weight[direction] for weight in weights_all)) + (h_init[direction], c_init[direction])
        objective_value, pullback, extras = jax.vjp(objective_fn, *primals, has_aux=True)
        gradients = pullback(jnp.ones((), jnp.float32))
        loss_total, picked = extras
        total_sq = jnp.zeros((), jnp.float32)
        for index_w in range(6):
            total_sq = total_sq + jnp.sum(gradients[index_w] * gradients[index_w])
        clip_scale = 0.25 / jnp.maximum(jnp.sqrt(total_sq), 0.25)
        for index_w in range(6):
            moment_next = 0.9 * moments_all[index_w][direction] + clip_scale * gradients[index_w]
            grad_lists[index_w].append(gradients[index_w])
            mom_lists[index_w].append(moment_next)
        loss_list.append(loss_total / (SEGS * SEG_LEN))
        picked_list.append(picked)
        hgrad_list.append(gradients[6])
        cgrad_list.append(gradients[7])
    losses = jnp.stack(loss_list)
    word_vectors = jnp.concatenate(picked_list, axis=-1).astype(jnp.bfloat16)
    grad_h = jnp.stack(hgrad_list)
    grad_c = jnp.stack(cgrad_list)
    grads_out = [jnp.stack(grad_lists[index_w]) for index_w in range(6)]
    moms_out = [jnp.stack(mom_lists[index_w]) for index_w in range(6)]
    return (losses, word_vectors, grad_h, grad_c, grads_out[0], grads_out[1], grads_out[2], grads_out[3], grads_out[4], grads_out[5], moms_out[0], moms_out[1], moms_out[2], moms_out[3], moms_out[4], moms_out[5])
```

```python
import functools

import jax
import jax.numpy as jnp
from jax import lax
from jax.experimental import pallas as pl
from jax.experimental.pallas import tpu as pltpu
from jax.sharding import PartitionSpec as P

MESH = pl.DeviceIdType.MESH
CHUNK = 256


def partner(value, axis, bit):
    mask = 2**bit
    pairs = [(source, source ^ mask) for source in range(lax.axis_size(axis))]
    return lax.ppermute(value, axis, pairs)


def momentum_step(moment, gradient, clip_scale):
    return 0.9 * moment + clip_scale * gradient


def squares_of(arrays):
    total_sq = jnp.zeros((), jnp.float32)
    for array in arrays:
        total_sq = total_sq + jnp.sum(array * array)
    return total_sq


def sigmoid(value):
    return 0.5 * jnp.tanh(0.5 * value) + 0.5


def core_peer():
    group = lax.axis_index("group")
    core = lax.rem(group, 2)
    return core, (lax.axis_index("dir"), group + 1 - 2 * core, lax.axis_index("dp"))


def greet(peers):
    barrier = pltpu.get_barrier_semaphore()
    for peer in peers:
        pl.semaphore_signal(barrier, inc=1, device_id=peer, device_id_type=MESH)
    pl.semaphore_wait(barrier, len(peers))


def forward_kernel(
    steps,
    emb_ref,
    keep_ref,
    h0_ref,
    c0_ref,
    w_hbm,
    hid_ref,
    kept_ref,
    gates_ref,
    cell_ref,
    ckept_ref,
    w_ref,
    hown,
    hpar,
    kown,
    kpar,
    cell,
    acc,
    w_sem,
    send_sem,
    recv_sem,
):
    t = pl.program_id(0)
    slot = lax.rem(t, 2)
    nxt = 1 - slot
    core, peer = core_peer()
    units = cell.shape[1]
    hidden = 2 * units
    chunks = units // CHUNK
    own0 = pl.multiple_of(core * units, units)
    par0 = pl.multiple_of((1 - core) * units, units)

    def exchange(which, u):
        return pltpu.make_async_remote_copy(
            src_ref=hown.at[which, u],
            dst_ref=hpar.at[which, u],
            send_sem=send_sem.at[which, u],
            recv_sem=recv_sem.at[which, u],
            device_id=peer,
            device_id_type=MESH,
        )

    @pl.when(t == 0)
    def _():
        copy = pltpu.make_async_copy(w_hbm, w_ref, w_sem)
        copy.start()
        greet([peer])
        for u in range(chunks):
            hown[0, u] = h0_ref[:, pl.ds(pl.multiple_of(own0 + u * CHUNK, CHUNK), CHUNK)]
            hpar[0, u] = h0_ref[:, pl.ds(pl.multiple_of(par0 + u * CHUNK, CHUNK), CHUNK)]
        cell[...] = c0_ref[...]
        copy.wait()

    keep = keep_ref[0][:, :1]
    keep_b = keep.astype(jnp.bfloat16)

    def early(u):
        for q in range(4):
            cols = pl.ds(q * units + u * CHUNK, CHUNK)
            acc[q, u] = jnp.dot(
                emb_ref[0], w_ref[hidden:, cols], preferred_element_type=jnp.float32
            ) + jnp.dot(kown[...], w_ref[pl.ds(own0, units), cols], preferred_element_type=jnp.float32)

    def late(u):
        pre = []
        for q in range(4):
            cols = pl.ds(q * units + u * CHUNK, CHUNK)
            pre.append(
                acc[q, u]
                + jnp.dot(kpar[...], w_ref[pl.ds(par0, units), cols], preferred_element_type=jnp.float32)
            )
        span = pl.ds(u * CHUNK, CHUNK)
        gate_in, gate_forget, gate_cell, gate_out = (
            sigmoid(pre[0]),
            sigmoid(pre[1]),
            jnp.tanh(pre[2]),
            sigmoid(pre[3]),
        )
        kept_cell = cell[:, span] * keep
        cell_next = gate_forget * kept_cell + gate_in * gate_cell
        hown[nxt, u] = (gate_out * jnp.tanh(cell_next)).astype(jnp.bfloat16)
        cell[:, span] = cell_next
        gates_ref[0, 0, :, span] = gate_in
        gates_ref[0, 1, :, span] = gate_forget
        gates_ref[0, 2, :, span] = gate_cell
        gates_ref[0, 3, :, span] = gate_out
        cell_ref[0, :, span] = cell_next
        ckept_ref[0, :, span] = kept_cell
        exchange(nxt, u).start()

    @pl.when(t < steps)
    def _():
        for u in range(chunks):
            kown[:, pl.ds(u * CHUNK, CHUNK)] = hown[slot, u] * keep_b
        early(0)
        early(1)

    @pl.when(t > 0)
    def _():
        for u in range(chunks):
            exchange(slot, u).wait()

    for u in range(chunks):
        hid_ref[0, :, pl.ds(pl.multiple_of(own0 + u * CHUNK, CHUNK), CHUNK)] = hown[slot, u]
        hid_ref[0, :, pl.ds(pl.multiple_of(par0 + u * CHUNK, CHUNK), CHUNK)] = hpar[slot, u]

    @pl.when(t < steps)
    def _():
        for u in range(chunks):
            kpar[:, pl.ds(u * CHUNK, CHUNK)] = hpar[slot, u] * keep_b
        kept_ref[0, :, pl.ds(own0, units)] = kown[...]
        kept_ref[0, :, pl.ds(par0, units)] = kpar[...]
        for u in range(chunks):
            late(u)
            if u + 2 < chunks:
                early(u + 2)


def run_forward(embedded, keep, h0, c0, weights):
    steps, rows, depth = embedded.shape
    units = c0.shape[1]
    hidden = 2 * units
    chunks = units // CHUNK

    def at(t):
        return jnp.minimum(t, steps - 1)

    whole = pl.BlockSpec(memory_space=pltpu.VMEM)
    return pl.pallas_call(
        functools.partial(forward_kernel, steps),
        grid=(steps + 1,),
        in_specs=[
            pl.BlockSpec((1, rows, depth), lambda t: (at(t), 0, 0)),
            pl.BlockSpec((1, rows, 128), lambda t: (at(t), 0, 0)),
            whole,
            whole,
            pl.BlockSpec(memory_space=pl.ANY),
        ],
        out_specs=[
            pl.BlockSpec((1, rows, hidden), lambda t: (t, 0, 0)),
            pl.BlockSpec((1, rows, hidden), lambda t: (at(t), 0, 0)),
            pl.BlockSpec((1, 4, rows, units), lambda t: (at(t), 0, 0, 0)),
            pl.BlockSpec((1, rows, units), lambda t: (at(t), 0, 0)),
            pl.BlockSpec((1, rows, units), lambda t: (at(t), 0, 0)),
        ],
        out_shape=[
            jax.ShapeDtypeStruct((steps + 1, rows, hidden), jnp.bfloat16),
            jax.ShapeDtypeStruct((steps, rows, hidden), jnp.bfloat16),
            jax.ShapeDtypeStruct((steps, 4, rows, units), jnp.float32),
            jax.ShapeDtypeStruct((steps, rows, units), jnp.float32),
            jax.ShapeDtypeStruct((steps, rows, units), jnp.float32),
        ],
        scratch_shapes=[
            pltpu.VMEM(weights.shape, jnp.bfloat16),
            pltpu.VMEM((2, chunks, rows, CHUNK), jnp.bfloat16),
            pltpu.VMEM((2, chunks, rows, CHUNK), jnp.bfloat16),
            pltpu.VMEM((rows, units), jnp.bfloat16),
            pltpu.VMEM((rows, units), jnp.bfloat16),
            pltpu.VMEM((rows, units), jnp.float32),
            pltpu.VMEM((4, chunks, rows, CHUNK), jnp.float32),
            pltpu.SemaphoreType.DMA,
            pltpu.SemaphoreType.DMA((2, chunks)),
            pltpu.SemaphoreType.DMA((2, chunks)),
        ],
        compiler_params=pltpu.CompilerParams(
            collective_id=1, has_side_effects=True, vmem_limit_bytes=56 << 20
        ),
        cost_estimate=pl.CostEstimate(
            flops=2 * steps * rows * weights.shape[0] * weights.shape[1],
            bytes_accessed=500 << 20,
            transcendentals=0,
        ),
    )(embedded, keep, h0, c0, weights)


def backward_kernel(
    steps,
    outg_ref,
    gates_ref,
    cell_ref,
    ckept_ref,
    keep_ref,
    w_hbm,
    pre_ref,
    gh_ref,
    gc_ref,
    w_ref,
    dh,
    dc,
    pg,
    outbox,
    inbox,
    w_sem,
    send_sem,
    recv_sem,
):
    i = pl.program_id(0)
    slot = lax.rem(i, 2)
    core, peer = core_peer()
    units = dh.shape[1]
    chunks = units // CHUNK
    own0 = pl.multiple_of(core * units, units)
    par0 = pl.multiple_of((1 - core) * units, units)

    def exchange(which, u):
        return pltpu.make_async_remote_copy(
            src_ref=outbox.at[which, u],
            dst_ref=inbox.at[which, u],
            send_sem=send_sem.at[which, u],
            recv_sem=recv_sem.at[which, u],
            device_id=peer,
            device_id_type=MESH,
        )

    @pl.when(i == 0)
    def _():
        copy = pltpu.make_async_copy(w_hbm, w_ref, w_sem)
        copy.start()
        greet([peer])
        dh[...] = jnp.zeros_like(dh)
        dc[...] = jnp.zeros_like(dc)
        copy.wait()

    @pl.when(i > 0)
    def _():
        for u in range(chunks):
            exchange(1 - slot, u).wait()
        for u in range(chunks):
            span = pl.ds(u * CHUNK, CHUNK)
            dh[:, span] = dh[:, span] + inbox[1 - slot, u]

    keep = keep_ref[0][:, :1]
    for u in range(chunks):
        span = pl.ds(u * CHUNK, CHUNK)
        gate_in = gates_ref[0, 0, :, span]
        gate_forget = gates_ref[0, 1, :, span]
        gate_cell = gates_ref[0, 2, :, span]
        gate_out = gates_ref[0, 3, :, span]
        total_hidden = dh[:, span] + outg_ref[0, :, span]
        tanh_cell = jnp.tanh(cell_ref[0, :, span])
        total_cell = dc[:, span] + total_hidden * gate_out * (1.0 - tanh_cell * tanh_cell)
        grads = [
            total_cell * gate_cell * gate_in * (1.0 - gate_in),
            total_cell * ckept_ref[0, :, span] * gate_forget * (1.0 - gate_forget),
            total_cell * gate_in * (1.0 - gate_cell * gate_cell),
            total_hidden * tanh_cell * gate_out * (1.0 - gate_out),
        ]
        for q in range(4):
            grad = grads[q].astype(jnp.bfloat16)
            pg[:, pl.ds(q * units + u * CHUNK, CHUNK)] = grad
            pre_ref[0, :, pl.ds(q * units + u * CHUNK, CHUNK)] = grad
        dc[:, span] = total_cell * gate_forget * keep
    for u in range(chunks):
        cols = pl.ds(pl.multiple_of(par0 + u * CHUNK, CHUNK), CHUNK)
        outbox[slot, u] = (
            jnp.dot(pg[...], w_ref[:, cols], preferred_element_type=jnp.float32) * keep
        )
        exchange(slot, u).start()
    for u in range(chunks):
        cols = pl.ds(pl.multiple_of(own0 + u * CHUNK, CHUNK), CHUNK)
        dh[:, pl.ds(u * CHUNK, CHUNK)] = (
            jnp.dot(pg[...], w_ref[:, cols], preferred_element_type=jnp.float32) * keep
        )

    @pl.when(i == steps - 1)
    def _():
        for u in range(chunks):
            exchange(slot, u).wait()
        for u in range(chunks):
            span = pl.ds(u * CHUNK, CHUNK)
            gh_ref[:, span] = dh[:, span] + inbox[slot, u]
        gc_ref[...] = dc[...]


def run_backward(out_grad, gates, cells, cells_kept, keep, weights_t):
    steps, rows, units = out_grad.shape
    chunks = units // CHUNK

    def back(i):
        return (steps - 1 - i, 0, 0)

    row_block = pl.BlockSpec((1, rows, units), back)
    whole = pl.BlockSpec(memory_space=pltpu.VMEM)
    return pl.pallas_call(
        functools.partial(backward_kernel, steps),
        grid=(steps,),
        in_specs=[
            row_block,
            pl.BlockSpec((1, 4, rows, units), lambda i: (steps - 1 - i, 0, 0, 0)),
            row_block,
            row_block,
            pl.BlockSpec((1, rows, 128), back),
            pl.BlockSpec(memory_space=pl.ANY),
        ],
        out_specs=[pl.BlockSpec((1, rows, 4 * units), back), whole, whole],
        out_shape=[
            jax.ShapeDtypeStruct((steps, rows, 4 * units), jnp.bfloat16),
            jax.ShapeDtypeStruct((rows, units), jnp.float32),
            jax.ShapeDtypeStruct((rows, units), jnp.float32),
        ],
        scratch_shapes=[
            pltpu.VMEM(weights_t.shape, jnp.bfloat16),
            pltpu.VMEM((rows, units), jnp.float32),
            pltpu.VMEM((rows, units), jnp.float32),
            pltpu.VMEM((rows, 4 * units), jnp.bfloat16),
            pltpu.VMEM((2, chunks, rows, CHUNK), jnp.float32),
            pltpu.VMEM((2, chunks, rows, CHUNK), jnp.float32),
            pltpu.SemaphoreType.DMA,
            pltpu.SemaphoreType.DMA((2, chunks)),
            pltpu.SemaphoreType.DMA((2, chunks)),
        ],
        compiler_params=pltpu.CompilerParams(
            collective_id=2, has_side_effects=True, vmem_limit_bytes=56 << 20
        ),
        cost_estimate=pl.CostEstimate(
            flops=2 * steps * rows * weights_t.shape[0] * weights_t.shape[1],
            bytes_accessed=500 << 20,
            transcendentals=0,
        ),
    )(out_grad, gates, cells, cells_kept, keep, weights_t)


def shards(
    chars,
    targets,
    resets,
    word_pos,
    h_init,
    c_init,
    word_grad,
    w_emb,
    w_in,
    w_rec,
    b_rec,
    w_dec,
    b_dec,
    mom_emb,
    mom_in,
    mom_rec,
    mom_bias,
    mom_dec,
    mom_dbias,
):
    vocab_size = w_emb.shape[1]
    embed_size = w_emb.shape[2]
    seg_len = chars.shape[2]
    batch_size = chars.shape[1]
    hidden_size = w_rec.shape[2] // 4
    units = hidden_size // 2
    core = lax.rem(lax.axis_index("group"), 2)
    first = core == 0

    def pair(own):
        other = partner(own, "group", 0)
        return jnp.where(first, jnp.concatenate([own, other]), jnp.concatenate([other, own]))

    def half(value, axis, index):
        return lax.dynamic_slice_in_dim(value, index * units, units, axis)

    def own_columns(value):
        return jnp.concatenate(
            [half(value[:, q * hidden_size : (q + 1) * hidden_size], 1, core) for q in range(4)],
            axis=1,
        )

    def spread(value):
        wide = jnp.zeros((value.shape[0], 4 * hidden_size), value.dtype)
        for q in range(4):
            wide = lax.dynamic_update_slice_in_dim(
                wide, value[:, q * units : (q + 1) * units], q * hidden_size + core * units, 1
            )
        return wide

    in_full, rec_full, bias_full, dec_full = (
        lax.all_gather(w_in[0].astype(jnp.bfloat16), "group", axis=1, tiled=True),
        lax.all_gather(w_rec[0].astype(jnp.bfloat16), "group", axis=0, tiled=True),
        lax.all_gather(b_rec[0].astype(jnp.bfloat16), "group", axis=0, tiled=True),
        lax.all_gather(w_dec[0].astype(jnp.bfloat16), "group", axis=0, tiled=True),
    )
    packed = pair(jnp.concatenate([chars[0], targets[0], resets[0], word_pos[0]], axis=1))
    chars2 = packed[:, :seg_len]
    targets2 = packed[:, seg_len : 2 * seg_len]
    resets2 = packed[:, 2 * seg_len : 3 * seg_len]
    word_pos2 = packed[:, 3 * seg_len :]
    h_pair = pair(h_init[0].astype(jnp.bfloat16))
    c_mine = half(c_init[0], 1, core)
    c_other = partner(half(c_init[0], 1, 1 - core), "group", 0)
    wg_mine = half(word_grad, 2, core)
    wg_other = partner(half(word_grad, 2, 1 - core), "group", 0)

    def ordered(mine, other):
        return jnp.where(first, jnp.concatenate([mine, other]), jnp.concatenate([other, mine]))

    c_pair = ordered(c_mine, c_other)
    wg_pair = ordered(wg_mine, wg_other)
    in_own = own_columns(in_full)
    rec_own = own_columns(rec_full)
    bias_own = own_columns(bias_full[None])
    depth = 128
    weights = jnp.concatenate(
        [
            rec_own,
            in_own,
            bias_own,
            jnp.zeros((depth - embed_size - 1, 4 * units), jnp.bfloat16),
        ]
    )
    char_major = jnp.transpose(chars2)
    char_onehot = (char_major[:, :, None] == jnp.arange(vocab_size, dtype=jnp.int32)).astype(
        jnp.bfloat16
    )
    embedded = jnp.einsum(
        "tbv,ve->tbe",
        char_onehot,
        w_emb[0].astype(jnp.bfloat16),
        preferred_element_type=jnp.float32,
    ).astype(jnp.bfloat16)
    pad_shape = (seg_len, 2 * batch_size, depth - embed_size - 1)
    embedded_one = jnp.concatenate(
        [
            embedded,
            jnp.ones((seg_len, 2 * batch_size, 1), jnp.bfloat16),
            jnp.zeros(pad_shape, jnp.bfloat16),
        ],
        axis=-1,
    )
    keep_major = jnp.broadcast_to(
        (1 - jnp.transpose(resets2)).astype(jnp.float32)[:, :, None],
        (seg_len, 2 * batch_size, 128),
    )
    hidden_all, kept_all, gate_all, cell_all, cellkept_all = run_forward(
        embedded_one, keep_major, h_pair, c_pair, weights
    )
    out_all = hidden_all[1:]
    logits = (
        jnp.einsum("tbh,hv->tbv", out_all, dec_full, preferred_element_type=jnp.float32) + b_dec[0]
    )
    log_probs = jax.nn.log_softmax(logits, axis=-1)
    target_onehot = (
        jnp.transpose(targets2)[:, :, None] == jnp.arange(vocab_size, dtype=jnp.int32)
    ).astype(jnp.float32)
    loss_part = -0.5 * jnp.sum(log_probs * target_onehot)
    logit_grad = ((jnp.exp(log_probs) - target_onehot) / seg_len).astype(jnp.bfloat16)
    from_output = jnp.einsum(
        "tbv,hv->tbh",
        logit_grad,
        lax.dynamic_slice_in_dim(dec_full, core * units, units, 0),
        preferred_element_type=jnp.float32,
    )
    pos_onehot2 = (word_pos2[:, :, None] == jnp.arange(seg_len, dtype=jnp.int32)).astype(
        jnp.bfloat16
    )
    from_words = jnp.einsum(
        "bkt,bkh->tbh", pos_onehot2, wg_pair, preferred_element_type=jnp.float32
    )
    out_own = lax.dynamic_slice_in_dim(out_all, core * batch_size, batch_size, 1)
    pos_onehot = (word_pos[0][:, :, None] == jnp.arange(seg_len, dtype=jnp.int32)).astype(
        jnp.bfloat16
    )
    picked = jnp.einsum(
        "bkt,tbh->bkh", pos_onehot, out_own, preferred_element_type=jnp.float32
    ).astype(jnp.bfloat16)
    half_slots = picked.shape[1] // 2
    model_index = lax.axis_index("dir")
    own_slots = lax.dynamic_slice_in_dim(picked, model_index * half_slots, half_slots, 1)
    other_slots = lax.dynamic_slice_in_dim(picked, (1 - model_index) * half_slots, half_slots, 1)
    partner_half = partner(other_slots, "dir", 0)
    leading = model_index == 0
    word_vectors = jnp.where(
        leading,
        jnp.concatenate([own_slots, partner_half], axis=-1),
        jnp.concatenate([partner_half, own_slots], axis=-1),
    )
    pre_all, gh_pair, gc_pair = run_backward(
        from_output + from_words, gate_all, cell_all, cellkept_all, keep_major, rec_own.T
    )

    def own_rows(value):
        mine = lax.dynamic_slice_in_dim(value, core * batch_size, batch_size, 0)
        theirs = lax.dynamic_slice_in_dim(value, (1 - core) * batch_size, batch_size, 0)
        other = partner(theirs, "group", 0)
        return jnp.where(
            first,
            jnp.concatenate([mine, other], axis=1),
            jnp.concatenate([other, mine], axis=1),
        )

    grad_hidden0 = own_rows(gh_pair)
    grad_cell0 = own_rows(gc_pair)
    rec_grad = spread(
        jnp.einsum("tbh,tbg->hg", kept_all, pre_all, preferred_element_type=jnp.float32).astype(
            jnp.bfloat16
        )
    )
    in_grad = spread(
        jnp.einsum("tbe,tbg->eg", embedded, pre_all, preferred_element_type=jnp.float32).astype(
            jnp.bfloat16
        )
    )
    bias_grad = spread(jnp.sum(pre_all, axis=(0, 1), dtype=jnp.float32).astype(jnp.bfloat16)[None])[0]
    lg_own = lax.dynamic_slice_in_dim(logit_grad, core * batch_size, batch_size, 1)
    dec_grad = jnp.einsum("tbh,tbv->hv", out_own, lg_own, preferred_element_type=jnp.float32)
    dbias_grad = jnp.sum(lg_own, axis=(0, 1), dtype=jnp.float32)
    embed_in = jnp.einsum("tbg,eg->tbe", pre_all, in_own, preferred_element_type=jnp.float32)
    emb_grad = jnp.einsum(
        "tbv,tbe->ve", char_onehot.astype(jnp.float32), embed_in, precision=lax.Precision.HIGHEST
    )
    loss_part = jnp.reshape(loss_part, (1,))
    in_sum, rec_sum, bias_sum, dec_sum = (
        lax.psum_scatter(in_grad, "group", scatter_dimension=1, tiled=True).astype(jnp.float32),
        lax.psum_scatter(rec_grad, "group", scatter_dimension=0, tiled=True).astype(jnp.float32),
        lax.psum_scatter(bias_grad, "group", scatter_dimension=0, tiled=True).astype(jnp.float32),
        lax.psum_scatter(
            dec_grad.astype(jnp.bfloat16), "group", scatter_dimension=0, tiled=True
        ).astype(jnp.float32),
    )
    in_sum, rec_sum, bias_sum, dec_sum, emb_sum, dbias_sum, loss_sum = (
        lax.psum(in_sum.astype(jnp.bfloat16), "dp").astype(jnp.float32),
        lax.psum(rec_sum.astype(jnp.bfloat16), "dp").astype(jnp.float32),
        lax.psum(bias_sum.astype(jnp.bfloat16), "dp").astype(jnp.float32),
        lax.psum(dec_sum.astype(jnp.bfloat16), "dp").astype(jnp.float32),
        lax.psum(emb_grad.astype(jnp.bfloat16), "dp").astype(jnp.float32),
        lax.psum(dbias_grad.astype(jnp.bfloat16), "dp").astype(jnp.float32),
        lax.psum(loss_part.astype(jnp.bfloat16), "dp").astype(jnp.float32),
    )
    shard_sq = squares_of((in_sum, rec_sum, bias_sum, dec_sum))
    shard_sq, emb_sum, dbias_sum, loss_sum = (
        lax.psum(shard_sq.astype(jnp.bfloat16), "group").astype(jnp.float32),
        lax.psum(emb_sum.astype(jnp.bfloat16), "group").astype(jnp.float32),
        lax.psum(dbias_sum.astype(jnp.bfloat16), "group").astype(jnp.float32),
        lax.psum(loss_sum.astype(jnp.bfloat16), "group").astype(jnp.float32),
    )
    total_sq = shard_sq + squares_of((emb_sum, dbias_sum))
    clip_scale = 0.25 / jnp.maximum(jnp.sqrt(total_sq), 0.25)
    mom_in_next = momentum_step(mom_in[0], in_sum, clip_scale)
    mom_rec_next = momentum_step(mom_rec[0], rec_sum, clip_scale)
    mom_bias_next = momentum_step(mom_bias[0], bias_sum, clip_scale)
    mom_dec_next = momentum_step(mom_dec[0], dec_sum, clip_scale)
    mom_emb_next = momentum_step(mom_emb[0], emb_sum, clip_scale)
    mom_dbias_next = momentum_step(mom_dbias[0], dbias_sum, clip_scale)
    token_count = seg_len * batch_size * lax.axis_size("group") * lax.axis_size("dp")
    losses = loss_sum / token_count
    return (
        losses,
        word_vectors,
        grad_hidden0[None],
        grad_cell0[None],
        emb_sum[None],
        in_sum[None],
        rec_sum[None],
        bias_sum[None],
        dec_sum[None],
        dbias_sum[None],
        mom_emb_next[None],
        mom_in_next[None],
        mom_rec_next[None],
        mom_bias_next[None],
        mom_dec_next[None],
        mom_dbias_next[None],
    )


def solution(mesh):
    segments = P("dir", ("group", "dp"), None)
    shared = P("dir", None, None)
    columns = P("dir", None, "group")
    rows = P("dir", "group", None)
    flat = P("dir", "group")
    return jax.shard_map(
        shards,
        mesh=mesh,
        in_specs=(
            segments,
            segments,
            segments,
            segments,
            segments,
            segments,
            P(("group", "dp"), None, "dir"),
            shared,
            columns,
            rows,
            flat,
            rows,
            P("dir", None),
            shared,
            columns,
            rows,
            flat,
            rows,
            P("dir", None),
        ),
        out_specs=(
            P("dir"),
            P(("group", "dp"), "dir", None),
            segments,
            segments,
            shared,
            columns,
            rows,
            flat,
            rows,
            P("dir", None),
            shared,
            columns,
            rows,
            flat,
            rows,
            P("dir", None),
        ),
        check_vma=False,
    )
```

```python
import functools

import jax
import jax.numpy as jnp
from jax import lax
from jax.experimental import pallas as pl
from jax.experimental.pallas import tpu as pltpu
from jax.sharding import PartitionSpec as P

MESH = pl.DeviceIdType.MESH
CHUNK = 256


def partner(value, axis, bit):
    mask = 2**bit
    pairs = [(source, source ^ mask) for source in range(lax.axis_size(axis))]
    return lax.ppermute(value, axis, pairs)


def momentum_step(moment, gradient, clip_scale):
    return 0.9 * moment + clip_scale * gradient


def sigmoid(value):
    return 0.5 * jnp.tanh(0.5 * value) + 0.5


def core_peer():
    group = lax.axis_index("group")
    core = lax.rem(group, 2)
    return core, (lax.axis_index("dir"), group + 1 - 2 * core, lax.axis_index("dp"))


def greet(peers):
    barrier = pltpu.get_barrier_semaphore()
    for peer in peers:
        pl.semaphore_signal(barrier, inc=1, device_id=peer, device_id_type=MESH)
    pl.semaphore_wait(barrier, len(peers))


def forward_kernel(
    steps,
    emb_ref,
    keep_ref,
    h0_ref,
    c0_ref,
    w_hbm,
    hid_ref,
    kept_ref,
    gates_ref,
    cell_ref,
    ckept_ref,
    w_ref,
    hown,
    hpar,
    kown,
    kpar,
    cell,
    acc,
    w_sem,
    send_sem,
    recv_sem,
):
    t = pl.program_id(0)
    slot = lax.rem(t, 2)
    nxt = 1 - slot
    core, peer = core_peer()
    units = cell.shape[1]
    hidden = 2 * units
    chunks = units // CHUNK
    own0 = pl.multiple_of(core * units, units)
    par0 = pl.multiple_of((1 - core) * units, units)

    def exchange(which, u):
        return pltpu.make_async_remote_copy(
            src_ref=hown.at[which, u],
            dst_ref=hpar.at[which, u],
            send_sem=send_sem.at[which, u],
            recv_sem=recv_sem.at[which, u],
            device_id=peer,
            device_id_type=MESH,
        )

    @pl.when(t == 0)
    def _():
        copy = pltpu.make_async_copy(w_hbm, w_ref, w_sem)
        copy.start()
        greet([peer])
        for u in range(chunks):
            hown[0, u] = h0_ref[:, pl.ds(pl.multiple_of(own0 + u * CHUNK, CHUNK), CHUNK)]
            hpar[0, u] = h0_ref[:, pl.ds(pl.multiple_of(par0 + u * CHUNK, CHUNK), CHUNK)]
        cell[...] = c0_ref[...]
        copy.wait()

    keep = keep_ref[0][:, :1]
    keep_b = keep.astype(jnp.bfloat16)

    def early(u):
        for q in range(4):
            cols = pl.ds(q * units + u * CHUNK, CHUNK)
            acc[q, u] = jnp.dot(
                emb_ref[0], w_ref[hidden:, cols], preferred_element_type=jnp.float32
            ) + jnp.dot(kown[...], w_ref[pl.ds(own0, units), cols], preferred_element_type=jnp.float32)

    def late(u):
        pre = []
        for q in range(4):
            cols = pl.ds(q * units + u * CHUNK, CHUNK)
            pre.append(
                acc[q, u]
                + jnp.dot(kpar[...], w_ref[pl.ds(par0, units), cols], preferred_element_type=jnp.float32)
            )
        span = pl.ds(u * CHUNK, CHUNK)
        gate_in, gate_forget, gate_cell, gate_out = (
            sigmoid(pre[0]),
            sigmoid(pre[1]),
            jnp.tanh(pre[2]),
            sigmoid(pre[3]),
        )
        kept_cell = cell[:, span] * keep
        cell_next = gate_forget * kept_cell + gate_in * gate_cell
        hown[nxt, u] = (gate_out * jnp.tanh(cell_next)).astype(jnp.bfloat16)
        cell[:, span] = cell_next
        gates_ref[0, 0, :, span] = gate_in
        gates_ref[0, 1, :, span] = gate_forget
        gates_ref[0, 2, :, span] = gate_cell
        gates_ref[0, 3, :, span] = gate_out
        cell_ref[0, :, span] = cell_next
        ckept_ref[0, :, span] = kept_cell
        exchange(nxt, u).start()

    @pl.when(t < steps)
    def _():
        for u in range(chunks):
            kown[:, pl.ds(u * CHUNK, CHUNK)] = hown[slot, u] * keep_b
        early(0)
        early(1)

    @pl.when(t > 0)
    def _():
        for u in range(chunks):
            exchange(slot, u).wait()

    for u in range(chunks):
        hid_ref[0, :, pl.ds(pl.multiple_of(own0 + u * CHUNK, CHUNK), CHUNK)] = hown[slot, u]
        hid_ref[0, :, pl.ds(pl.multiple_of(par0 + u * CHUNK, CHUNK), CHUNK)] = hpar[slot, u]

    @pl.when(t < steps)
    def _():
        for u in range(chunks):
            kpar[:, pl.ds(u * CHUNK, CHUNK)] = hpar[slot, u] * keep_b
        kept_ref[0, :, pl.ds(own0, units)] = kown[...]
        kept_ref[0, :, pl.ds(par0, units)] = kpar[...]
        for u in range(chunks):
            late(u)
            if u + 2 < chunks:
                early(u + 2)


def run_forward(embedded, keep, h0, c0, weights):
    steps, rows, depth = embedded.shape
    units = c0.shape[1]
    hidden = 2 * units
    chunks = units // CHUNK

    def at(t):
        return jnp.minimum(t, steps - 1)

    whole = pl.BlockSpec(memory_space=pltpu.VMEM)
    return pl.pallas_call(
        functools.partial(forward_kernel, steps),
        grid=(steps + 1,),
        in_specs=[
            pl.BlockSpec((1, rows, depth), lambda t: (at(t), 0, 0)),
            pl.BlockSpec((1, rows, 128), lambda t: (at(t), 0, 0)),
            whole,
            whole,
            pl.BlockSpec(memory_space=pl.ANY),
        ],
        out_specs=[
            pl.BlockSpec((1, rows, hidden), lambda t: (t, 0, 0)),
            pl.BlockSpec((1, rows, hidden), lambda t: (at(t), 0, 0)),
            pl.BlockSpec((1, 4, rows, units), lambda t: (at(t), 0, 0, 0)),
            pl.BlockSpec((1, rows, units), lambda t: (at(t), 0, 0)),
            pl.BlockSpec((1, rows, units), lambda t: (at(t), 0, 0)),
        ],
        out_shape=[
            jax.ShapeDtypeStruct((steps + 1, rows, hidden), jnp.bfloat16),
            jax.ShapeDtypeStruct((steps, rows, hidden), jnp.bfloat16),
            jax.ShapeDtypeStruct((steps, 4, rows, units), jnp.float32),
            jax.ShapeDtypeStruct((steps, rows, units), jnp.float32),
            jax.ShapeDtypeStruct((steps, rows, units), jnp.float32),
        ],
        scratch_shapes=[
            pltpu.VMEM(weights.shape, jnp.bfloat16),
            pltpu.VMEM((2, chunks, rows, CHUNK), jnp.bfloat16),
            pltpu.VMEM((2, chunks, rows, CHUNK), jnp.bfloat16),
            pltpu.VMEM((rows, units), jnp.bfloat16),
            pltpu.VMEM((rows, units), jnp.bfloat16),
            pltpu.VMEM((rows, units), jnp.float32),
            pltpu.VMEM((4, chunks, rows, CHUNK), jnp.float32),
            pltpu.SemaphoreType.DMA,
            pltpu.SemaphoreType.DMA((2, chunks)),
            pltpu.SemaphoreType.DMA((2, chunks)),
        ],
        compiler_params=pltpu.CompilerParams(
            collective_id=1, has_side_effects=True, vmem_limit_bytes=56 << 20
        ),
        cost_estimate=pl.CostEstimate(
            flops=2 * steps * rows * weights.shape[0] * weights.shape[1],
            bytes_accessed=500 << 20,
            transcendentals=0,
        ),
    )(embedded, keep, h0, c0, weights)


def backward_kernel(
    steps,
    outg_ref,
    gates_ref,
    cell_ref,
    ckept_ref,
    keep_ref,
    w_hbm,
    pre_ref,
    gh_ref,
    gc_ref,
    w_ref,
    dh,
    dc,
    pg,
    outbox,
    inbox,
    w_sem,
    send_sem,
    recv_sem,
):
    i = pl.program_id(0)
    slot = lax.rem(i, 2)
    core, peer = core_peer()
    units = dh.shape[1]
    chunks = units // CHUNK
    own0 = pl.multiple_of(core * units, units)
    par0 = pl.multiple_of((1 - core) * units, units)

    def exchange(which, u):
        return pltpu.make_async_remote_copy(
            src_ref=outbox.at[which, u],
            dst_ref=inbox.at[which, u],
            send_sem=send_sem.at[which, u],
            recv_sem=recv_sem.at[which, u],
            device_id=peer,
            device_id_type=MESH,
        )

    @pl.when(i == 0)
    def _():
        copy = pltpu.make_async_copy(w_hbm, w_ref, w_sem)
        copy.start()
        greet([peer])
        dh[...] = jnp.zeros_like(dh)
        dc[...] = jnp.zeros_like(dc)
        copy.wait()

    @pl.when(i > 0)
    def _():
        for u in range(chunks):
            exchange(1 - slot, u).wait()
        for u in range(chunks):
            span = pl.ds(u * CHUNK, CHUNK)
            dh[:, span] = dh[:, span] + inbox[1 - slot, u]

    keep = keep_ref[0][:, :1]
    for u in range(chunks):
        span = pl.ds(u * CHUNK, CHUNK)
        gate_in = gates_ref[0, 0, :, span]
        gate_forget = gates_ref[0, 1, :, span]
        gate_cell = gates_ref[0, 2, :, span]
        gate_out = gates_ref[0, 3, :, span]
        total_hidden = dh[:, span] + outg_ref[0, :, span]
        tanh_cell = jnp.tanh(cell_ref[0, :, span])
        total_cell = dc[:, span] + total_hidden * gate_out * (1.0 - tanh_cell * tanh_cell)
        grads = [
            total_cell * gate_cell * gate_in * (1.0 - gate_in),
            total_cell * ckept_ref[0, :, span] * gate_forget * (1.0 - gate_forget),
            total_cell * gate_in * (1.0 - gate_cell * gate_cell),
            total_hidden * tanh_cell * gate_out * (1.0 - gate_out),
        ]
        for q in range(4):
            grad = grads[q].astype(jnp.bfloat16)
            pg[:, pl.ds(q * units + u * CHUNK, CHUNK)] = grad
            pre_ref[0, :, pl.ds(q * units + u * CHUNK, CHUNK)] = grad
        dc[:, span] = total_cell * gate_forget * keep
    for u in range(chunks):
        cols = pl.ds(pl.multiple_of(par0 + u * CHUNK, CHUNK), CHUNK)
        outbox[slot, u] = (
            jnp.dot(pg[...], w_ref[:, cols], preferred_element_type=jnp.float32) * keep
        )
        exchange(slot, u).start()
    for u in range(chunks):
        cols = pl.ds(pl.multiple_of(own0 + u * CHUNK, CHUNK), CHUNK)
        dh[:, pl.ds(u * CHUNK, CHUNK)] = (
            jnp.dot(pg[...], w_ref[:, cols], preferred_element_type=jnp.float32) * keep
        )

    @pl.when(i == steps - 1)
    def _():
        for u in range(chunks):
            exchange(slot, u).wait()
        for u in range(chunks):
            span = pl.ds(u * CHUNK, CHUNK)
            gh_ref[:, span] = dh[:, span] + inbox[slot, u]
        gc_ref[...] = dc[...]


def run_backward(out_grad, gates, cells, cells_kept, keep, weights_t):
    steps, rows, units = out_grad.shape
    chunks = units // CHUNK

    def back(i):
        return (steps - 1 - i, 0, 0)

    row_block = pl.BlockSpec((1, rows, units), back)
    whole = pl.BlockSpec(memory_space=pltpu.VMEM)
    return pl.pallas_call(
        functools.partial(backward_kernel, steps),
        grid=(steps,),
        in_specs=[
            row_block,
            pl.BlockSpec((1, 4, rows, units), lambda i: (steps - 1 - i, 0, 0, 0)),
            row_block,
            row_block,
            pl.BlockSpec((1, rows, 128), back),
            pl.BlockSpec(memory_space=pl.ANY),
        ],
        out_specs=[pl.BlockSpec((1, rows, 4 * units), back), whole, whole],
        out_shape=[
            jax.ShapeDtypeStruct((steps, rows, 4 * units), jnp.bfloat16),
            jax.ShapeDtypeStruct((rows, units), jnp.float32),
            jax.ShapeDtypeStruct((rows, units), jnp.float32),
        ],
        scratch_shapes=[
            pltpu.VMEM(weights_t.shape, jnp.bfloat16),
            pltpu.VMEM((rows, units), jnp.float32),
            pltpu.VMEM((rows, units), jnp.float32),
            pltpu.VMEM((rows, 4 * units), jnp.bfloat16),
            pltpu.VMEM((2, chunks, rows, CHUNK), jnp.float32),
            pltpu.VMEM((2, chunks, rows, CHUNK), jnp.float32),
            pltpu.SemaphoreType.DMA,
            pltpu.SemaphoreType.DMA((2, chunks)),
            pltpu.SemaphoreType.DMA((2, chunks)),
        ],
        compiler_params=pltpu.CompilerParams(
            collective_id=2, has_side_effects=True, vmem_limit_bytes=56 << 20
        ),
        cost_estimate=pl.CostEstimate(
            flops=2 * steps * rows * weights_t.shape[0] * weights_t.shape[1],
            bytes_accessed=500 << 20,
            transcendentals=0,
        ),
    )(out_grad, gates, cells, cells_kept, keep, weights_t)


def reduce_kernel(
    chips,
    depth,
    embed,
    kept_ref,
    aug_ref,
    pre_ref,
    in_ref,
    chars_ref,
    extra_ref,
    decsq_ref,
    rec_hbm,
    inout_ref,
    emb_ref,
    clip_ref,
    turned,
    inbox,
    outbox,
    partial,
    final,
    in_all,
    in_box,
    in_mine,
    in_part,
    in_final,
    in_swap,
    emb_box,
    emb_mine,
    emb_part,
    emb_final,
    ssq,
    norm_box,
    y_send,
    y_recv,
    part_recv,
    final_recv,
    part_send,
    final_send,
    write_sem,
    in_send,
    in_recv,
    emb_send,
    emb_recv,
    misc_recv,
    misc_send,
    norm_send,
    norm_recv,
):
    model = lax.axis_index("dir")
    group = lax.axis_index("group")
    z = lax.axis_index("dp")
    core = lax.rem(group, 2)
    chip = group // 2
    peers = 2 * chips
    middle = depth // 2
    rows_out = kept_ref.shape[1] // peers
    wide = pre_ref.shape[1]
    tall = turned.shape[0]
    lot = tall // 16
    batches = rows_out // tall
    groups = rows_out // 16
    per_pass = lot // peers
    upper = depth - 1 > middle
    is_middle = z == middle
    low = z < middle
    has_away = jnp.logical_or(jnp.logical_and(low, z > 0), jnp.logical_and(z > middle, z < depth - 1))
    toward = jnp.where(low, z + 1, jnp.maximum(z - 1, 0))
    away = jnp.where(low, jnp.maximum(z - 1, 0), jnp.minimum(z + 1, depth - 1))

    def in_group(index):
        return (model, index, z)

    def in_line(index):
        return (model, group, index)

    def owner_of(slot):
        if slot == 0:
            return group
        if slot == 1:
            return group + 1 - 2 * core
        step = (slot - 2) // 2 + 1
        side = core if slot % 2 == 0 else 1 - core
        return 2 * lax.rem(chip + step, chips) + side

    def slot_there(slot):
        if slot == 1:
            return 1
        step = (slot - 2) // 2 + 1
        return 2 + 2 * (chips - step - 1) + slot % 2

    barrier = pltpu.get_barrier_semaphore()
    for slot in range(1, peers):
        pl.semaphore_signal(barrier, inc=1, device_id=in_group(owner_of(slot)), device_id_type=MESH)

    @pl.when(z > 0)
    def _():
        pl.semaphore_signal(
            barrier, inc=1, device_id=in_line(jnp.maximum(z - 1, 0)), device_id_type=MESH
        )

    @pl.when(z < depth - 1)
    def _():
        pl.semaphore_signal(
            barrier, inc=1, device_id=in_line(jnp.minimum(z + 1, depth - 1)), device_id_type=MESH
        )

    pl.semaphore_wait(
        barrier,
        peers - 1 + jnp.where(z > 0, 1, 0) + jnp.where(z < depth - 1, 1, 0),
    )
    ssq[...] = jnp.zeros_like(ssq)

    def remote(src, dst, send, recv, device):
        return pltpu.make_async_remote_copy(
            src_ref=src,
            dst_ref=dst,
            send_sem=send,
            recv_sem=recv,
            device_id=device,
            device_id_type=MESH,
        )

    def squares(value):
        square = value * value
        total = square[:, :128]
        for lane in range(128, value.shape[1], 128):
            total = total + square[:, lane : lane + 128]
        rows = total[:16]
        for row in range(16, value.shape[0], 16):
            rows = rows + total[row : row + 16]
        ssq[...] = ssq[...] + rows

    def send_partial(mine, part, fin, sems):
        @pl.when(jnp.logical_not(is_middle))
        def _():
            @pl.when(has_away)
            def _():
                remote(mine, part, sems["ps"], sems["pr"], in_line(away)).wait_recv()
                mine[...] = (
                    mine[...].astype(jnp.float32) + part[...].astype(jnp.float32)
                ).astype(mine.dtype)

            if upper:

                @pl.when(z == middle + 1)
                def _():
                    remote(mine, fin, sems["ps"], sems["fr"], in_line(toward)).start()

            @pl.when(z != middle + 1)
            def _():
                remote(mine, part, sems["ps"], sems["pr"], in_line(toward)).start()

        @pl.when(is_middle)
        def _():
            remote(mine, part, sems["ps"], sems["pr"], in_line(toward)).wait_recv()
            total = mine[...].astype(jnp.float32) + part[...].astype(jnp.float32)
            if upper:
                remote(mine, fin, sems["ps"], sems["fr"], in_line(toward)).wait_recv()
                total = total + fin[...].astype(jnp.float32)
            fin[...] = total.astype(fin.dtype)
            remote(fin, fin, sems["f0"], sems["fr"], in_line(middle - 1)).start()
            if upper:
                remote(fin, fin, sems["f1"], sems["fr"], in_line(middle + 1)).start()

    def pass_final(fin, sems):
        @pl.when(jnp.logical_not(is_middle))
        def _():
            remote(fin, fin, sems["f0"], sems["fr"], in_line(toward)).wait_recv()

            @pl.when(has_away)
            def _():
                remote(fin, fin, sems["f0"], sems["fr"], in_line(away)).start()

    def wait_line(mine, fin, sems):
        @pl.when(is_middle)
        def _():
            remote(fin, fin, sems["f0"], sems["fr"], in_line(toward)).wait_send()
            if upper:
                remote(fin, fin, sems["f1"], sems["fr"], in_line(toward)).wait_send()

        @pl.when(jnp.logical_not(is_middle))
        def _():
            remote(mine, fin, sems["ps"], sems["fr"], in_line(toward)).wait_send()

            @pl.when(has_away)
            def _():
                remote(fin, fin, sems["f0"], sems["fr"], in_line(away)).wait_send()

    def line_sems(unit):
        return {
            "pr": part_recv.at[unit],
            "fr": final_recv.at[unit],
            "ps": part_send.at[unit],
            "f0": final_send.at[0, unit],
            "f1": final_send.at[1, unit],
        }

    units = 2 * groups
    in_sems, emb_sems = line_sems(units), line_sems(units + 1)

    def send_block(slot, parity, index, row):
        return remote(
            outbox.at[slot - 1, parity, index],
            inbox.at[slot_there(slot), row],
            y_send.at[slot - 1, parity, index],
            y_recv.at[slot_there(slot) - 1, row],
            in_group(owner_of(slot)),
        )

    span = 1024

    def product(dest):
        def columns(j, carry):
            cols = pl.ds(pl.multiple_of(j * span, span), span)
            dest[:, :, cols] = (
                jnp.dot(turned[...], pre_ref[:, cols], preferred_element_type=jnp.float32)
                .astype(jnp.bfloat16)
                .reshape(lot, 16, span)
            )
            return carry

        lax.fori_loop(0, wide // span, columns, 0)

    def block(slot, b, parity):
        start = owner_of(slot) * rows_out + b * tall
        turned[...] = jnp.transpose(kept_ref[:, pl.ds(pl.multiple_of(start, tall), tall)])
        if slot == 0:
            product(inbox.at[0, pl.ds(b * lot, lot)])
        else:

            @pl.when(b >= 2)
            def _():
                for index in range(lot):
                    send_block(slot, parity, index, 0).wait_send()

            product(outbox.at[slot - 1, parity])

    def send(row):
        parity, index = lax.rem(row // lot, 2), lax.rem(row, lot)
        for slot in list(range(2, peers)) + [1]:
            send_block(slot, parity, index, row).start()

    def take(row):
        for slot in range(1, peers):
            remote(
                outbox.at[slot - 1, 0, 0],
                inbox.at[slot, row],
                y_send.at[slot - 1, 0, 0],
                y_recv.at[slot - 1, row],
                in_group(owner_of(slot)),
            ).wait_recv()
        for part in range(2):
            if chips > 1:
                total = inbox[part, row].astype(jnp.float32)
                for slot in range(2 + part, peers, 2):
                    total = total + inbox[slot, row].astype(jnp.float32)
                inbox[part, row] = total.astype(jnp.bfloat16)
            send_partial(
                inbox.at[part, row],
                partial.at[2 * row + part],
                final.at[2 * row + part],
                line_sems(2 * row + part),
            )

    def write_out(row, part):
        side = core if part == 0 else 1 - core
        return pltpu.make_async_copy(
            final.at[2 * row + part],
            rec_hbm.at[side, pl.ds(pl.multiple_of(row * 16, 16), 16)],
            write_sem.at[2 * row + part],
        )

    def finish(row):
        for part in range(2):
            pass_final(final.at[2 * row + part], line_sems(2 * row + part))
            write_out(row, part).start()
            squares(final[2 * row + part].astype(jnp.float32))

    in_rows, in_wide = in_mine.shape

    def in_columns(index):
        return pl.ds(pl.multiple_of(index * in_wide, in_wide), in_wide)

    def in_copy(step):
        there = lax.rem(chip + step, chips)
        return remote(
            in_all.at[:, in_columns(there)],
            in_box.at[chips - step - 1],
            in_send.at[step - 1],
            in_recv.at[chips - step - 1],
            in_group(2 * there + core),
        )

    def emb_copy(slot, source):
        return remote(
            emb_mine,
            emb_box.at[source],
            emb_send.at[slot - 1],
            emb_recv.at[source],
            in_group(owner_of(slot)),
        )

    def small_products():
        turned[...] = jnp.transpose(aug_ref[...])

        def columns(j, carry):
            cols = pl.ds(pl.multiple_of(j * span, span), span)
            in_all[:, cols] = jnp.dot(
                turned[...], pre_ref[:, cols], preferred_element_type=jnp.float32
            )[:in_rows].astype(jnp.bfloat16)
            return carry

        lax.fori_loop(0, wide // span, columns, 0)
        for step in range(1, chips):
            in_copy(step).start()
        into = lax.dot_general(
            pre_ref[...], in_ref[...], (((1,), (1,)), ((), ())), preferred_element_type=jnp.float32
        ).astype(jnp.bfloat16)
        vocab_rows = emb_mine.shape[0]
        ids = lax.broadcasted_iota(jnp.int32, (vocab_rows, chars_ref.shape[1]), 0)
        onehot = jnp.where(chars_ref[...] == ids, 1.0, 0.0).astype(jnp.bfloat16)
        summed = jnp.dot(onehot, into, preferred_element_type=jnp.float32)
        lanes = lax.broadcasted_iota(jnp.int32, summed.shape, 1)
        emb_mine[...] = jnp.where(lanes < embed, summed, 0.0) + extra_ref[...]
        for slot in range(1, peers):
            emb_copy(slot, group).start()

    def small_partials():
        for step in range(1, chips):
            in_copy(step).wait_recv()
        total = in_all[:, in_columns(chip)].astype(jnp.float32)
        for step in range(1, chips):
            total = total + in_box[step - 1].astype(jnp.float32)
        in_mine[...] = total.astype(jnp.bfloat16)
        send_partial(in_mine, in_part, in_final, in_sems)
        for slot in range(1, peers):
            emb_copy(slot, owner_of(slot)).wait_recv()
        for slot in range(1, peers):
            emb_copy(slot, group).wait_send()
        emb_box[group] = emb_mine[...]
        total = emb_box[0]
        for source in range(1, peers):
            total = total + emb_box[source]
        emb_mine[...] = total
        send_partial(emb_mine, emb_part, emb_final, emb_sems)

    def small_finals():
        pass_final(in_final, in_sems)
        squares(in_final[...].astype(jnp.float32))
        pass_final(emb_final, emb_sems)

    order = list(range(2, peers)) + [1, 0]
    lead = (peers - 2) * per_pass
    y_lag, hop_lag = 3, 4
    hops = jnp.where(low, middle - z, z - middle)
    most_hops = max(middle, depth - 1 - middle)
    steps = groups + y_lag + hop_lag * most_hops + lead
    rounds = max(-(-steps // lot), 3 + most_hops)

    def round_of(b, carry):
        parity = lax.rem(b, 2)

        @pl.when(b == 1)
        def _():
            small_products()

        for turn, slot in enumerate(order):

            @pl.when(b < batches)
            def _():
                block(slot, b, parity)

            def step(j, inner):
                row = b * lot + turn * per_pass + j - lead
                arrived = row - y_lag
                summed = arrived - hop_lag * hops

                @pl.when(jnp.logical_and(row >= 0, row < groups))
                def _():
                    send(row)

                @pl.when(jnp.logical_and(arrived >= 0, arrived < groups))
                def _():
                    take(arrived)

                @pl.when(jnp.logical_and(summed >= 0, summed < groups))
                def _():
                    finish(summed)

                return inner

            lax.fori_loop(0, per_pass, step, 0)

        @pl.when(b == 2)
        def _():
            small_partials()

        @pl.when(b == 2 + hops)
        def _():
            small_finals()

        return carry

    lax.fori_loop(0, rounds, round_of, 0)

    keep_cols = in_wide // 2
    if in_wide > wide // 4:
        mine = pl.ds(pl.multiple_of(core * keep_cols, keep_cols), keep_cols)
        theirs = pl.ds(pl.multiple_of((1 - core) * keep_cols, keep_cols), keep_cols)
        swap = remote(
            in_final.at[:, theirs], in_swap, misc_send, misc_recv, in_group(owner_of(1))
        )
        swap.start()
        swap.wait()
        inout_ref[:, mine] = in_final[:, mine]
        inout_ref[:, theirs] = in_swap[...]
    else:
        inout_ref[...] = in_final[...]
    emb_ref[...] = emb_final[...]

    ssq[...] = ssq[...] + decsq_ref[...]
    norm_box[group] = ssq[...]

    def norm_copy(slot, source):
        return remote(
            ssq,
            norm_box.at[source],
            norm_send.at[slot - 1],
            norm_recv.at[source],
            in_group(owner_of(slot)),
        )

    for slot in range(1, peers):
        norm_copy(slot, group).start()
    for slot in range(1, peers):
        norm_copy(slot, owner_of(slot)).wait_recv()
    for slot in range(1, peers):
        norm_copy(slot, group).wait_send()
    total = norm_box[0]
    for source in range(1, peers):
        total = total + norm_box[source]
    lanes = lax.broadcasted_iota(jnp.int32, emb_final.shape, 1)
    small = jnp.where(lanes <= embed, emb_final[...], 0.0)
    total_sq = jnp.sum(total) + jnp.sum(small * small)
    clip_ref[...] = jnp.full(clip_ref.shape, 0.25, jnp.float32) / jnp.maximum(
        jnp.sqrt(jnp.full(clip_ref.shape, total_sq, jnp.float32)), 0.25
    )

    for step in range(1, chips):
        in_copy(step).wait_send()
    wait_line(in_mine, in_final, in_sems)
    wait_line(emb_mine, emb_final, emb_sems)
    for slot in range(1, peers):
        for parity in range(min(2, batches)):
            for index in range(lot):
                send_block(slot, parity, index, 0).wait_send()

    def settle(row, carry):
        for part in range(2):
            wait_line(
                inbox.at[part, row], final.at[2 * row + part], line_sems(2 * row + part)
            )
            write_out(row, part).wait()
        return carry

    lax.fori_loop(0, groups, settle, 0)


def run_reduce(chips, depth, embed, kept, aug, pre, in_own, chars, extra, dec_sq):
    hidden = kept.shape[1]
    count, wide = pre.shape
    peers = 2 * chips
    rows_out = hidden // peers
    tall = 128
    lot = tall // 16
    groups = rows_out // 16
    units = 2 * groups
    in_rows = -(-(embed + 1) // 16) * 16
    in_wide = wide // chips
    in_cols = 2 * wide // peers
    vmem = pl.BlockSpec(memory_space=pltpu.VMEM)
    bf16, f32 = jnp.bfloat16, jnp.float32
    small = extra.shape
    dma = pltpu.SemaphoreType.DMA
    return pl.pallas_call(
        functools.partial(reduce_kernel, chips, depth, embed),
        in_specs=[vmem] * 7,
        out_specs=[pl.BlockSpec(memory_space=pl.ANY), vmem, vmem, vmem],
        out_shape=[
            jax.ShapeDtypeStruct((2, rows_out, wide), bf16),
            jax.ShapeDtypeStruct((in_rows, in_cols), bf16),
            jax.ShapeDtypeStruct(small, f32),
            jax.ShapeDtypeStruct((8, 128), f32),
        ],
        scratch_shapes=[
            pltpu.VMEM((tall, count), bf16),
            pltpu.VMEM((peers, groups, 16, wide), bf16),
            pltpu.VMEM((peers - 1, 2, lot, 16, wide), bf16),
            pltpu.VMEM((units, 16, wide), bf16),
            pltpu.VMEM((units, 16, wide), bf16),
            pltpu.VMEM((in_rows, wide), bf16),
            pltpu.VMEM((max(chips - 1, 1), in_rows, in_wide), bf16),
            pltpu.VMEM((in_rows, in_wide), bf16),
            pltpu.VMEM((in_rows, in_wide), bf16),
            pltpu.VMEM((in_rows, in_wide), bf16),
            pltpu.VMEM((in_rows, in_wide // 2), bf16),
            pltpu.VMEM((peers,) + small, f32),
            pltpu.VMEM(small, f32),
            pltpu.VMEM(small, f32),
            pltpu.VMEM(small, f32),
            pltpu.VMEM((16, 128), f32),
            pltpu.VMEM((peers, 16, 128), f32),
            dma((peers - 1, 2, lot)),
            dma((peers - 1, groups)),
            dma((units + 2,)),
            dma((units + 2,)),
            dma((units + 2,)),
            dma((2, units + 2)),
            dma((units,)),
            dma((max(chips - 1, 1),)),
            dma((max(chips - 1, 1),)),
            dma((peers - 1,)),
            dma((peers,)),
            dma,
            dma,
            dma((peers - 1,)),
            dma((peers,)),
        ],
        compiler_params=pltpu.CompilerParams(
            collective_id=3, has_side_effects=True, vmem_limit_bytes=60 << 20
        ),
        cost_estimate=pl.CostEstimate(
            flops=2 * count * hidden * wide, bytes_accessed=700 << 20, transcendentals=0
        ),
    )(kept, aug, pre, in_own, chars, extra, dec_sq)


def momentum_kernel(clip_ref, sum_ref, moment_ref, grad_ref, next_ref):
    gradient = sum_ref[0].astype(jnp.float32)
    grad_ref[0] = gradient
    next_ref[0] = momentum_step(moment_ref[0], gradient, clip_ref[0, 0])


def run_momentum(clip, sums, moment):
    halves, rows, wide = sums.shape
    span = wide // 4
    block = pl.BlockSpec((1, rows, span), lambda q, s: (0, 0, 2 * q + s))
    shape = jax.ShapeDtypeStruct(moment.shape, jnp.float32)
    return pl.pallas_call(
        momentum_kernel,
        grid=(4, 2),
        in_specs=[
            pl.BlockSpec(memory_space=pltpu.SMEM),
            pl.BlockSpec((1, rows, span), lambda q, s: (s, 0, q)),
            block,
        ],
        out_specs=[block, block],
        out_shape=[shape, shape],
        compiler_params=pltpu.CompilerParams(vmem_limit_bytes=48 << 20),
    )(clip, sums, moment)


def shards(
    chars,
    targets,
    resets,
    word_pos,
    h_init,
    c_init,
    word_grad,
    w_emb,
    w_in,
    w_rec,
    b_rec,
    w_dec,
    b_dec,
    mom_emb,
    mom_in,
    mom_rec,
    mom_bias,
    mom_dec,
    mom_dbias,
):
    vocab_size = w_emb.shape[1]
    embed_size = w_emb.shape[2]
    seg_len = chars.shape[2]
    batch_size = chars.shape[1]
    hidden_size = w_rec.shape[2] // 4
    units = hidden_size // 2
    core = lax.rem(lax.axis_index("group"), 2)
    first = core == 0

    def pair(own):
        other = partner(own, "group", 0)
        return jnp.where(first, jnp.concatenate([own, other]), jnp.concatenate([other, own]))

    def half(value, axis, index):
        return lax.dynamic_slice_in_dim(value, index * units, units, axis)

    def own_columns(value):
        return jnp.concatenate(
            [half(value[:, q * hidden_size : (q + 1) * hidden_size], 1, core) for q in range(4)],
            axis=1,
        )

    in_full, rec_full, bias_full, dec_full = (
        lax.all_gather(w_in[0].astype(jnp.bfloat16), "group", axis=1, tiled=True),
        lax.all_gather(w_rec[0].astype(jnp.bfloat16), "group", axis=0, tiled=True),
        lax.all_gather(b_rec[0].astype(jnp.bfloat16), "group", axis=0, tiled=True),
        lax.all_gather(w_dec[0].astype(jnp.bfloat16), "group", axis=0, tiled=True),
    )
    packed = pair(jnp.concatenate([chars[0], targets[0], resets[0], word_pos[0]], axis=1))
    chars2 = packed[:, :seg_len]
    targets2 = packed[:, seg_len : 2 * seg_len]
    resets2 = packed[:, 2 * seg_len : 3 * seg_len]
    word_pos2 = packed[:, 3 * seg_len :]
    h_pair = pair(h_init[0].astype(jnp.bfloat16))
    c_mine = half(c_init[0], 1, core)
    c_other = partner(half(c_init[0], 1, 1 - core), "group", 0)
    wg_mine = half(word_grad, 2, core)
    wg_other = partner(half(word_grad, 2, 1 - core), "group", 0)

    def ordered(mine, other):
        return jnp.where(first, jnp.concatenate([mine, other]), jnp.concatenate([other, mine]))

    c_pair = ordered(c_mine, c_other)
    wg_pair = ordered(wg_mine, wg_other)
    in_own = own_columns(in_full)
    rec_own = own_columns(rec_full)
    bias_own = own_columns(bias_full[None])
    depth = 128
    weights = jnp.concatenate(
        [
            rec_own,
            in_own,
            bias_own,
            jnp.zeros((depth - embed_size - 1, 4 * units), jnp.bfloat16),
        ]
    )
    char_major = jnp.transpose(chars2)
    char_onehot = (char_major[:, :, None] == jnp.arange(vocab_size, dtype=jnp.int32)).astype(
        jnp.bfloat16
    )
    embedded = jnp.einsum(
        "tbv,ve->tbe",
        char_onehot,
        w_emb[0].astype(jnp.bfloat16),
        preferred_element_type=jnp.float32,
    ).astype(jnp.bfloat16)
    pad_shape = (seg_len, 2 * batch_size, depth - embed_size - 1)
    embedded_one = jnp.concatenate(
        [
            embedded,
            jnp.ones((seg_len, 2 * batch_size, 1), jnp.bfloat16),
            jnp.zeros(pad_shape, jnp.bfloat16),
        ],
        axis=-1,
    )
    keep_major = jnp.broadcast_to(
        (1 - jnp.transpose(resets2)).astype(jnp.float32)[:, :, None],
        (seg_len, 2 * batch_size, 128),
    )
    hidden_all, kept_all, gate_all, cell_all, cellkept_all = run_forward(
        embedded_one, keep_major, h_pair, c_pair, weights
    )
    out_all = hidden_all[1:]
    logits = (
        jnp.einsum("tbh,hv->tbv", out_all, dec_full, preferred_element_type=jnp.float32) + b_dec[0]
    )
    log_probs = jax.nn.log_softmax(logits, axis=-1)
    target_onehot = (
        jnp.transpose(targets2)[:, :, None] == jnp.arange(vocab_size, dtype=jnp.int32)
    ).astype(jnp.float32)
    loss_part = -0.5 * jnp.sum(log_probs * target_onehot)
    logit_grad = ((jnp.exp(log_probs) - target_onehot) / seg_len).astype(jnp.bfloat16)
    from_output = jnp.einsum(
        "tbv,hv->tbh",
        logit_grad,
        lax.dynamic_slice_in_dim(dec_full, core * units, units, 0),
        preferred_element_type=jnp.float32,
    )
    pos_onehot2 = (word_pos2[:, :, None] == jnp.arange(seg_len, dtype=jnp.int32)).astype(
        jnp.bfloat16
    )
    from_words = jnp.einsum(
        "bkt,bkh->tbh", pos_onehot2, wg_pair, preferred_element_type=jnp.float32
    )
    out_own = lax.dynamic_slice_in_dim(out_all, core * batch_size, batch_size, 1)
    pos_onehot = (word_pos[0][:, :, None] == jnp.arange(seg_len, dtype=jnp.int32)).astype(
        jnp.bfloat16
    )
    picked = jnp.einsum(
        "bkt,tbh->bkh", pos_onehot, out_own, preferred_element_type=jnp.float32
    ).astype(jnp.bfloat16)
    half_slots = picked.shape[1] // 2
    model_index = lax.axis_index("dir")
    own_slots = lax.dynamic_slice_in_dim(picked, model_index * half_slots, half_slots, 1)
    other_slots = lax.dynamic_slice_in_dim(picked, (1 - model_index) * half_slots, half_slots, 1)
    partner_half = partner(other_slots, "dir", 0)
    leading = model_index == 0
    word_vectors = jnp.where(
        leading,
        jnp.concatenate([own_slots, partner_half], axis=-1),
        jnp.concatenate([partner_half, own_slots], axis=-1),
    )
    pre_all, gh_pair, gc_pair = run_backward(
        from_output + from_words, gate_all, cell_all, cellkept_all, keep_major, rec_own.T
    )

    def own_rows(value):
        mine = lax.dynamic_slice_in_dim(value, core * batch_size, batch_size, 0)
        theirs = lax.dynamic_slice_in_dim(value, (1 - core) * batch_size, batch_size, 0)
        other = partner(theirs, "group", 0)
        return jnp.where(
            first,
            jnp.concatenate([mine, other], axis=1),
            jnp.concatenate([other, mine], axis=1),
        )

    grad_hidden0 = own_rows(gh_pair)
    grad_cell0 = own_rows(gc_pair)
    lg_own = lax.dynamic_slice_in_dim(logit_grad, core * batch_size, batch_size, 1)
    dec_grad = jnp.einsum("tbh,tbv->hv", out_own, lg_own, preferred_element_type=jnp.float32)
    dbias_grad = jnp.sum(lg_own, axis=(0, 1), dtype=jnp.float32)
    dec_sum = lax.psum_scatter(
        dec_grad.astype(jnp.bfloat16), "group", scatter_dimension=0, tiled=True
    )
    dec_sum = lax.psum(dec_sum, "dp").astype(jnp.float32)
    vocab_rows = -(-vocab_size // 32) * 32
    extra = jnp.zeros((vocab_rows, depth), jnp.float32)
    extra = lax.dynamic_update_slice(extra, dbias_grad[:, None], (0, embed_size))
    extra = lax.dynamic_update_slice(extra, loss_part.reshape(1, 1), (0, embed_size + 1))
    dec_sq = jnp.zeros((16, 128), jnp.float32).at[0, 0].set(jnp.sum(dec_sum * dec_sum))
    positions = seg_len * 2 * batch_size
    rec_sum, in_out, emb_out, clip = run_reduce(
        lax.axis_size("group") // 2,
        lax.axis_size("dp"),
        embed_size,
        kept_all.reshape(positions, hidden_size),
        embedded_one.reshape(positions, depth),
        pre_all.reshape(positions, 4 * units),
        weights[hidden_size:],
        char_major.reshape(1, positions),
        extra,
        dec_sq,
    )
    rec_grad, mom_rec_next = run_momentum(clip, rec_sum, mom_rec)
    clip_scale = clip[0, 0]
    in_sum = in_out[:embed_size].astype(jnp.float32)
    bias_sum = in_out[embed_size].astype(jnp.float32)
    emb_sum = emb_out[:vocab_size, :embed_size]
    dbias_sum = emb_out[:vocab_size, embed_size]
    loss_sum = emb_out[0, embed_size + 1].reshape(1)
    mom_in_next = momentum_step(mom_in[0], in_sum, clip_scale)
    mom_bias_next = momentum_step(mom_bias[0], bias_sum, clip_scale)
    mom_dec_next = momentum_step(mom_dec[0], dec_sum, clip_scale)
    mom_emb_next = momentum_step(mom_emb[0], emb_sum, clip_scale)
    mom_dbias_next = momentum_step(mom_dbias[0], dbias_sum, clip_scale)
    token_count = seg_len * batch_size * lax.axis_size("group") * lax.axis_size("dp")
    losses = loss_sum / token_count
    return (
        losses,
        word_vectors,
        grad_hidden0[None],
        grad_cell0[None],
        emb_sum[None],
        in_sum[None],
        rec_grad,
        bias_sum[None],
        dec_sum[None],
        dbias_sum[None],
        mom_emb_next[None],
        mom_in_next[None],
        mom_rec_next,
        mom_bias_next[None],
        mom_dec_next[None],
        mom_dbias_next[None],
    )


def solution(mesh):
    segments = P("dir", ("group", "dp"), None)
    shared = P("dir", None, None)
    columns = P("dir", None, "group")
    rows = P("dir", "group", None)
    flat = P("dir", "group")
    return jax.shard_map(
        shards,
        mesh=mesh,
        in_specs=(
            segments,
            segments,
            segments,
            segments,
            segments,
            segments,
            P(("group", "dp"), None, "dir"),
            shared,
            columns,
            rows,
            flat,
            rows,
            P("dir", None),
            shared,
            columns,
            rows,
            flat,
            rows,
            P("dir", None),
        ),
        out_specs=(
            P("dir"),
            P(("group", "dp"), "dir", None),
            segments,
            segments,
            shared,
            columns,
            rows,
            flat,
            rows,
            P("dir", None),
            shared,
            columns,
            rows,
            flat,
            rows,
            P("dir", None),
        ),
        check_vma=False,
    )
```

```python
import functools

import jax
import jax.numpy as jnp
from jax import lax
from jax.experimental import pallas as pl
from jax.experimental.pallas import tpu as pltpu
from jax.sharding import PartitionSpec as P

MESH = pl.DeviceIdType.MESH
CHUNK = 256


def partner(value, axis, bit):
    mask = 2**bit
    pairs = [(source, source ^ mask) for source in range(lax.axis_size(axis))]
    return lax.ppermute(value, axis, pairs)


def momentum_step(moment, gradient, clip_scale):
    return 0.9 * moment + clip_scale * gradient


def sigmoid(value):
    return 0.5 * jnp.tanh(0.5 * value) + 0.5


def core_peer():
    group = lax.axis_index("group")
    core = lax.rem(group, 2)
    return core, (lax.axis_index("dir"), group + 1 - 2 * core, lax.axis_index("dp"))


def greet(peers):
    barrier = pltpu.get_barrier_semaphore()
    for peer in peers:
        pl.semaphore_signal(barrier, inc=1, device_id=peer, device_id_type=MESH)
    pl.semaphore_wait(barrier, len(peers))


def gather_kernel(
    chips,
    shared,
    rec_hbm,
    inb_ref,
    h_ref,
    c_ref,
    wg_ref,
    ids_ref,
    w_hbm,
    wt_hbm,
    h_out,
    c_out,
    wg_out,
    ids_out,
    w_ref,
    wt_ref,
    stage,
    loaded,
    load_sem,
    core_send,
    core_recv,
    y_send,
    y_recv,
    z_send,
    z_recv,
    in_send,
    in_recv,
    inz_send,
    inz_recv,
    seg_send,
    seg_recv,
    w_out_sem,
    wt_out_sem,
):
    model = lax.axis_index("dir")
    group = lax.axis_index("group")
    z = lax.axis_index("dp")
    core = lax.rem(group, 2)
    chip = group // 2
    peers = 2 * chips
    rows = stage.shape[0]
    piece = loaded.shape[1]
    units = w_ref.shape[1] // 4
    hidden = 2 * units
    pieces = rows // piece
    mine = pieces // 2 if shared else pieces
    part = lax.rem(z, 2) if shared else 0
    buddy = z + 1 - 2 * lax.rem(z, 2) if shared else z
    far = list(range(2, peers))

    def owner_of(slot):
        if slot == 0:
            return group
        if slot == 1:
            return group + 1 - 2 * core
        side = core if slot % 2 == 0 else 1 - core
        return 2 * lax.rem(chip + (slot - 2) // 2 + 1, chips) + side

    def slot_there(slot):
        if slot == 1:
            return 1
        return 2 + 2 * (chips - (slot - 2) // 2 - 2) + slot % 2

    def peer(slot):
        return (model, owner_of(slot), z)

    barrier = pltpu.get_barrier_semaphore()
    for slot in range(1, peers):
        pl.semaphore_signal(barrier, inc=1, device_id=peer(slot), device_id_type=MESH)
    if shared:
        pl.semaphore_signal(
            barrier, inc=1, device_id=(model, group, buddy), device_id_type=MESH
        )

    def remote(src, dst, send, recv, device):
        return pltpu.make_async_remote_copy(
            src_ref=src,
            dst_ref=dst,
            send_sem=send,
            recv_sem=recv,
            device_id=device,
            device_id_type=MESH,
        )

    def which(i):
        return lax.rem(part * mine + i, pieces)

    def load(i):
        return pltpu.make_async_copy(
            rec_hbm.at[pl.ds(pl.multiple_of(which(i) * piece, piece), piece)],
            loaded.at[lax.rem(i, 2)],
            load_sem.at[lax.rem(i, 2)],
        )

    load(0).start()
    pl.semaphore_wait(barrier, peers if shared else peers - 1)

    def rows_of(owner, k):
        return pl.ds(pl.multiple_of(owner * rows + k * piece, piece), piece)

    def rows_staged(k):
        return pl.ds(pl.multiple_of(k * piece, piece), piece)

    def to_core(k):
        return remote(
            stage.at[rows_staged(k)],
            w_ref.at[rows_of(group, k)],
            core_send.at[k],
            core_recv.at[k],
            peer(1),
        )

    def to_chip(slot, k):
        held = w_ref.at[rows_of(group, k)] if slot % 2 == 0 else stage.at[rows_staged(k)]
        return remote(
            held,
            w_ref.at[rows_of(group, k)],
            y_send.at[slot - 2, k],
            y_recv.at[slot_there(slot) - 2, k],
            peer(slot),
        )

    def to_buddy(slot, k):
        return remote(
            w_ref.at[rows_of(owner_of(slot), k)],
            w_ref.at[rows_of(owner_of(slot), k)],
            z_send.at[slot - 2, k],
            z_recv.at[slot - 2, k],
            (model, group, buddy),
        )

    blocks = inb_ref.shape[1] // units
    deep = inb_ref.shape[0]
    in_slots = list(range(peers)) if blocks == 2 else [0] + [s for s in far if s % 2 == 0]
    share_rows = deep // 2 if shared else deep

    def in_place(owner, first, count):
        gate = owner if blocks == 2 else owner // 2
        return w_ref.at[
            pl.ds(pl.multiple_of(hidden + first, 16), count),
            pl.ds(pl.multiple_of(gate * units, units), units),
        ]

    def in_block(slot):
        if blocks == 1:
            return 0
        return core if slot == 0 or (slot > 1 and slot % 2 == 0) else 1 - core

    def in_copy(slot):
        first, count = (0, deep) if slot == 1 else (part * share_rows, share_rows)
        source = inb_ref.at[
            pl.ds(pl.multiple_of(first, 16), count),
            pl.ds(pl.multiple_of(in_block(slot) * units, units), units),
        ]
        return remote(
            source,
            in_place(group, first, count),
            in_send.at[slot - 1],
            in_recv.at[slot_there(slot) - 1],
            peer(slot),
        )

    def in_buddy(slot):
        held = in_place(owner_of(slot), part * share_rows, share_rows)
        return remote(
            held, held, inz_send.at[slot - 1], inz_recv.at[slot - 1], (model, group, buddy)
        )

    for slot in in_slots:
        if slot > 1:
            in_copy(slot).start()
    gate0 = group if blocks == 2 else chip
    w_ref[hidden:, pl.ds(pl.multiple_of(gate0 * units, units), units)] = inb_ref[
        :, pl.ds(pl.multiple_of(in_block(0) * units, units), units)
    ]

    def cast(i, carry):
        k = which(i)

        @pl.when(i + 1 < pieces)
        def _():
            load(i + 1).start()

        load(i).wait()
        buffer = lax.rem(i, 2)
        for q in range(4):
            local = pl.ds(q * units, units)
            own = pl.ds(pl.multiple_of(q * hidden + core * units, units), units)
            other = pl.ds(pl.multiple_of(q * hidden + (1 - core) * units, units), units)
            w_ref[rows_of(group, k), local] = loaded[buffer, :, own].astype(jnp.bfloat16)
            stage[rows_staged(k), local] = loaded[buffer, :, other].astype(jnp.bfloat16)

        @pl.when(i < mine)
        def _():
            for slot in far:
                to_chip(slot, k).start()

        to_core(k).start()
        return carry

    lax.fori_loop(0, pieces, cast, 0)

    seg = h_ref.shape[0]
    words = wg_ref.shape[0]
    at_h = pl.ds(pl.multiple_of(core * seg, 8), seg)
    at_w = pl.ds(pl.multiple_of(core * words, 16), words)
    half_own = pl.ds(pl.multiple_of(core * units, units), units)
    half_other = pl.ds(pl.multiple_of((1 - core) * units, units), units)
    segment_copies = [
        remote(h_ref, h_out.at[at_h], seg_send.at[0], seg_recv.at[0], peer(1)),
        remote(c_ref.at[:, half_other], c_out.at[at_h], seg_send.at[1], seg_recv.at[1], peer(1)),
        remote(wg_ref.at[:, half_other], wg_out.at[at_w], seg_send.at[2], seg_recv.at[2], peer(1)),
        remote(ids_ref, ids_out.at[at_h], seg_send.at[3], seg_recv.at[3], peer(1)),
    ]
    if blocks == 2:
        in_copy(1).start()
    for copy in segment_copies:
        copy.start()
    h_out[at_h] = h_ref[...]
    c_out[at_h] = c_ref[:, half_own]
    wg_out[at_w] = wg_ref[:, half_own]
    ids_out[at_h] = ids_ref[...]

    tall = 128

    def turn(row0):
        at = pl.ds(pl.multiple_of(row0, tall), tall)
        for q in range(4):
            local = pl.ds(q * units, units)
            wt_ref[local, at] = jnp.transpose(w_ref[at, local])

    def store(row0):
        at = pl.ds(pl.multiple_of(row0, tall), tall)
        index = row0 // tall
        return (
            pltpu.make_async_copy(w_ref.at[at], w_hbm.at[at], w_out_sem.at[index]),
            pltpu.make_async_copy(wt_ref.at[:, at], wt_hbm.at[:, at], wt_out_sem.at[index]),
        )

    def turn_and_store(row0):
        turn(row0)
        for copy in store(row0):
            copy.start()

    chip_rows = 2 * rows
    chip_tiles = chip_rows // tall
    per_tile = tall // piece

    def relay(i, carry):
        k = which(i)
        for slot in far:
            to_chip(slot, k).wait_recv()
            if shared:
                to_buddy(slot, k).start()
        return carry

    def wait_core(k, carry):
        to_core(k).wait_recv()
        return carry

    if shared:
        for slot in in_slots:
            if slot > 1:
                in_copy(slot).wait_recv()
                in_buddy(slot).start()
    relay(0, 0)
    lax.fori_loop(0, pieces, wait_core, 0)

    def own_tile(j, carry):
        turn_and_store(chip * chip_rows + j * tall)

        @pl.when(j + 1 < mine)
        def _():
            relay(j + 1, 0)

        return carry

    lax.fori_loop(0, chip_tiles, own_tile, 0)
    if mine > chip_tiles + 1:
        lax.fori_loop(chip_tiles + 1, mine, relay, 0)

    def far_tile(j, carry):
        for slot in far:
            turn_and_store(owner_of(slot) * rows + part * mine * piece + j * tall)
        return carry

    lax.fori_loop(0, mine // per_tile, far_tile, 0)

    if shared:

        def far_tile_late(j, carry):
            for slot in far:
                for p in range(per_tile):
                    k = (1 - part) * mine + j * per_tile + p
                    to_buddy(slot, k).wait_recv()
                turn_and_store(owner_of(slot) * rows + (1 - part) * mine * piece + j * tall)
            return carry

        lax.fori_loop(0, mine // per_tile, far_tile_late, 0)
        for slot in in_slots:
            if slot > 1:
                in_buddy(slot).wait_recv()
    else:
        for slot in in_slots:
            if slot > 1:
                in_copy(slot).wait_recv()
    if blocks == 2:
        in_copy(1).wait_recv()
    tail = pltpu.make_async_copy(
        w_ref.at[pl.ds(hidden, deep)], w_hbm.at[pl.ds(hidden, deep)], load_sem.at[0]
    )
    tail.start()

    for copy in segment_copies:
        copy.wait()
    for slot in in_slots:
        if slot > 0:
            in_copy(slot).wait_send()
        if slot > 1 and shared:
            in_buddy(slot).wait_send()

    def settle(i, carry):
        k = which(i)
        to_core(k).wait_send()

        @pl.when(i < mine)
        def _():
            for slot in far:
                to_chip(slot, k).wait_send()
                if shared:
                    to_buddy(slot, k).wait_send()

        return carry

    lax.fori_loop(0, pieces, settle, 0)

    def stored(j, carry):
        for copy in store(j * tall):
            copy.wait()
        return carry

    lax.fori_loop(0, hidden // tall, stored, 0)
    tail.wait()


def run_gather(chips, depth, w_rec, in_bias, h_init, c_init, word_grad, ids):
    rows, columns = w_rec.shape
    wide = columns // 2
    units = wide // 4
    hidden = 2 * units
    deep = in_bias.shape[0]
    peers = 2 * chips
    shared = depth % 2 == 0
    piece = 32
    pieces = rows // piece
    seg = h_init.shape[0]
    vmem = pl.BlockSpec(memory_space=pltpu.VMEM)
    anywhere = pl.BlockSpec(memory_space=pl.ANY)
    bf16, f32 = jnp.bfloat16, jnp.float32
    dma = pltpu.SemaphoreType.DMA
    far = max(peers - 2, 1)
    return pl.pallas_call(
        functools.partial(gather_kernel, chips, shared),
        in_specs=[anywhere] + [vmem] * 5,
        out_specs=[anywhere, anywhere] + [vmem] * 4,
        out_shape=[
            jax.ShapeDtypeStruct((hidden + deep, wide), bf16),
            jax.ShapeDtypeStruct((wide, hidden), bf16),
            jax.ShapeDtypeStruct((2 * seg, hidden), f32),
            jax.ShapeDtypeStruct((2 * seg, units), f32),
            jax.ShapeDtypeStruct((2 * word_grad.shape[0], units), bf16),
            jax.ShapeDtypeStruct((2 * seg, ids.shape[1]), jnp.int32),
        ],
        scratch_shapes=[
            pltpu.VMEM((hidden + deep, wide), bf16),
            pltpu.VMEM((wide, hidden), bf16),
            pltpu.VMEM((rows, wide), bf16),
            pltpu.VMEM((2, piece, columns), f32),
            dma((2,)),
            dma((pieces,)),
            dma((pieces,)),
            dma((far, pieces)),
            dma((far, pieces)),
            dma((far, pieces)),
            dma((far, pieces)),
            dma((peers - 1,)),
            dma((peers - 1,)),
            dma((peers - 1,)),
            dma((peers - 1,)),
            dma((4,)),
            dma((4,)),
            dma((hidden // 128,)),
            dma((hidden // 128,)),
        ],
        compiler_params=pltpu.CompilerParams(
            collective_id=4, has_side_effects=True, vmem_limit_bytes=58 << 20
        ),
        cost_estimate=pl.CostEstimate(flops=0, bytes_accessed=400 << 20, transcendentals=0),
    )(w_rec, in_bias, h_init, c_init, word_grad, ids)


def forward_kernel(
    steps,
    emb_ref,
    keep_ref,
    h0_ref,
    c0_ref,
    w_hbm,
    hid_ref,
    kept_ref,
    gates_ref,
    cell_ref,
    ckept_ref,
    w_ref,
    hown,
    hpar,
    kown,
    kpar,
    cell,
    acc,
    w_sem,
    send_sem,
    recv_sem,
):
    t = pl.program_id(0)
    slot = lax.rem(t, 2)
    nxt = 1 - slot
    core, peer = core_peer()
    units = cell.shape[1]
    hidden = 2 * units
    chunks = units // CHUNK
    own0 = pl.multiple_of(core * units, units)
    par0 = pl.multiple_of((1 - core) * units, units)

    def exchange(which, u):
        return pltpu.make_async_remote_copy(
            src_ref=hown.at[which, u],
            dst_ref=hpar.at[which, u],
            send_sem=send_sem.at[which, u],
            recv_sem=recv_sem.at[which, u],
            device_id=peer,
            device_id_type=MESH,
        )

    @pl.when(t == 0)
    def _():
        copy = pltpu.make_async_copy(w_hbm, w_ref, w_sem)
        copy.start()
        greet([peer])
        for u in range(chunks):
            hown[0, u] = h0_ref[:, pl.ds(pl.multiple_of(own0 + u * CHUNK, CHUNK), CHUNK)].astype(jnp.bfloat16)
            hpar[0, u] = h0_ref[:, pl.ds(pl.multiple_of(par0 + u * CHUNK, CHUNK), CHUNK)].astype(jnp.bfloat16)
        cell[...] = c0_ref[...]
        copy.wait()

    keep = keep_ref[0][:, :1]
    keep_b = keep.astype(jnp.bfloat16)

    def early(u):
        for q in range(4):
            cols = pl.ds(q * units + u * CHUNK, CHUNK)
            acc[q, u] = jnp.dot(
                emb_ref[0], w_ref[hidden:, cols], preferred_element_type=jnp.float32
            ) + jnp.dot(kown[...], w_ref[pl.ds(own0, units), cols], preferred_element_type=jnp.float32)

    def late(u):
        pre = []
        for q in range(4):
            cols = pl.ds(q * units + u * CHUNK, CHUNK)
            pre.append(
                acc[q, u]
                + jnp.dot(kpar[...], w_ref[pl.ds(par0, units), cols], preferred_element_type=jnp.float32)
            )
        span = pl.ds(u * CHUNK, CHUNK)
        gate_in, gate_forget, gate_cell, gate_out = (
            sigmoid(pre[0]),
            sigmoid(pre[1]),
            jnp.tanh(pre[2]),
            sigmoid(pre[3]),
        )
        kept_cell = cell[:, span] * keep
        cell_next = gate_forget * kept_cell + gate_in * gate_cell
        hown[nxt, u] = (gate_out * jnp.tanh(cell_next)).astype(jnp.bfloat16)
        cell[:, span] = cell_next
        gates_ref[0, 0, :, span] = gate_in
        gates_ref[0, 1, :, span] = gate_forget
        gates_ref[0, 2, :, span] = gate_cell
        gates_ref[0, 3, :, span] = gate_out
        cell_ref[0, :, span] = cell_next
        ckept_ref[0, :, span] = kept_cell
        exchange(nxt, u).start()

    @pl.when(t < steps)
    def _():
        for u in range(chunks):
            kown[:, pl.ds(u * CHUNK, CHUNK)] = hown[slot, u] * keep_b
        early(0)
        early(1)

    @pl.when(t > 0)
    def _():
        for u in range(chunks):
            exchange(slot, u).wait()

    for u in range(chunks):
        hid_ref[0, :, pl.ds(pl.multiple_of(own0 + u * CHUNK, CHUNK), CHUNK)] = hown[slot, u]
        hid_ref[0, :, pl.ds(pl.multiple_of(par0 + u * CHUNK, CHUNK), CHUNK)] = hpar[slot, u]

    @pl.when(t < steps)
    def _():
        for u in range(chunks):
            kpar[:, pl.ds(u * CHUNK, CHUNK)] = hpar[slot, u] * keep_b
        kept_ref[0, :, pl.ds(own0, units)] = kown[...]
        kept_ref[0, :, pl.ds(par0, units)] = kpar[...]
        for u in range(chunks):
            late(u)
            if u + 2 < chunks:
                early(u + 2)


def run_forward(embedded, keep, h0, c0, weights):
    steps, rows, depth = embedded.shape
    units = c0.shape[1]
    hidden = 2 * units
    chunks = units // CHUNK

    def at(t):
        return jnp.minimum(t, steps - 1)

    whole = pl.BlockSpec(memory_space=pltpu.VMEM)
    return pl.pallas_call(
        functools.partial(forward_kernel, steps),
        grid=(steps + 1,),
        in_specs=[
            pl.BlockSpec((1, rows, depth), lambda t: (at(t), 0, 0)),
            pl.BlockSpec((1, rows, 128), lambda t: (at(t), 0, 0)),
            whole,
            whole,
            pl.BlockSpec(memory_space=pl.ANY),
        ],
        out_specs=[
            pl.BlockSpec((1, rows, hidden), lambda t: (t, 0, 0)),
            pl.BlockSpec((1, rows, hidden), lambda t: (at(t), 0, 0)),
            pl.BlockSpec((1, 4, rows, units), lambda t: (at(t), 0, 0, 0)),
            pl.BlockSpec((1, rows, units), lambda t: (at(t), 0, 0)),
            pl.BlockSpec((1, rows, units), lambda t: (at(t), 0, 0)),
        ],
        out_shape=[
            jax.ShapeDtypeStruct((steps + 1, rows, hidden), jnp.bfloat16),
            jax.ShapeDtypeStruct((steps, rows, hidden), jnp.bfloat16),
            jax.ShapeDtypeStruct((steps, 4, rows, units), jnp.float32),
            jax.ShapeDtypeStruct((steps, rows, units), jnp.float32),
            jax.ShapeDtypeStruct((steps, rows, units), jnp.float32),
        ],
        scratch_shapes=[
            pltpu.VMEM(weights.shape, jnp.bfloat16),
            pltpu.VMEM((2, chunks, rows, CHUNK), jnp.bfloat16),
            pltpu.VMEM((2, chunks, rows, CHUNK), jnp.bfloat16),
            pltpu.VMEM((rows, units), jnp.bfloat16),
            pltpu.VMEM((rows, units), jnp.bfloat16),
            pltpu.VMEM((rows, units), jnp.float32),
            pltpu.VMEM((4, chunks, rows, CHUNK), jnp.float32),
            pltpu.SemaphoreType.DMA,
            pltpu.SemaphoreType.DMA((2, chunks)),
            pltpu.SemaphoreType.DMA((2, chunks)),
        ],
        compiler_params=pltpu.CompilerParams(
            collective_id=1, has_side_effects=True, vmem_limit_bytes=56 << 20
        ),
        cost_estimate=pl.CostEstimate(
            flops=2 * steps * rows * weights.shape[0] * weights.shape[1],
            bytes_accessed=500 << 20,
            transcendentals=0,
        ),
    )(embedded, keep, h0, c0, weights)


def backward_kernel(
    steps,
    outg_ref,
    gates_ref,
    cell_ref,
    ckept_ref,
    keep_ref,
    w_hbm,
    pre_ref,
    gh_ref,
    gc_ref,
    w_ref,
    dh,
    dc,
    pg,
    outbox,
    inbox,
    w_sem,
    send_sem,
    recv_sem,
):
    i = pl.program_id(0)
    slot = lax.rem(i, 2)
    core, peer = core_peer()
    units = dh.shape[1]
    chunks = units // CHUNK
    own0 = pl.multiple_of(core * units, units)
    par0 = pl.multiple_of((1 - core) * units, units)

    def exchange(which, u):
        return pltpu.make_async_remote_copy(
            src_ref=outbox.at[which, u],
            dst_ref=inbox.at[which, u],
            send_sem=send_sem.at[which, u],
            recv_sem=recv_sem.at[which, u],
            device_id=peer,
            device_id_type=MESH,
        )

    @pl.when(i == 0)
    def _():
        copy = pltpu.make_async_copy(w_hbm, w_ref, w_sem)
        copy.start()
        greet([peer])
        dh[...] = jnp.zeros_like(dh)
        dc[...] = jnp.zeros_like(dc)
        copy.wait()

    @pl.when(i > 0)
    def _():
        for u in range(chunks):
            exchange(1 - slot, u).wait()
        for u in range(chunks):
            span = pl.ds(u * CHUNK, CHUNK)
            dh[:, span] = dh[:, span] + inbox[1 - slot, u]

    keep = keep_ref[0][:, :1]
    for u in range(chunks):
        span = pl.ds(u * CHUNK, CHUNK)
        gate_in = gates_ref[0, 0, :, span]
        gate_forget = gates_ref[0, 1, :, span]
        gate_cell = gates_ref[0, 2, :, span]
        gate_out = gates_ref[0, 3, :, span]
        total_hidden = dh[:, span] + outg_ref[0, :, span]
        tanh_cell = jnp.tanh(cell_ref[0, :, span])
        total_cell = dc[:, span] + total_hidden * gate_out * (1.0 - tanh_cell * tanh_cell)
        grads = [
            total_cell * gate_cell * gate_in * (1.0 - gate_in),
            total_cell * ckept_ref[0, :, span] * gate_forget * (1.0 - gate_forget),
            total_cell * gate_in * (1.0 - gate_cell * gate_cell),
            total_hidden * tanh_cell * gate_out * (1.0 - gate_out),
        ]
        for q in range(4):
            grad = grads[q].astype(jnp.bfloat16)
            pg[:, pl.ds(q * units + u * CHUNK, CHUNK)] = grad
            pre_ref[0, :, pl.ds(q * units + u * CHUNK, CHUNK)] = grad
        dc[:, span] = total_cell * gate_forget * keep
    for u in range(chunks):
        cols = pl.ds(pl.multiple_of(par0 + u * CHUNK, CHUNK), CHUNK)
        outbox[slot, u] = (
            jnp.dot(pg[...], w_ref[:, cols], preferred_element_type=jnp.float32) * keep
        )
        exchange(slot, u).start()
    for u in range(chunks):
        cols = pl.ds(pl.multiple_of(own0 + u * CHUNK, CHUNK), CHUNK)
        dh[:, pl.ds(u * CHUNK, CHUNK)] = (
            jnp.dot(pg[...], w_ref[:, cols], preferred_element_type=jnp.float32) * keep
        )

    @pl.when(i == steps - 1)
    def _():
        for u in range(chunks):
            exchange(slot, u).wait()
        for u in range(chunks):
            span = pl.ds(u * CHUNK, CHUNK)
            gh_ref[:, span] = dh[:, span] + inbox[slot, u]
        gc_ref[...] = dc[...]


def run_backward(out_grad, gates, cells, cells_kept, keep, weights_t):
    steps, rows, units = out_grad.shape
    chunks = units // CHUNK

    def back(i):
        return (steps - 1 - i, 0, 0)

    row_block = pl.BlockSpec((1, rows, units), back)
    whole = pl.BlockSpec(memory_space=pltpu.VMEM)
    return pl.pallas_call(
        functools.partial(backward_kernel, steps),
        grid=(steps,),
        in_specs=[
            row_block,
            pl.BlockSpec((1, 4, rows, units), lambda i: (steps - 1 - i, 0, 0, 0)),
            row_block,
            row_block,
            pl.BlockSpec((1, rows, 128), back),
            pl.BlockSpec(memory_space=pl.ANY),
        ],
        out_specs=[pl.BlockSpec((1, rows, 4 * units), back), whole, whole],
        out_shape=[
            jax.ShapeDtypeStruct((steps, rows, 4 * units), jnp.bfloat16),
            jax.ShapeDtypeStruct((rows, units), jnp.float32),
            jax.ShapeDtypeStruct((rows, units), jnp.float32),
        ],
        scratch_shapes=[
            pltpu.VMEM(weights_t.shape, jnp.bfloat16),
            pltpu.VMEM((rows, units), jnp.float32),
            pltpu.VMEM((rows, units), jnp.float32),
            pltpu.VMEM((rows, 4 * units), jnp.bfloat16),
            pltpu.VMEM((2, chunks, rows, CHUNK), jnp.float32),
            pltpu.VMEM((2, chunks, rows, CHUNK), jnp.float32),
            pltpu.SemaphoreType.DMA,
            pltpu.SemaphoreType.DMA((2, chunks)),
            pltpu.SemaphoreType.DMA((2, chunks)),
        ],
        compiler_params=pltpu.CompilerParams(
            collective_id=2, has_side_effects=True, vmem_limit_bytes=56 << 20
        ),
        cost_estimate=pl.CostEstimate(
            flops=2 * steps * rows * weights_t.shape[0] * weights_t.shape[1],
            bytes_accessed=500 << 20,
            transcendentals=0,
        ),
    )(out_grad, gates, cells, cells_kept, keep, weights_t)


def reduce_kernel(
    chips,
    depth,
    embed,
    kept_ref,
    aug_ref,
    pre_ref,
    in_ref,
    chars_ref,
    extra_ref,
    decsq_ref,
    rec_hbm,
    inout_ref,
    emb_ref,
    clip_ref,
    turned,
    inbox,
    outbox,
    partial,
    final,
    in_all,
    in_box,
    in_mine,
    in_part,
    in_final,
    in_swap,
    emb_box,
    emb_mine,
    emb_part,
    emb_final,
    ssq,
    norm_box,
    y_send,
    y_recv,
    part_recv,
    final_recv,
    part_send,
    final_send,
    write_sem,
    in_send,
    in_recv,
    emb_send,
    emb_recv,
    misc_recv,
    misc_send,
    norm_send,
    norm_recv,
):
    model = lax.axis_index("dir")
    group = lax.axis_index("group")
    z = lax.axis_index("dp")
    core = lax.rem(group, 2)
    chip = group // 2
    peers = 2 * chips
    middle = depth // 2
    rows_out = kept_ref.shape[1] // peers
    wide = pre_ref.shape[1]
    tall = turned.shape[0]
    lot = tall // 16
    batches = rows_out // tall
    groups = rows_out // 16
    per_pass = lot // peers
    upper = depth - 1 > middle
    is_middle = z == middle
    low = z < middle
    has_away = jnp.logical_or(jnp.logical_and(low, z > 0), jnp.logical_and(z > middle, z < depth - 1))
    toward = jnp.where(low, z + 1, jnp.maximum(z - 1, 0))
    away = jnp.where(low, jnp.maximum(z - 1, 0), jnp.minimum(z + 1, depth - 1))

    def in_group(index):
        return (model, index, z)

    def in_line(index):
        return (model, group, index)

    def owner_of(slot):
        if slot == 0:
            return group
        if slot == 1:
            return group + 1 - 2 * core
        step = (slot - 2) // 2 + 1
        side = core if slot % 2 == 0 else 1 - core
        return 2 * lax.rem(chip + step, chips) + side

    def slot_there(slot):
        if slot == 1:
            return 1
        step = (slot - 2) // 2 + 1
        return 2 + 2 * (chips - step - 1) + slot % 2

    barrier = pltpu.get_barrier_semaphore()
    for slot in range(1, peers):
        pl.semaphore_signal(barrier, inc=1, device_id=in_group(owner_of(slot)), device_id_type=MESH)

    @pl.when(z > 0)
    def _():
        pl.semaphore_signal(
            barrier, inc=1, device_id=in_line(jnp.maximum(z - 1, 0)), device_id_type=MESH
        )

    @pl.when(z < depth - 1)
    def _():
        pl.semaphore_signal(
            barrier, inc=1, device_id=in_line(jnp.minimum(z + 1, depth - 1)), device_id_type=MESH
        )

    pl.semaphore_wait(
        barrier,
        peers - 1 + jnp.where(z > 0, 1, 0) + jnp.where(z < depth - 1, 1, 0),
    )
    ssq[...] = jnp.zeros_like(ssq)

    def remote(src, dst, send, recv, device):
        return pltpu.make_async_remote_copy(
            src_ref=src,
            dst_ref=dst,
            send_sem=send,
            recv_sem=recv,
            device_id=device,
            device_id_type=MESH,
        )

    def squares(value):
        square = value * value
        total = square[:, :128]
        for lane in range(128, value.shape[1], 128):
            total = total + square[:, lane : lane + 128]
        rows = total[:16]
        for row in range(16, value.shape[0], 16):
            rows = rows + total[row : row + 16]
        ssq[...] = ssq[...] + rows

    def send_partial(mine, part, fin, sems):
        @pl.when(jnp.logical_not(is_middle))
        def _():
            @pl.when(has_away)
            def _():
                remote(mine, part, sems["ps"], sems["pr"], in_line(away)).wait_recv()
                mine[...] = (
                    mine[...].astype(jnp.float32) + part[...].astype(jnp.float32)
                ).astype(mine.dtype)

            if upper:

                @pl.when(z == middle + 1)
                def _():
                    remote(mine, fin, sems["ps"], sems["fr"], in_line(toward)).start()

            @pl.when(z != middle + 1)
            def _():
                remote(mine, part, sems["ps"], sems["pr"], in_line(toward)).start()

        @pl.when(is_middle)
        def _():
            remote(mine, part, sems["ps"], sems["pr"], in_line(toward)).wait_recv()
            total = mine[...].astype(jnp.float32) + part[...].astype(jnp.float32)
            if upper:
                remote(mine, fin, sems["ps"], sems["fr"], in_line(toward)).wait_recv()
                total = total + fin[...].astype(jnp.float32)
            fin[...] = total.astype(fin.dtype)
            remote(fin, fin, sems["f0"], sems["fr"], in_line(middle - 1)).start()
            if upper:
                remote(fin, fin, sems["f1"], sems["fr"], in_line(middle + 1)).start()

    def pass_final(fin, sems):
        @pl.when(jnp.logical_not(is_middle))
        def _():
            remote(fin, fin, sems["f0"], sems["fr"], in_line(toward)).wait_recv()

            @pl.when(has_away)
            def _():
                remote(fin, fin, sems["f0"], sems["fr"], in_line(away)).start()

    def wait_line(mine, fin, sems):
        @pl.when(is_middle)
        def _():
            remote(fin, fin, sems["f0"], sems["fr"], in_line(toward)).wait_send()
            if upper:
                remote(fin, fin, sems["f1"], sems["fr"], in_line(toward)).wait_send()

        @pl.when(jnp.logical_not(is_middle))
        def _():
            remote(mine, fin, sems["ps"], sems["fr"], in_line(toward)).wait_send()

            @pl.when(has_away)
            def _():
                remote(fin, fin, sems["f0"], sems["fr"], in_line(away)).wait_send()

    def line_sems(unit):
        return {
            "pr": part_recv.at[unit],
            "fr": final_recv.at[unit],
            "ps": part_send.at[unit],
            "f0": final_send.at[0, unit],
            "f1": final_send.at[1, unit],
        }

    units = 2 * groups
    in_sems, emb_sems = line_sems(units), line_sems(units + 1)

    def send_block(slot, parity, index, row):
        return remote(
            outbox.at[slot - 1, parity, index],
            inbox.at[slot_there(slot), row],
            y_send.at[slot - 1, parity, index],
            y_recv.at[slot_there(slot) - 1, row],
            in_group(owner_of(slot)),
        )

    span = 1024

    def product(dest):
        def columns(j, carry):
            cols = pl.ds(pl.multiple_of(j * span, span), span)
            dest[:, :, cols] = (
                jnp.dot(turned[...], pre_ref[:, cols], preferred_element_type=jnp.float32)
                .astype(jnp.bfloat16)
                .reshape(lot, 16, span)
            )
            return carry

        lax.fori_loop(0, wide // span, columns, 0)

    def block(slot, b, parity):
        start = owner_of(slot) * rows_out + b * tall
        turned[...] = jnp.transpose(kept_ref[:, pl.ds(pl.multiple_of(start, tall), tall)])
        if slot == 0:
            product(inbox.at[0, pl.ds(b * lot, lot)])
        else:

            @pl.when(b >= 2)
            def _():
                for index in range(lot):
                    send_block(slot, parity, index, 0).wait_send()

            product(outbox.at[slot - 1, parity])

    def send(row):
        parity, index = lax.rem(row // lot, 2), lax.rem(row, lot)
        for slot in list(range(2, peers)) + [1]:
            send_block(slot, parity, index, row).start()

    def take(row):
        for slot in range(1, peers):
            remote(
                outbox.at[slot - 1, 0, 0],
                inbox.at[slot, row],
                y_send.at[slot - 1, 0, 0],
                y_recv.at[slot - 1, row],
                in_group(owner_of(slot)),
            ).wait_recv()
        for part in range(2):
            if chips > 1:
                total = inbox[part, row].astype(jnp.float32)
                for slot in range(2 + part, peers, 2):
                    total = total + inbox[slot, row].astype(jnp.float32)
                inbox[part, row] = total.astype(jnp.bfloat16)
            send_partial(
                inbox.at[part, row],
                partial.at[2 * row + part],
                final.at[2 * row + part],
                line_sems(2 * row + part),
            )

    def write_out(row, part):
        side = core if part == 0 else 1 - core
        return pltpu.make_async_copy(
            final.at[2 * row + part],
            rec_hbm.at[side, pl.ds(pl.multiple_of(row * 16, 16), 16)],
            write_sem.at[2 * row + part],
        )

    def finish(row):
        for part in range(2):
            pass_final(final.at[2 * row + part], line_sems(2 * row + part))
            write_out(row, part).start()
            squares(final[2 * row + part].astype(jnp.float32))

    in_rows, in_wide = in_mine.shape

    def in_columns(index):
        return pl.ds(pl.multiple_of(index * in_wide, in_wide), in_wide)

    def in_copy(step):
        there = lax.rem(chip + step, chips)
        return remote(
            in_all.at[:, in_columns(there)],
            in_box.at[chips - step - 1],
            in_send.at[step - 1],
            in_recv.at[chips - step - 1],
            in_group(2 * there + core),
        )

    def emb_copy(slot, source):
        return remote(
            emb_mine,
            emb_box.at[source],
            emb_send.at[slot - 1],
            emb_recv.at[source],
            in_group(owner_of(slot)),
        )

    def small_products():
        turned[...] = jnp.transpose(aug_ref[...])

        def columns(j, carry):
            cols = pl.ds(pl.multiple_of(j * span, span), span)
            in_all[:, cols] = jnp.dot(
                turned[...], pre_ref[:, cols], preferred_element_type=jnp.float32
            )[:in_rows].astype(jnp.bfloat16)
            return carry

        lax.fori_loop(0, wide // span, columns, 0)
        for step in range(1, chips):
            in_copy(step).start()
        into = lax.dot_general(
            pre_ref[...], in_ref[...], (((1,), (1,)), ((), ())), preferred_element_type=jnp.float32
        ).astype(jnp.bfloat16)
        vocab_rows = emb_mine.shape[0]
        ids = lax.broadcasted_iota(jnp.int32, (vocab_rows, chars_ref.shape[1]), 0)
        onehot = jnp.where(chars_ref[...] == ids, 1.0, 0.0).astype(jnp.bfloat16)
        summed = jnp.dot(onehot, into, preferred_element_type=jnp.float32)
        lanes = lax.broadcasted_iota(jnp.int32, summed.shape, 1)
        emb_mine[...] = jnp.where(lanes < embed, summed, 0.0) + extra_ref[...]
        for slot in range(1, peers):
            emb_copy(slot, group).start()

    def small_partials():
        for step in range(1, chips):
            in_copy(step).wait_recv()
        total = in_all[:, in_columns(chip)].astype(jnp.float32)
        for step in range(1, chips):
            total = total + in_box[step - 1].astype(jnp.float32)
        in_mine[...] = total.astype(jnp.bfloat16)
        send_partial(in_mine, in_part, in_final, in_sems)
        for slot in range(1, peers):
            emb_copy(slot, owner_of(slot)).wait_recv()
        for slot in range(1, peers):
            emb_copy(slot, group).wait_send()
        emb_box[group] = emb_mine[...]
        total = emb_box[0]
        for source in range(1, peers):
            total = total + emb_box[source]
        emb_mine[...] = total
        send_partial(emb_mine, emb_part, emb_final, emb_sems)

    def small_finals():
        pass_final(in_final, in_sems)
        squares(in_final[...].astype(jnp.float32))
        pass_final(emb_final, emb_sems)

    order = list(range(2, peers)) + [1, 0]
    lead = (peers - 2) * per_pass
    y_lag, hop_lag = 3, 4
    hops = jnp.where(low, middle - z, z - middle)
    most_hops = max(middle, depth - 1 - middle)
    steps = groups + y_lag + hop_lag * most_hops + lead
    rounds = max(-(-steps // lot), 3 + most_hops)

    def round_of(b, carry):
        parity = lax.rem(b, 2)

        @pl.when(b == 1)
        def _():
            small_products()

        for turn, slot in enumerate(order):

            @pl.when(b < batches)
            def _():
                block(slot, b, parity)

            def step(j, inner):
                row = b * lot + turn * per_pass + j - lead
                arrived = row - y_lag
                summed = arrived - hop_lag * hops

                @pl.when(jnp.logical_and(row >= 0, row < groups))
                def _():
                    send(row)

                @pl.when(jnp.logical_and(arrived >= 0, arrived < groups))
                def _():
                    take(arrived)

                @pl.when(jnp.logical_and(summed >= 0, summed < groups))
                def _():
                    finish(summed)

                return inner

            lax.fori_loop(0, per_pass, step, 0)

        @pl.when(b == 2)
        def _():
            small_partials()

        @pl.when(b == 2 + hops)
        def _():
            small_finals()

        return carry

    lax.fori_loop(0, rounds, round_of, 0)

    keep_cols = in_wide // 2
    if in_wide > wide // 4:
        mine = pl.ds(pl.multiple_of(core * keep_cols, keep_cols), keep_cols)
        theirs = pl.ds(pl.multiple_of((1 - core) * keep_cols, keep_cols), keep_cols)
        swap = remote(
            in_final.at[:, theirs], in_swap, misc_send, misc_recv, in_group(owner_of(1))
        )
        swap.start()
        swap.wait()
        inout_ref[:, mine] = in_final[:, mine]
        inout_ref[:, theirs] = in_swap[...]
    else:
        inout_ref[...] = in_final[...]
    emb_ref[...] = emb_final[...]

    ssq[...] = ssq[...] + decsq_ref[...]
    norm_box[group] = ssq[...]

    def norm_copy(slot, source):
        return remote(
            ssq,
            norm_box.at[source],
            norm_send.at[slot - 1],
            norm_recv.at[source],
            in_group(owner_of(slot)),
        )

    for slot in range(1, peers):
        norm_copy(slot, group).start()
    for slot in range(1, peers):
        norm_copy(slot, owner_of(slot)).wait_recv()
    for slot in range(1, peers):
        norm_copy(slot, group).wait_send()
    total = norm_box[0]
    for source in range(1, peers):
        total = total + norm_box[source]
    lanes = lax.broadcasted_iota(jnp.int32, emb_final.shape, 1)
    small = jnp.where(lanes <= embed, emb_final[...], 0.0)
    total_sq = jnp.sum(total) + jnp.sum(small * small)
    clip_ref[...] = jnp.full(clip_ref.shape, 0.25, jnp.float32) / jnp.maximum(
        jnp.sqrt(jnp.full(clip_ref.shape, total_sq, jnp.float32)), 0.25
    )

    for step in range(1, chips):
        in_copy(step).wait_send()
    wait_line(in_mine, in_final, in_sems)
    wait_line(emb_mine, emb_final, emb_sems)
    for slot in range(1, peers):
        for parity in range(min(2, batches)):
            for index in range(lot):
                send_block(slot, parity, index, 0).wait_send()

    def settle(row, carry):
        for part in range(2):
            wait_line(
                inbox.at[part, row], final.at[2 * row + part], line_sems(2 * row + part)
            )
            write_out(row, part).wait()
        return carry

    lax.fori_loop(0, groups, settle, 0)


def run_reduce(chips, depth, embed, kept, aug, pre, in_own, chars, extra, dec_sq):
    hidden = kept.shape[1]
    count, wide = pre.shape
    peers = 2 * chips
    rows_out = hidden // peers
    tall = 128
    lot = tall // 16
    groups = rows_out // 16
    units = 2 * groups
    in_rows = -(-(embed + 1) // 16) * 16
    in_wide = wide // chips
    in_cols = 2 * wide // peers
    vmem = pl.BlockSpec(memory_space=pltpu.VMEM)
    bf16, f32 = jnp.bfloat16, jnp.float32
    small = extra.shape
    dma = pltpu.SemaphoreType.DMA
    return pl.pallas_call(
        functools.partial(reduce_kernel, chips, depth, embed),
        in_specs=[vmem] * 7,
        out_specs=[pl.BlockSpec(memory_space=pl.ANY), vmem, vmem, vmem],
        out_shape=[
            jax.ShapeDtypeStruct((2, rows_out, wide), bf16),
            jax.ShapeDtypeStruct((in_rows, in_cols), bf16),
            jax.ShapeDtypeStruct(small, f32),
            jax.ShapeDtypeStruct((8, 128), f32),
        ],
        scratch_shapes=[
            pltpu.VMEM((tall, count), bf16),
            pltpu.VMEM((peers, groups, 16, wide), bf16),
            pltpu.VMEM((peers - 1, 2, lot, 16, wide), bf16),
            pltpu.VMEM((units, 16, wide), bf16),
            pltpu.VMEM((units, 16, wide), bf16),
            pltpu.VMEM((in_rows, wide), bf16),
            pltpu.VMEM((max(chips - 1, 1), in_rows, in_wide), bf16),
            pltpu.VMEM((in_rows, in_wide), bf16),
            pltpu.VMEM((in_rows, in_wide), bf16),
            pltpu.VMEM((in_rows, in_wide), bf16),
            pltpu.VMEM((in_rows, in_wide // 2), bf16),
            pltpu.VMEM((peers,) + small, f32),
            pltpu.VMEM(small, f32),
            pltpu.VMEM(small, f32),
            pltpu.VMEM(small, f32),
            pltpu.VMEM((16, 128), f32),
            pltpu.VMEM((peers, 16, 128), f32),
            dma((peers - 1, 2, lot)),
            dma((peers - 1, groups)),
            dma((units + 2,)),
            dma((units + 2,)),
            dma((units + 2,)),
            dma((2, units + 2)),
            dma((units,)),
            dma((max(chips - 1, 1),)),
            dma((max(chips - 1, 1),)),
            dma((peers - 1,)),
            dma((peers,)),
            dma,
            dma,
            dma((peers - 1,)),
            dma((peers,)),
        ],
        compiler_params=pltpu.CompilerParams(
            collective_id=3, has_side_effects=True, vmem_limit_bytes=60 << 20
        ),
        cost_estimate=pl.CostEstimate(
            flops=2 * count * hidden * wide, bytes_accessed=700 << 20, transcendentals=0
        ),
    )(kept, aug, pre, in_own, chars, extra, dec_sq)


def momentum_kernel(clip_ref, sum_ref, moment_ref, grad_ref, next_ref):
    gradient = sum_ref[0].astype(jnp.float32)
    grad_ref[0] = gradient
    next_ref[0] = momentum_step(moment_ref[0], gradient, clip_ref[0, 0])


def run_momentum(clip, sums, moment):
    halves, rows, wide = sums.shape
    span = wide // 4
    block = pl.BlockSpec((1, rows, span), lambda q, s: (0, 0, 2 * q + s))
    shape = jax.ShapeDtypeStruct(moment.shape, jnp.float32)
    return pl.pallas_call(
        momentum_kernel,
        grid=(4, 2),
        in_specs=[
            pl.BlockSpec(memory_space=pltpu.SMEM),
            pl.BlockSpec((1, rows, span), lambda q, s: (s, 0, q)),
            block,
        ],
        out_specs=[block, block],
        out_shape=[shape, shape],
        compiler_params=pltpu.CompilerParams(vmem_limit_bytes=48 << 20),
    )(clip, sums, moment)


def shards(
    chars,
    targets,
    resets,
    word_pos,
    h_init,
    c_init,
    word_grad,
    w_emb,
    w_in,
    w_rec,
    b_rec,
    w_dec,
    b_dec,
    mom_emb,
    mom_in,
    mom_rec,
    mom_bias,
    mom_dec,
    mom_dbias,
):
    vocab_size = w_emb.shape[1]
    embed_size = w_emb.shape[2]
    seg_len = chars.shape[2]
    batch_size = chars.shape[1]
    hidden_size = w_rec.shape[2] // 4
    units = hidden_size // 2
    core = lax.rem(lax.axis_index("group"), 2)
    first = core == 0

    depth = 128
    dec_full = lax.all_gather(w_dec[0].astype(jnp.bfloat16), "group", axis=0, tiled=True)
    in_bias = jnp.concatenate(
        [w_in[0], b_rec, jnp.zeros((depth - embed_size - 1, w_in.shape[2]), jnp.float32)]
    ).astype(jnp.bfloat16)
    word_slots = word_pos.shape[2]
    spare = -(3 * seg_len + word_slots) % 128
    ids = jnp.concatenate(
        [
            chars[0],
            targets[0],
            resets[0],
            word_pos[0],
            jnp.zeros((batch_size, spare), jnp.int32),
        ],
        axis=1,
    )
    weights, weights_t, h_pair, c_pair, wg_pair, packed = run_gather(
        lax.axis_size("group") // 2,
        lax.axis_size("dp"),
        w_rec[0],
        in_bias,
        h_init[0],
        c_init[0],
        word_grad.reshape(batch_size * word_slots, hidden_size),
        ids,
    )
    wg_pair = wg_pair.reshape(2 * batch_size, word_slots, units)
    chars2 = packed[:, :seg_len]
    targets2 = packed[:, seg_len : 2 * seg_len]
    resets2 = packed[:, 2 * seg_len : 3 * seg_len]
    word_pos2 = packed[:, 3 * seg_len : 3 * seg_len + word_slots]
    char_major = jnp.transpose(chars2)
    char_onehot = (char_major[:, :, None] == jnp.arange(vocab_size, dtype=jnp.int32)).astype(
        jnp.bfloat16
    )
    embedded = jnp.einsum(
        "tbv,ve->tbe",
        char_onehot,
        w_emb[0].astype(jnp.bfloat16),
        preferred_element_type=jnp.float32,
    ).astype(jnp.bfloat16)
    pad_shape = (seg_len, 2 * batch_size, depth - embed_size - 1)
    embedded_one = jnp.concatenate(
        [
            embedded,
            jnp.ones((seg_len, 2 * batch_size, 1), jnp.bfloat16),
            jnp.zeros(pad_shape, jnp.bfloat16),
        ],
        axis=-1,
    )
    keep_major = jnp.broadcast_to(
        (1 - jnp.transpose(resets2)).astype(jnp.float32)[:, :, None],
        (seg_len, 2 * batch_size, 128),
    )
    hidden_all, kept_all, gate_all, cell_all, cellkept_all = run_forward(
        embedded_one, keep_major, h_pair, c_pair, weights
    )
    out_all = hidden_all[1:]
    logits = (
        jnp.einsum("tbh,hv->tbv", out_all, dec_full, preferred_element_type=jnp.float32) + b_dec[0]
    )
    log_probs = jax.nn.log_softmax(logits, axis=-1)
    target_onehot = (
        jnp.transpose(targets2)[:, :, None] == jnp.arange(vocab_size, dtype=jnp.int32)
    ).astype(jnp.float32)
    loss_part = -0.5 * jnp.sum(log_probs * target_onehot)
    logit_grad = ((jnp.exp(log_probs) - target_onehot) / seg_len).astype(jnp.bfloat16)
    from_output = jnp.einsum(
        "tbv,hv->tbh",
        logit_grad,
        lax.dynamic_slice_in_dim(dec_full, core * units, units, 0),
        preferred_element_type=jnp.float32,
    )
    pos_onehot2 = (word_pos2[:, :, None] == jnp.arange(seg_len, dtype=jnp.int32)).astype(
        jnp.bfloat16
    )
    from_words = jnp.einsum(
        "bkt,bkh->tbh", pos_onehot2, wg_pair, preferred_element_type=jnp.float32
    )
    out_own = lax.dynamic_slice_in_dim(out_all, core * batch_size, batch_size, 1)
    pos_onehot = (word_pos[0][:, :, None] == jnp.arange(seg_len, dtype=jnp.int32)).astype(
        jnp.bfloat16
    )
    picked = jnp.einsum(
        "bkt,tbh->bkh", pos_onehot, out_own, preferred_element_type=jnp.float32
    ).astype(jnp.bfloat16)
    half_slots = picked.shape[1] // 2
    model_index = lax.axis_index("dir")
    own_slots = lax.dynamic_slice_in_dim(picked, model_index * half_slots, half_slots, 1)
    other_slots = lax.dynamic_slice_in_dim(picked, (1 - model_index) * half_slots, half_slots, 1)
    partner_half = partner(other_slots, "dir", 0)
    leading = model_index == 0
    word_vectors = jnp.where(
        leading,
        jnp.concatenate([own_slots, partner_half], axis=-1),
        jnp.concatenate([partner_half, own_slots], axis=-1),
    )
    pre_all, gh_pair, gc_pair = run_backward(
        from_output + from_words, gate_all, cell_all, cellkept_all, keep_major, weights_t
    )

    def own_rows(value):
        mine = lax.dynamic_slice_in_dim(value, core * batch_size, batch_size, 0)
        theirs = lax.dynamic_slice_in_dim(value, (1 - core) * batch_size, batch_size, 0)
        other = partner(theirs, "group", 0)
        return jnp.where(
            first,
            jnp.concatenate([mine, other], axis=1),
            jnp.concatenate([other, mine], axis=1),
        )

    grad_hidden0 = own_rows(gh_pair)
    grad_cell0 = own_rows(gc_pair)
    lg_own = lax.dynamic_slice_in_dim(logit_grad, core * batch_size, batch_size, 1)
    dec_grad = jnp.einsum("tbh,tbv->hv", out_own, lg_own, preferred_element_type=jnp.float32)
    dbias_grad = jnp.sum(lg_own, axis=(0, 1), dtype=jnp.float32)
    dec_sum = lax.psum_scatter(
        dec_grad.astype(jnp.bfloat16), "group", scatter_dimension=0, tiled=True
    )
    dec_sum = lax.psum(dec_sum, "dp").astype(jnp.float32)
    vocab_rows = -(-vocab_size // 32) * 32
    extra = jnp.zeros((vocab_rows, depth), jnp.float32)
    extra = lax.dynamic_update_slice(extra, dbias_grad[:, None], (0, embed_size))
    extra = lax.dynamic_update_slice(extra, loss_part.reshape(1, 1), (0, embed_size + 1))
    dec_sq = jnp.zeros((16, 128), jnp.float32).at[0, 0].set(jnp.sum(dec_sum * dec_sum))
    positions = seg_len * 2 * batch_size
    rec_sum, in_out, emb_out, clip = run_reduce(
        lax.axis_size("group") // 2,
        lax.axis_size("dp"),
        embed_size,
        kept_all.reshape(positions, hidden_size),
        embedded_one.reshape(positions, depth),
        pre_all.reshape(positions, 4 * units),
        weights[hidden_size:],
        char_major.reshape(1, positions),
        extra,
        dec_sq,
    )
    rec_grad, mom_rec_next = run_momentum(clip, rec_sum, mom_rec)
    clip_scale = clip[0, 0]
    in_sum = in_out[:embed_size].astype(jnp.float32)
    bias_sum = in_out[embed_size].astype(jnp.float32)
    emb_sum = emb_out[:vocab_size, :embed_size]
    dbias_sum = emb_out[:vocab_size, embed_size]
    loss_sum = emb_out[0, embed_size + 1].reshape(1)
    mom_in_next = momentum_step(mom_in[0], in_sum, clip_scale)
    mom_bias_next = momentum_step(mom_bias[0], bias_sum, clip_scale)
    mom_dec_next = momentum_step(mom_dec[0], dec_sum, clip_scale)
    mom_emb_next = momentum_step(mom_emb[0], emb_sum, clip_scale)
    mom_dbias_next = momentum_step(mom_dbias[0], dbias_sum, clip_scale)
    token_count = seg_len * batch_size * lax.axis_size("group") * lax.axis_size("dp")
    losses = loss_sum / token_count
    return (
        losses,
        word_vectors,
        grad_hidden0[None],
        grad_cell0[None],
        emb_sum[None],
        in_sum[None],
        rec_grad,
        bias_sum[None],
        dec_sum[None],
        dbias_sum[None],
        mom_emb_next[None],
        mom_in_next[None],
        mom_rec_next,
        mom_bias_next[None],
        mom_dec_next[None],
        mom_dbias_next[None],
    )


def solution(mesh):
    segments = P("dir", ("group", "dp"), None)
    shared = P("dir", None, None)
    columns = P("dir", None, "group")
    rows = P("dir", "group", None)
    flat = P("dir", "group")
    return jax.shard_map(
        shards,
        mesh=mesh,
        in_specs=(
            segments,
            segments,
            segments,
            segments,
            segments,
            segments,
            P(("group", "dp"), None, "dir"),
            shared,
            columns,
            rows,
            flat,
            rows,
            P("dir", None),
            shared,
            columns,
            rows,
            flat,
            rows,
            P("dir", None),
        ),
        out_specs=(
            P("dir"),
            P(("group", "dp"), "dir", None),
            segments,
            segments,
            shared,
            columns,
            rows,
            flat,
            rows,
            P("dir", None),
            shared,
            columns,
            rows,
            flat,
            rows,
            P("dir", None),
        ),
        check_vma=False,
    )
```

```python
import functools

import jax
import jax.numpy as jnp
from jax import lax
from jax.experimental import pallas as pl
from jax.experimental.pallas import tpu as pltpu
from jax.sharding import PartitionSpec as P

MESH = pl.DeviceIdType.MESH
CHUNK = 256


def partner(value, axis, bit):
    mask = 2**bit
    pairs = [(source, source ^ mask) for source in range(lax.axis_size(axis))]
    return lax.ppermute(value, axis, pairs)


def momentum_step(moment, gradient, clip_scale):
    return 0.9 * moment + clip_scale * gradient


def sigmoid(value):
    return 0.5 * jnp.tanh(0.5 * value) + 0.5


def core_peer():
    group = lax.axis_index("group")
    core = lax.rem(group, 2)
    return core, (lax.axis_index("dir"), group + 1 - 2 * core, lax.axis_index("dp"))


def greet(peers):
    barrier = pltpu.get_barrier_semaphore()
    for peer in peers:
        pl.semaphore_signal(barrier, inc=1, device_id=peer, device_id_type=MESH)
    pl.semaphore_wait(barrier, len(peers))


def gather_kernel(
    chips,
    shared,
    rec_hbm,
    inb_ref,
    h_ref,
    c_ref,
    wg_ref,
    ids_ref,
    w_hbm,
    wt_hbm,
    h_out,
    c_out,
    wg_out,
    ids_out,
    w_ref,
    wt_ref,
    stage,
    loaded,
    load_sem,
    core_send,
    core_recv,
    y_send,
    y_recv,
    z_send,
    z_recv,
    in_send,
    in_recv,
    inz_send,
    inz_recv,
    seg_send,
    seg_recv,
    w_out_sem,
    wt_out_sem,
):
    model = lax.axis_index("dir")
    group = lax.axis_index("group")
    z = lax.axis_index("dp")
    core = lax.rem(group, 2)
    chip = group // 2
    peers = 2 * chips
    rows = stage.shape[0]
    piece = loaded.shape[1]
    units = w_ref.shape[1] // 4
    hidden = 2 * units
    pieces = rows // piece
    mine = pieces // 2 if shared else pieces
    part = lax.rem(z, 2) if shared else 0
    buddy = z + 1 - 2 * lax.rem(z, 2) if shared else z
    far = list(range(2, peers))

    def owner_of(slot):
        if slot == 0:
            return group
        if slot == 1:
            return group + 1 - 2 * core
        side = core if slot % 2 == 0 else 1 - core
        return 2 * lax.rem(chip + (slot - 2) // 2 + 1, chips) + side

    def slot_there(slot):
        if slot == 1:
            return 1
        return 2 + 2 * (chips - (slot - 2) // 2 - 2) + slot % 2

    def peer(slot):
        return (model, owner_of(slot), z)

    barrier = pltpu.get_barrier_semaphore()
    for slot in range(1, peers):
        pl.semaphore_signal(barrier, inc=1, device_id=peer(slot), device_id_type=MESH)
    if shared:
        pl.semaphore_signal(
            barrier, inc=1, device_id=(model, group, buddy), device_id_type=MESH
        )

    def remote(src, dst, send, recv, device):
        return pltpu.make_async_remote_copy(
            src_ref=src,
            dst_ref=dst,
            send_sem=send,
            recv_sem=recv,
            device_id=device,
            device_id_type=MESH,
        )

    def which(i):
        return lax.rem(part * mine + i, pieces)

    def load(i):
        return pltpu.make_async_copy(
            rec_hbm.at[pl.ds(pl.multiple_of(which(i) * piece, piece), piece)],
            loaded.at[lax.rem(i, 2)],
            load_sem.at[lax.rem(i, 2)],
        )

    load(0).start()
    pl.semaphore_wait(barrier, peers if shared else peers - 1)

    def rows_of(owner, k):
        return pl.ds(pl.multiple_of(owner * rows + k * piece, piece), piece)

    def rows_staged(k):
        return pl.ds(pl.multiple_of(k * piece, piece), piece)

    def to_core(k):
        return remote(
            stage.at[rows_staged(k)],
            w_ref.at[rows_of(group, k)],
            core_send.at[k],
            core_recv.at[k],
            peer(1),
        )

    def to_chip(slot, k):
        held = w_ref.at[rows_of(group, k)] if slot % 2 == 0 else stage.at[rows_staged(k)]
        return remote(
            held,
            w_ref.at[rows_of(group, k)],
            y_send.at[slot - 2, k],
            y_recv.at[slot_there(slot) - 2, k],
            peer(slot),
        )

    def to_buddy(slot, k):
        return remote(
            w_ref.at[rows_of(owner_of(slot), k)],
            w_ref.at[rows_of(owner_of(slot), k)],
            z_send.at[slot - 2, k],
            z_recv.at[slot - 2, k],
            (model, group, buddy),
        )

    blocks = inb_ref.shape[1] // units
    deep = inb_ref.shape[0]
    in_slots = list(range(peers)) if blocks == 2 else [0] + [s for s in far if s % 2 == 0]
    share_rows = deep // 2 if shared else deep

    def in_place(owner, first, count):
        gate = owner if blocks == 2 else owner // 2
        return w_ref.at[
            pl.ds(pl.multiple_of(hidden + first, 16), count),
            pl.ds(pl.multiple_of(gate * units, units), units),
        ]

    def in_block(slot):
        if blocks == 1:
            return 0
        return core if slot == 0 or (slot > 1 and slot % 2 == 0) else 1 - core

    def in_copy(slot):
        first, count = (0, deep) if slot == 1 else (part * share_rows, share_rows)
        source = inb_ref.at[
            pl.ds(pl.multiple_of(first, 16), count),
            pl.ds(pl.multiple_of(in_block(slot) * units, units), units),
        ]
        return remote(
            source,
            in_place(group, first, count),
            in_send.at[slot - 1],
            in_recv.at[slot_there(slot) - 1],
            peer(slot),
        )

    def in_buddy(slot):
        held = in_place(owner_of(slot), part * share_rows, share_rows)
        return remote(
            held, held, inz_send.at[slot - 1], inz_recv.at[slot - 1], (model, group, buddy)
        )

    for slot in in_slots:
        if slot > 1:
            in_copy(slot).start()
    gate0 = group if blocks == 2 else chip
    w_ref[hidden:, pl.ds(pl.multiple_of(gate0 * units, units), units)] = inb_ref[
        :, pl.ds(pl.multiple_of(in_block(0) * units, units), units)
    ]

    def cast(i, carry):
        k = which(i)

        @pl.when(i + 1 < pieces)
        def _():
            load(i + 1).start()

        load(i).wait()
        buffer = lax.rem(i, 2)
        for q in range(4):
            local = pl.ds(q * units, units)
            own = pl.ds(pl.multiple_of(q * hidden + core * units, units), units)
            other = pl.ds(pl.multiple_of(q * hidden + (1 - core) * units, units), units)
            w_ref[rows_of(group, k), local] = loaded[buffer, :, own].astype(jnp.bfloat16)
            stage[rows_staged(k), local] = loaded[buffer, :, other].astype(jnp.bfloat16)

        @pl.when(i < mine)
        def _():
            for slot in far:
                to_chip(slot, k).start()

        to_core(k).start()
        return carry

    lax.fori_loop(0, pieces, cast, 0)

    seg = h_ref.shape[0]
    words = wg_ref.shape[0]
    at_h = pl.ds(pl.multiple_of(core * seg, 8), seg)
    at_w = pl.ds(pl.multiple_of(core * words, 16), words)
    half_own = pl.ds(pl.multiple_of(core * units, units), units)
    half_other = pl.ds(pl.multiple_of((1 - core) * units, units), units)
    segment_copies = [
        remote(h_ref, h_out.at[at_h], seg_send.at[0], seg_recv.at[0], peer(1)),
        remote(c_ref.at[:, half_other], c_out.at[at_h], seg_send.at[1], seg_recv.at[1], peer(1)),
        remote(wg_ref.at[:, half_other], wg_out.at[at_w], seg_send.at[2], seg_recv.at[2], peer(1)),
        remote(ids_ref, ids_out.at[at_h], seg_send.at[3], seg_recv.at[3], peer(1)),
    ]
    if blocks == 2:
        in_copy(1).start()
    for copy in segment_copies:
        copy.start()
    h_out[at_h] = h_ref[...]
    c_out[at_h] = c_ref[:, half_own]
    wg_out[at_w] = wg_ref[:, half_own]
    ids_out[at_h] = ids_ref[...]

    tall = 128

    def turn(row0):
        at = pl.ds(pl.multiple_of(row0, tall), tall)
        for q in range(4):
            local = pl.ds(q * units, units)
            wt_ref[local, at] = jnp.transpose(w_ref[at, local])

    def store(row0):
        at = pl.ds(pl.multiple_of(row0, tall), tall)
        index = row0 // tall
        return (
            pltpu.make_async_copy(w_ref.at[at], w_hbm.at[at], w_out_sem.at[index]),
            pltpu.make_async_copy(wt_ref.at[:, at], wt_hbm.at[:, at], wt_out_sem.at[index]),
        )

    def turn_and_store(row0):
        turn(row0)
        for copy in store(row0):
            copy.start()

    chip_rows = 2 * rows
    chip_tiles = chip_rows // tall
    per_tile = tall // piece

    def relay(i, carry):
        k = which(i)
        for slot in far:
            to_chip(slot, k).wait_recv()
            if shared:
                to_buddy(slot, k).start()
        return carry

    def wait_core(k, carry):
        to_core(k).wait_recv()
        return carry

    if shared:
        for slot in in_slots:
            if slot > 1:
                in_copy(slot).wait_recv()
                in_buddy(slot).start()
    relay(0, 0)
    lax.fori_loop(0, pieces, wait_core, 0)

    def own_tile(j, carry):
        turn_and_store(chip * chip_rows + j * tall)

        @pl.when(j + 1 < mine)
        def _():
            relay(j + 1, 0)

        return carry

    lax.fori_loop(0, chip_tiles, own_tile, 0)
    if mine > chip_tiles + 1:
        lax.fori_loop(chip_tiles + 1, mine, relay, 0)

    def far_tile(j, carry):
        for slot in far:
            turn_and_store(owner_of(slot) * rows + part * mine * piece + j * tall)
        return carry

    lax.fori_loop(0, mine // per_tile, far_tile, 0)

    if shared:

        def far_tile_late(j, carry):
            for slot in far:
                for p in range(per_tile):
                    k = (1 - part) * mine + j * per_tile + p
                    to_buddy(slot, k).wait_recv()
                turn_and_store(owner_of(slot) * rows + (1 - part) * mine * piece + j * tall)
            return carry

        lax.fori_loop(0, mine // per_tile, far_tile_late, 0)
        for slot in in_slots:
            if slot > 1:
                in_buddy(slot).wait_recv()
    else:
        for slot in in_slots:
            if slot > 1:
                in_copy(slot).wait_recv()
    if blocks == 2:
        in_copy(1).wait_recv()
    tail = pltpu.make_async_copy(
        w_ref.at[pl.ds(hidden, deep)], w_hbm.at[pl.ds(hidden, deep)], load_sem.at[0]
    )
    tail.start()

    for copy in segment_copies:
        copy.wait()
    for slot in in_slots:
        if slot > 0:
            in_copy(slot).wait_send()
        if slot > 1 and shared:
            in_buddy(slot).wait_send()

    def settle(i, carry):
        k = which(i)
        to_core(k).wait_send()

        @pl.when(i < mine)
        def _():
            for slot in far:
                to_chip(slot, k).wait_send()
                if shared:
                    to_buddy(slot, k).wait_send()

        return carry

    lax.fori_loop(0, pieces, settle, 0)

    def stored(j, carry):
        for copy in store(j * tall):
            copy.wait()
        return carry

    lax.fori_loop(0, hidden // tall, stored, 0)
    tail.wait()


def run_gather(chips, depth, w_rec, in_bias, h_init, c_init, word_grad, ids):
    rows, columns = w_rec.shape
    wide = columns // 2
    units = wide // 4
    hidden = 2 * units
    deep = in_bias.shape[0]
    peers = 2 * chips
    shared = depth % 2 == 0
    piece = 32
    pieces = rows // piece
    seg = h_init.shape[0]
    vmem = pl.BlockSpec(memory_space=pltpu.VMEM)
    anywhere = pl.BlockSpec(memory_space=pl.ANY)
    bf16, f32 = jnp.bfloat16, jnp.float32
    dma = pltpu.SemaphoreType.DMA
    far = max(peers - 2, 1)
    return pl.pallas_call(
        functools.partial(gather_kernel, chips, shared),
        in_specs=[anywhere] + [vmem] * 5,
        out_specs=[anywhere, anywhere] + [vmem] * 4,
        out_shape=[
            jax.ShapeDtypeStruct((hidden + deep, wide), bf16),
            jax.ShapeDtypeStruct((wide, hidden), bf16),
            jax.ShapeDtypeStruct((2 * seg, hidden), f32),
            jax.ShapeDtypeStruct((2 * seg, units), f32),
            jax.ShapeDtypeStruct((2 * word_grad.shape[0], units), bf16),
            jax.ShapeDtypeStruct((2 * seg, ids.shape[1]), jnp.int32),
        ],
        scratch_shapes=[
            pltpu.VMEM((hidden + deep, wide), bf16),
            pltpu.VMEM((wide, hidden), bf16),
            pltpu.VMEM((rows, wide), bf16),
            pltpu.VMEM((2, piece, columns), f32),
            dma((2,)),
            dma((pieces,)),
            dma((pieces,)),
            dma((far, pieces)),
            dma((far, pieces)),
            dma((far, pieces)),
            dma((far, pieces)),
            dma((peers - 1,)),
            dma((peers - 1,)),
            dma((peers - 1,)),
            dma((peers - 1,)),
            dma((4,)),
            dma((4,)),
            dma((hidden // 128,)),
            dma((hidden // 128,)),
        ],
        compiler_params=pltpu.CompilerParams(
            collective_id=4, has_side_effects=True, vmem_limit_bytes=58 << 20
        ),
        cost_estimate=pl.CostEstimate(flops=0, bytes_accessed=400 << 20, transcendentals=0),
    )(w_rec, in_bias, h_init, c_init, word_grad, ids)


def forward_kernel(
    steps,
    emb_ref,
    keep_ref,
    h0_ref,
    c0_ref,
    w_hbm,
    hid_ref,
    kept_ref,
    gates_ref,
    cell_ref,
    ckept_ref,
    w_ref,
    hown,
    hpar,
    kown,
    kpar,
    cell,
    acc,
    w_sem,
    send_sem,
    recv_sem,
):
    t = pl.program_id(0)
    slot = lax.rem(t, 2)
    nxt = 1 - slot
    core, peer = core_peer()
    units = cell.shape[1]
    hidden = 2 * units
    chunks = units // CHUNK
    own0 = pl.multiple_of(core * units, units)
    par0 = pl.multiple_of((1 - core) * units, units)

    def exchange(which, u):
        return pltpu.make_async_remote_copy(
            src_ref=hown.at[which, u],
            dst_ref=hpar.at[which, u],
            send_sem=send_sem.at[which, u],
            recv_sem=recv_sem.at[which, u],
            device_id=peer,
            device_id_type=MESH,
        )

    @pl.when(t == 0)
    def _():
        copy = pltpu.make_async_copy(w_hbm, w_ref, w_sem)
        copy.start()
        greet([peer])
        for u in range(chunks):
            hown[0, u] = h0_ref[:, pl.ds(pl.multiple_of(own0 + u * CHUNK, CHUNK), CHUNK)].astype(jnp.bfloat16)
            hpar[0, u] = h0_ref[:, pl.ds(pl.multiple_of(par0 + u * CHUNK, CHUNK), CHUNK)].astype(jnp.bfloat16)
        cell[...] = c0_ref[...]
        copy.wait()

    keep = keep_ref[0][:, :1]
    keep_b = keep.astype(jnp.bfloat16)

    def early(u):
        for q in range(4):
            cols = pl.ds(q * units + u * CHUNK, CHUNK)
            acc[q, u] = jnp.dot(
                emb_ref[0], w_ref[hidden:, cols], preferred_element_type=jnp.float32
            ) + jnp.dot(kown[...], w_ref[pl.ds(own0, units), cols], preferred_element_type=jnp.float32)

    def late(u):
        pre = []
        for q in range(4):
            cols = pl.ds(q * units + u * CHUNK, CHUNK)
            pre.append(
                acc[q, u]
                + jnp.dot(kpar[...], w_ref[pl.ds(par0, units), cols], preferred_element_type=jnp.float32)
            )
        span = pl.ds(u * CHUNK, CHUNK)
        gate_in, gate_forget, gate_cell, gate_out = (
            sigmoid(pre[0]),
            sigmoid(pre[1]),
            jnp.tanh(pre[2]),
            sigmoid(pre[3]),
        )
        kept_cell = cell[:, span] * keep
        cell_next = gate_forget * kept_cell + gate_in * gate_cell
        hown[nxt, u] = (gate_out * jnp.tanh(cell_next)).astype(jnp.bfloat16)
        cell[:, span] = cell_next
        gates_ref[0, 0, :, span] = gate_in
        gates_ref[0, 1, :, span] = gate_forget
        gates_ref[0, 2, :, span] = gate_cell
        gates_ref[0, 3, :, span] = gate_out
        cell_ref[0, :, span] = cell_next
        ckept_ref[0, :, span] = kept_cell
        exchange(nxt, u).start()

    @pl.when(t < steps)
    def _():
        for u in range(chunks):
            kown[:, pl.ds(u * CHUNK, CHUNK)] = hown[slot, u] * keep_b
        early(0)
        early(1)

    @pl.when(t > 0)
    def _():
        for u in range(chunks):
            exchange(slot, u).wait()

    for u in range(chunks):
        hid_ref[0, :, pl.ds(pl.multiple_of(own0 + u * CHUNK, CHUNK), CHUNK)] = hown[slot, u]
        hid_ref[0, :, pl.ds(pl.multiple_of(par0 + u * CHUNK, CHUNK), CHUNK)] = hpar[slot, u]

    @pl.when(t < steps)
    def _():
        for u in range(chunks):
            kpar[:, pl.ds(u * CHUNK, CHUNK)] = hpar[slot, u] * keep_b
        kept_ref[0, :, pl.ds(own0, units)] = kown[...]
        kept_ref[0, :, pl.ds(par0, units)] = kpar[...]
        for u in range(chunks):
            late(u)
            if u + 2 < chunks:
                early(u + 2)


def run_forward(embedded, keep, h0, c0, weights):
    steps, rows, depth = embedded.shape
    units = c0.shape[1]
    hidden = 2 * units
    chunks = units // CHUNK

    def at(t):
        return jnp.minimum(t, steps - 1)

    whole = pl.BlockSpec(memory_space=pltpu.VMEM)
    return pl.pallas_call(
        functools.partial(forward_kernel, steps),
        grid=(steps + 1,),
        in_specs=[
            pl.BlockSpec((1, rows, depth), lambda t: (at(t), 0, 0)),
            pl.BlockSpec((1, rows, 128), lambda t: (at(t), 0, 0)),
            whole,
            whole,
            pl.BlockSpec(memory_space=pl.ANY),
        ],
        out_specs=[
            pl.BlockSpec((1, rows, hidden), lambda t: (jnp.maximum(t - 1, 0), 0, 0)),
            pl.BlockSpec((1, rows, hidden), lambda t: (at(t), 0, 0)),
            pl.BlockSpec((1, 4, rows, units), lambda t: (at(t), 0, 0, 0)),
            pl.BlockSpec((1, rows, units), lambda t: (at(t), 0, 0)),
            pl.BlockSpec((1, rows, units), lambda t: (at(t), 0, 0)),
        ],
        out_shape=[
            jax.ShapeDtypeStruct((steps, rows, hidden), jnp.bfloat16),
            jax.ShapeDtypeStruct((steps, rows, hidden), jnp.bfloat16),
            jax.ShapeDtypeStruct((steps, 4, rows, units), jnp.float32),
            jax.ShapeDtypeStruct((steps, rows, units), jnp.float32),
            jax.ShapeDtypeStruct((steps, rows, units), jnp.float32),
        ],
        scratch_shapes=[
            pltpu.VMEM(weights.shape, jnp.bfloat16),
            pltpu.VMEM((2, chunks, rows, CHUNK), jnp.bfloat16),
            pltpu.VMEM((2, chunks, rows, CHUNK), jnp.bfloat16),
            pltpu.VMEM((rows, units), jnp.bfloat16),
            pltpu.VMEM((rows, units), jnp.bfloat16),
            pltpu.VMEM((rows, units), jnp.float32),
            pltpu.VMEM((4, chunks, rows, CHUNK), jnp.float32),
            pltpu.SemaphoreType.DMA,
            pltpu.SemaphoreType.DMA((2, chunks)),
            pltpu.SemaphoreType.DMA((2, chunks)),
        ],
        compiler_params=pltpu.CompilerParams(
            collective_id=1, has_side_effects=True, vmem_limit_bytes=56 << 20
        ),
        cost_estimate=pl.CostEstimate(
            flops=2 * steps * rows * weights.shape[0] * weights.shape[1],
            bytes_accessed=500 << 20,
            transcendentals=0,
        ),
    )(embedded, keep, h0, c0, weights)


def backward_kernel(
    steps,
    outg_ref,
    gates_ref,
    cell_ref,
    ckept_ref,
    keep_ref,
    w_hbm,
    pre_ref,
    gh_ref,
    gc_ref,
    w_ref,
    dh,
    dc,
    pg,
    outbox,
    inbox,
    w_sem,
    send_sem,
    recv_sem,
):
    i = pl.program_id(0)
    slot = lax.rem(i, 2)
    core, peer = core_peer()
    units = dh.shape[1]
    chunks = units // CHUNK
    own0 = pl.multiple_of(core * units, units)
    par0 = pl.multiple_of((1 - core) * units, units)

    def exchange(which, u):
        return pltpu.make_async_remote_copy(
            src_ref=outbox.at[which, u],
            dst_ref=inbox.at[which, u],
            send_sem=send_sem.at[which, u],
            recv_sem=recv_sem.at[which, u],
            device_id=peer,
            device_id_type=MESH,
        )

    @pl.when(i == 0)
    def _():
        copy = pltpu.make_async_copy(w_hbm, w_ref, w_sem)
        copy.start()
        greet([peer])
        dh[...] = jnp.zeros_like(dh)
        dc[...] = jnp.zeros_like(dc)
        copy.wait()

    @pl.when(i > 0)
    def _():
        for u in range(chunks):
            exchange(1 - slot, u).wait()
        for u in range(chunks):
            span = pl.ds(u * CHUNK, CHUNK)
            dh[:, span] = dh[:, span] + inbox[1 - slot, u]

    keep = keep_ref[0][:, :1]
    for u in range(chunks):
        span = pl.ds(u * CHUNK, CHUNK)
        gate_in = gates_ref[0, 0, :, span]
        gate_forget = gates_ref[0, 1, :, span]
        gate_cell = gates_ref[0, 2, :, span]
        gate_out = gates_ref[0, 3, :, span]
        total_hidden = dh[:, span] + outg_ref[0, :, span]
        tanh_cell = jnp.tanh(cell_ref[0, :, span])
        total_cell = dc[:, span] + total_hidden * gate_out * (1.0 - tanh_cell * tanh_cell)
        grads = [
            total_cell * gate_cell * gate_in * (1.0 - gate_in),
            total_cell * ckept_ref[0, :, span] * gate_forget * (1.0 - gate_forget),
            total_cell * gate_in * (1.0 - gate_cell * gate_cell),
            total_hidden * tanh_cell * gate_out * (1.0 - gate_out),
        ]
        for q in range(4):
            grad = grads[q].astype(jnp.bfloat16)
            pg[:, pl.ds(q * units + u * CHUNK, CHUNK)] = grad
            pre_ref[0, :, pl.ds(q * units + u * CHUNK, CHUNK)] = grad
        dc[:, span] = total_cell * gate_forget * keep
    for u in range(chunks):
        cols = pl.ds(pl.multiple_of(par0 + u * CHUNK, CHUNK), CHUNK)
        outbox[slot, u] = (
            jnp.dot(pg[...], w_ref[:, cols], preferred_element_type=jnp.float32) * keep
        )
        exchange(slot, u).start()
    for u in range(chunks):
        cols = pl.ds(pl.multiple_of(own0 + u * CHUNK, CHUNK), CHUNK)
        dh[:, pl.ds(u * CHUNK, CHUNK)] = (
            jnp.dot(pg[...], w_ref[:, cols], preferred_element_type=jnp.float32) * keep
        )

    @pl.when(i == steps - 1)
    def _():
        for u in range(chunks):
            exchange(slot, u).wait()
        for u in range(chunks):
            span = pl.ds(u * CHUNK, CHUNK)
            gh_ref[:, span] = dh[:, span] + inbox[slot, u]
        gc_ref[...] = dc[...]


def run_backward(out_grad, gates, cells, cells_kept, keep, weights_t):
    steps, rows, units = out_grad.shape
    chunks = units // CHUNK

    def back(i):
        return (steps - 1 - i, 0, 0)

    row_block = pl.BlockSpec((1, rows, units), back)
    whole = pl.BlockSpec(memory_space=pltpu.VMEM)
    return pl.pallas_call(
        functools.partial(backward_kernel, steps),
        grid=(steps,),
        in_specs=[
            row_block,
            pl.BlockSpec((1, 4, rows, units), lambda i: (steps - 1 - i, 0, 0, 0)),
            row_block,
            row_block,
            pl.BlockSpec((1, rows, 128), back),
            pl.BlockSpec(memory_space=pl.ANY),
        ],
        out_specs=[pl.BlockSpec((1, rows, 4 * units), back), whole, whole],
        out_shape=[
            jax.ShapeDtypeStruct((steps, rows, 4 * units), jnp.bfloat16),
            jax.ShapeDtypeStruct((rows, units), jnp.float32),
            jax.ShapeDtypeStruct((rows, units), jnp.float32),
        ],
        scratch_shapes=[
            pltpu.VMEM(weights_t.shape, jnp.bfloat16),
            pltpu.VMEM((rows, units), jnp.float32),
            pltpu.VMEM((rows, units), jnp.float32),
            pltpu.VMEM((rows, 4 * units), jnp.bfloat16),
            pltpu.VMEM((2, chunks, rows, CHUNK), jnp.float32),
            pltpu.VMEM((2, chunks, rows, CHUNK), jnp.float32),
            pltpu.SemaphoreType.DMA,
            pltpu.SemaphoreType.DMA((2, chunks)),
            pltpu.SemaphoreType.DMA((2, chunks)),
        ],
        compiler_params=pltpu.CompilerParams(
            collective_id=2, has_side_effects=True, vmem_limit_bytes=56 << 20
        ),
        cost_estimate=pl.CostEstimate(
            flops=2 * steps * rows * weights_t.shape[0] * weights_t.shape[1],
            bytes_accessed=500 << 20,
            transcendentals=0,
        ),
    )(out_grad, gates, cells, cells_kept, keep, weights_t)


def reduce_kernel(
    chips,
    depth,
    embed,
    kept_ref,
    aug_ref,
    pre_ref,
    in_ref,
    chars_ref,
    extra_ref,
    decsq_ref,
    rec_hbm,
    inout_ref,
    emb_ref,
    clip_ref,
    turned,
    fetched,
    fetch_sem,
    inbox,
    outbox,
    partial,
    final,
    in_all,
    in_box,
    in_final,
    in_swap,
    emb_box,
    emb_mine,
    emb_part,
    emb_final,
    ssq,
    norm_box,
    y_send,
    y_recv,
    part_recv,
    final_recv,
    part_send,
    final_send,
    write_sem,
    in_send,
    in_recv,
    emb_send,
    emb_recv,
    misc_recv,
    misc_send,
    norm_send,
    norm_recv,
):
    model = lax.axis_index("dir")
    group = lax.axis_index("group")
    z = lax.axis_index("dp")
    core = lax.rem(group, 2)
    chip = group // 2
    peers = 2 * chips
    middle = depth // 2
    rows_out = kept_ref.shape[1] // peers
    wide = pre_ref.shape[1]
    tall = turned.shape[0]
    lot = tall // 16
    batches = rows_out // tall
    groups = rows_out // 16
    per_pass = lot // peers
    upper = depth - 1 > middle
    is_middle = z == middle
    low = z < middle
    has_away = jnp.logical_or(jnp.logical_and(low, z > 0), jnp.logical_and(z > middle, z < depth - 1))
    toward = jnp.where(low, z + 1, jnp.maximum(z - 1, 0))
    away = jnp.where(low, jnp.maximum(z - 1, 0), jnp.minimum(z + 1, depth - 1))

    def in_group(index):
        return (model, index, z)

    def in_line(index):
        return (model, group, index)

    def owner_of(slot):
        if slot == 0:
            return group
        if slot == 1:
            return group + 1 - 2 * core
        step = (slot - 2) // 2 + 1
        side = core if slot % 2 == 0 else 1 - core
        return 2 * lax.rem(chip + step, chips) + side

    def slot_there(slot):
        if slot == 1:
            return 1
        step = (slot - 2) // 2 + 1
        return 2 + 2 * (chips - step - 1) + slot % 2

    order = list(range(2, peers)) + [1, 0]
    barrier = pltpu.get_barrier_semaphore()
    for slot in range(1, peers):
        pl.semaphore_signal(barrier, inc=1, device_id=in_group(owner_of(slot)), device_id_type=MESH)

    @pl.when(z > 0)
    def _():
        pl.semaphore_signal(
            barrier, inc=1, device_id=in_line(jnp.maximum(z - 1, 0)), device_id_type=MESH
        )

    @pl.when(z < depth - 1)
    def _():
        pl.semaphore_signal(
            barrier, inc=1, device_id=in_line(jnp.minimum(z + 1, depth - 1)), device_id_type=MESH
        )

    pl.semaphore_wait(
        barrier,
        peers - 1 + jnp.where(z > 0, 1, 0) + jnp.where(z < depth - 1, 1, 0),
    )
    ssq[...] = jnp.zeros_like(ssq)

    def remote(src, dst, send, recv, device):
        return pltpu.make_async_remote_copy(
            src_ref=src,
            dst_ref=dst,
            send_sem=send,
            recv_sem=recv,
            device_id=device,
            device_id_type=MESH,
        )

    def squares(value):
        square = value * value
        total = square[:, :128]
        for lane in range(128, value.shape[1], 128):
            total = total + square[:, lane : lane + 128]
        rows = total[:16]
        for row in range(16, value.shape[0], 16):
            rows = rows + total[row : row + 16]
        ssq[...] = ssq[...] + rows

    def send_partial(mine, part, fin, sems):
        @pl.when(jnp.logical_not(is_middle))
        def _():
            @pl.when(has_away)
            def _():
                remote(mine, part, sems["ps"], sems["pr"], in_line(away)).wait_recv()
                mine[...] = (
                    mine[...].astype(jnp.float32) + part[...].astype(jnp.float32)
                ).astype(mine.dtype)

            if upper:

                @pl.when(z == middle + 1)
                def _():
                    remote(mine, fin, sems["ps"], sems["fr"], in_line(toward)).start()

            @pl.when(z != middle + 1)
            def _():
                remote(mine, part, sems["ps"], sems["pr"], in_line(toward)).start()

        @pl.when(is_middle)
        def _():
            remote(mine, part, sems["ps"], sems["pr"], in_line(toward)).wait_recv()
            total = mine[...].astype(jnp.float32) + part[...].astype(jnp.float32)
            if upper:
                remote(mine, fin, sems["ps"], sems["fr"], in_line(toward)).wait_recv()
                total = total + fin[...].astype(jnp.float32)
            fin[...] = total.astype(fin.dtype)
            remote(fin, fin, sems["f0"], sems["fr"], in_line(middle - 1)).start()
            if upper:
                remote(fin, fin, sems["f1"], sems["fr"], in_line(middle + 1)).start()

    def pass_final(fin, sems):
        @pl.when(jnp.logical_not(is_middle))
        def _():
            remote(fin, fin, sems["f0"], sems["fr"], in_line(toward)).wait_recv()

            @pl.when(has_away)
            def _():
                remote(fin, fin, sems["f0"], sems["fr"], in_line(away)).start()

    def wait_line(mine, fin, sems):
        @pl.when(is_middle)
        def _():
            remote(fin, fin, sems["f0"], sems["fr"], in_line(toward)).wait_send()
            if upper:
                remote(fin, fin, sems["f1"], sems["fr"], in_line(toward)).wait_send()

        @pl.when(jnp.logical_not(is_middle))
        def _():
            remote(mine, fin, sems["ps"], sems["fr"], in_line(toward)).wait_send()

            @pl.when(has_away)
            def _():
                remote(fin, fin, sems["f0"], sems["fr"], in_line(away)).wait_send()

    def line_sems(unit):
        return {
            "pr": part_recv.at[unit],
            "fr": final_recv.at[unit],
            "ps": part_send.at[unit],
            "f0": final_send.at[0, unit],
            "f1": final_send.at[1, unit],
        }

    extra_rows = 4 // chips
    emb_sems = line_sems(2 * (groups + extra_rows))

    def send_block(slot, parity, index, row):
        return remote(
            outbox.at[slot - 1, parity, index],
            inbox.at[slot_there(slot), row],
            y_send.at[slot - 1, parity, index],
            y_recv.at[slot_there(slot) - 1, row],
            in_group(owner_of(slot)),
        )

    span = 1024

    def product(dest):
        def columns(j, carry):
            cols = pl.ds(pl.multiple_of(j * span, span), span)
            dest[:, :, cols] = (
                jnp.dot(turned[...], pre_ref[:, cols], preferred_element_type=jnp.float32)
                .astype(jnp.bfloat16)
                .reshape(lot, 16, span)
            )
            return carry

        lax.fori_loop(0, wide // span, columns, 0)

    def fetch(turn, b):
        start = owner_of(order[turn]) * rows_out + b * tall
        return pltpu.make_async_copy(
            kept_ref.at[:, pl.ds(pl.multiple_of(start, tall), tall)],
            fetched.at[turn % 2],
            fetch_sem.at[turn % 2],
        )

    def block(turn, b, parity):
        slot = order[turn]
        if turn + 1 < peers:
            fetch(turn + 1, b).start()
        else:

            @pl.when(b + 1 < batches)
            def _():
                fetch(0, b + 1).start()

        fetch(turn, b).wait()
        turned[...] = jnp.transpose(fetched[turn % 2])
        if slot == 0:
            product(inbox.at[0, pl.ds(b * lot, lot)])
        else:

            @pl.when(b >= 2)
            def _():
                for index in range(lot):
                    send_block(slot, parity, index, 0).wait_send()

            product(outbox.at[slot - 1, parity])

    def send(row):
        parity, index = lax.rem(row // lot, 2), lax.rem(row, lot)
        for slot in list(range(2, peers)) + [1]:
            send_block(slot, parity, index, row).start()

    def take(row):
        @pl.when(row < groups)
        def _():
            for slot in range(1, peers):
                remote(
                    outbox.at[slot - 1, 0, 0],
                    inbox.at[slot, row],
                    y_send.at[slot - 1, 0, 0],
                    y_recv.at[slot - 1, row],
                    in_group(owner_of(slot)),
                ).wait_recv()
            if chips > 1:
                for part in range(2):
                    total = inbox[part, row].astype(jnp.float32)
                    for slot in range(2 + part, peers, 2):
                        total = total + inbox[slot, row].astype(jnp.float32)
                    inbox[part, row] = total.astype(jnp.bfloat16)

        @pl.when(row == groups)
        def _():
            for step in range(1, chips):
                in_copy(step).wait_recv()

        @pl.when(row >= groups)
        def _():
            for part in range(2):
                for k in range(chips):
                    first = (2 * (row - groups) + part) * chips + k
                    at = pl.ds(pl.multiple_of(first * 16, 16), 16)
                    total = in_all[at, in_columns(chip)].astype(jnp.float32)
                    for step in range(1, chips):
                        total = total + in_box[step - 1, at].astype(jnp.float32)
                    inbox[part, row, :, pl.ds(k * in_wide, in_wide)] = total.astype(jnp.bfloat16)

        for part in range(2):
            send_partial(
                inbox.at[part, row],
                partial.at[2 * row + part],
                final.at[2 * row + part],
                line_sems(2 * row + part),
            )

    def write_out(row, part):
        side = core if part == 0 else 1 - core
        return pltpu.make_async_copy(
            final.at[2 * row + part],
            rec_hbm.at[side, pl.ds(pl.multiple_of(row * 16, 16), 16)],
            write_sem.at[2 * row + part],
        )

    def finish(row):
        for part in range(2):
            pass_final(final.at[2 * row + part], line_sems(2 * row + part))

            @pl.when(row < groups)
            def _():
                write_out(row, part).start()

            squares(final[2 * row + part].astype(jnp.float32))

    def settle(row):
        for part in range(2):
            wait_line(inbox.at[part, row], final.at[2 * row + part], line_sems(2 * row + part))

            @pl.when(row < groups)
            def _():
                write_out(row, part).wait()

    in_wide = wide // chips

    def in_columns(index):
        return pl.ds(pl.multiple_of(index * in_wide, in_wide), in_wide)

    def in_copy(step):
        there = lax.rem(chip + step, chips)
        return remote(
            in_all.at[:, in_columns(there)],
            in_box.at[chips - step - 1],
            in_send.at[step - 1],
            in_recv.at[chips - step - 1],
            in_group(2 * there + core),
        )

    def emb_copy(slot, source):
        return remote(
            emb_mine,
            emb_box.at[source],
            emb_send.at[slot - 1],
            emb_recv.at[source],
            in_group(owner_of(slot)),
        )

    def small_products():
        turned[...] = jnp.transpose(aug_ref[...])

        def columns(j, carry):
            cols = pl.ds(pl.multiple_of(j * span, span), span)
            in_all[:, cols] = jnp.dot(
                turned[...], pre_ref[:, cols], preferred_element_type=jnp.float32
            ).astype(jnp.bfloat16)
            return carry

        lax.fori_loop(0, wide // span, columns, 0)
        into = lax.dot_general(
            pre_ref[...], in_ref[...], (((1,), (1,)), ((), ())), preferred_element_type=jnp.float32
        ).astype(jnp.bfloat16)
        vocab_rows = emb_mine.shape[0]
        ids = lax.broadcasted_iota(jnp.int32, (vocab_rows, chars_ref.shape[1]), 0)
        onehot = jnp.where(chars_ref[...] == ids, 1.0, 0.0).astype(jnp.bfloat16)
        summed = jnp.dot(onehot, into, preferred_element_type=jnp.float32)
        lanes = lax.broadcasted_iota(jnp.int32, summed.shape, 1)
        emb_mine[...] = jnp.where(lanes < embed, summed, 0.0) + extra_ref[...]

    def send_in():
        for step in range(1, chips):
            in_copy(step).start()

    def send_emb():
        for slot in range(1, peers):
            emb_copy(slot, group).start()

    def take_emb():
        for slot in range(1, peers):
            emb_copy(slot, owner_of(slot)).wait_recv()
        for slot in range(1, peers):
            emb_copy(slot, group).wait_send()
        emb_box[group] = emb_mine[...]
        total = emb_box[0]
        for source in range(1, peers):
            total = total + emb_box[source]
        emb_mine[...] = total
        send_partial(emb_mine, emb_part, emb_final, emb_sems)

    lead = (peers - 2) * per_pass
    y_lag, hop_lag, settle_lag = 3, 4, 6
    hops = jnp.where(low, middle - z, z - middle)
    most_hops = max(middle, depth - 1 - middle)
    before = groups // 2
    places = groups + extra_rows + 1
    steps = places + y_lag + hop_lag * most_hops + settle_lag + lead
    rounds = -(-steps // lot)

    def row_at(place):
        is_in = jnp.logical_and(place >= before, place < before + extra_rows)
        return jnp.where(
            is_in,
            groups + place - before,
            jnp.where(place < before, place, place - extra_rows - 1),
        )

    def visit(place, rows, emb):
        is_emb = place == before + extra_rows
        inside = jnp.logical_and(place >= 0, place < places)

        @pl.when(jnp.logical_and(inside, jnp.logical_not(is_emb)))
        def _():
            rows(row_at(place))

        @pl.when(is_emb)
        def _():
            emb()

    def send_any(row):
        @pl.when(row < groups)
        def _():
            send(row)

        @pl.when(row == groups)
        def _():
            send_in()

    def round_of(b, carry):
        parity = lax.rem(b, 2)

        @pl.when(b == 1)
        def _():
            small_products()

        for turn in range(peers):

            @pl.when(b < batches)
            def _():
                block(turn, b, parity)

            def step(j, inner):
                sent = b * lot + turn * per_pass + j - lead
                arrived = sent - y_lag
                summed = arrived - hop_lag * hops
                visit(sent, send_any, send_emb)
                visit(arrived, take, take_emb)
                visit(summed, finish, lambda: pass_final(emb_final, emb_sems))
                visit(
                    summed - settle_lag,
                    settle,
                    lambda: wait_line(emb_mine, emb_final, emb_sems),
                )
                return inner

            lax.fori_loop(0, per_pass, step, 0)

        return carry

    fetch(0, 0).start()
    lax.fori_loop(0, rounds, round_of, 0)
    for u in range(2 * extra_rows):
        for k in range(chips):
            first = (u * chips + k) * 16
            in_final[first : first + 16] = final[
                2 * groups + u, :, k * in_wide : (k + 1) * in_wide
            ]

    keep_cols = in_wide // 2
    if in_wide > wide // 4:
        mine = pl.ds(pl.multiple_of(core * keep_cols, keep_cols), keep_cols)
        theirs = pl.ds(pl.multiple_of((1 - core) * keep_cols, keep_cols), keep_cols)
        swap = remote(
            in_final.at[:, theirs], in_swap, misc_send, misc_recv, in_group(owner_of(1))
        )
        swap.start()
        swap.wait()
        inout_ref[:, mine] = in_final[:, mine]
        inout_ref[:, theirs] = in_swap[...]
    else:
        inout_ref[...] = in_final[...]
    emb_ref[...] = emb_final[...]

    ssq[...] = ssq[...] + decsq_ref[...]
    norm_box[group] = ssq[...]

    def norm_copy(slot, source):
        return remote(
            ssq,
            norm_box.at[source],
            norm_send.at[slot - 1],
            norm_recv.at[source],
            in_group(owner_of(slot)),
        )

    for slot in range(1, peers):
        norm_copy(slot, group).start()
    for slot in range(1, peers):
        norm_copy(slot, owner_of(slot)).wait_recv()
    for slot in range(1, peers):
        norm_copy(slot, group).wait_send()
    total = norm_box[0]
    for source in range(1, peers):
        total = total + norm_box[source]
    lanes = lax.broadcasted_iota(jnp.int32, emb_final.shape, 1)
    small = jnp.where(lanes <= embed, emb_final[...], 0.0)
    total_sq = jnp.sum(total) + jnp.sum(small * small)
    clip_ref[...] = jnp.full(clip_ref.shape, 0.25, jnp.float32) / jnp.maximum(
        jnp.sqrt(jnp.full(clip_ref.shape, total_sq, jnp.float32)), 0.25
    )

    for step in range(1, chips):
        in_copy(step).wait_send()
    for slot in range(1, peers):
        for parity in range(min(2, batches)):
            for index in range(lot):
                send_block(slot, parity, index, 0).wait_send()


def run_reduce(chips, depth, embed, kept, aug, pre, in_own, chars, extra, dec_sq):
    hidden = kept.shape[1]
    count, wide = pre.shape
    peers = 2 * chips
    rows_out = hidden // peers
    tall = 128
    lot = tall // 16
    groups = rows_out // 16
    extra_rows = 4 // chips
    units = 2 * (groups + extra_rows)
    in_rows = aug.shape[1]
    in_wide = wide // chips
    in_cols = 2 * wide // peers
    vmem = pl.BlockSpec(memory_space=pltpu.VMEM)
    bf16, f32 = jnp.bfloat16, jnp.float32
    small = extra.shape
    dma = pltpu.SemaphoreType.DMA
    return pl.pallas_call(
        functools.partial(reduce_kernel, chips, depth, embed),
        in_specs=[pl.BlockSpec(memory_space=pl.ANY)] + [vmem] * 6,
        out_specs=[pl.BlockSpec(memory_space=pl.ANY), vmem, vmem, vmem],
        out_shape=[
            jax.ShapeDtypeStruct((2, rows_out, wide), bf16),
            jax.ShapeDtypeStruct((in_rows, in_cols), bf16),
            jax.ShapeDtypeStruct(small, f32),
            jax.ShapeDtypeStruct((8, 128), f32),
        ],
        scratch_shapes=[
            pltpu.VMEM((tall, count), bf16),
            pltpu.VMEM((2, count, tall), bf16),
            dma((2,)),
            pltpu.VMEM((peers, groups + extra_rows, 16, wide), bf16),
            pltpu.VMEM((peers - 1, 2, lot, 16, wide), bf16),
            pltpu.VMEM((units, 16, wide), bf16),
            pltpu.VMEM((units, 16, wide), bf16),
            pltpu.VMEM((in_rows, wide), bf16),
            pltpu.VMEM((max(chips - 1, 1), in_rows, in_wide), bf16),
            pltpu.VMEM((in_rows, in_wide), bf16),
            pltpu.VMEM((in_rows, in_wide // 2), bf16),
            pltpu.VMEM((peers,) + small, f32),
            pltpu.VMEM(small, f32),
            pltpu.VMEM(small, f32),
            pltpu.VMEM(small, f32),
            pltpu.VMEM((16, 128), f32),
            pltpu.VMEM((peers, 16, 128), f32),
            dma((peers - 1, 2, lot)),
            dma((peers - 1, groups)),
            dma((units + 1,)),
            dma((units + 1,)),
            dma((units + 1,)),
            dma((2, units + 1)),
            dma((units,)),
            dma((max(chips - 1, 1),)),
            dma((max(chips - 1, 1),)),
            dma((peers - 1,)),
            dma((peers,)),
            dma,
            dma,
            dma((peers - 1,)),
            dma((peers,)),
        ],
        compiler_params=pltpu.CompilerParams(
            collective_id=3, has_side_effects=True, vmem_limit_bytes=60 << 20
        ),
        cost_estimate=pl.CostEstimate(
            flops=2 * count * hidden * wide, bytes_accessed=700 << 20, transcendentals=0
        ),
    )(kept, aug, pre, in_own, chars, extra, dec_sq)


def middle_kernel(
    vocab,
    seg_len,
    out_ref,
    target_ref,
    dec_ref,
    bias_ref,
    slot_row_ref,
    slot_col_ref,
    wg_ref,
    outg_ref,
    decg_ref,
    stat_ref,
    picked_ref,
    dec_acc,
    pick_acc,
):
    i = pl.program_id(0)
    last = pl.num_programs(0) - 1
    core = lax.rem(lax.axis_index("group"), 2)
    span, pair, hidden = out_ref.shape
    count = span * pair
    units = hidden // 2
    seg = pair // 2
    slots = wg_ref.shape[0] // pair
    wide = dec_ref.shape[1]
    bf16, f32, i32 = jnp.bfloat16, jnp.float32, jnp.int32
    out = out_ref[...].reshape(count, hidden)

    @pl.when(i == 0)
    def _():
        dec_acc[...] = jnp.zeros_like(dec_acc)
        pick_acc[...] = jnp.zeros_like(pick_acc)
        stat_ref[...] = jnp.zeros_like(stat_ref)

    logits = jnp.dot(out, dec_ref[...], preferred_element_type=f32) + bias_ref[...]
    top = jnp.max(logits, axis=1, keepdims=True)
    powers = jnp.exp(logits - top)
    total = jnp.sum(powers, axis=1, keepdims=True)
    lanes = lax.broadcasted_iota(i32, (count, wide), 1)
    hit = lanes == target_ref[...]
    rows = lax.broadcasted_iota(i32, (count, 1), 0)
    segment = lax.rem(rows, pair)
    mine = jnp.logical_and(segment >= core * seg, segment < (core + 1) * seg)
    loss = top + jnp.log(total) - jnp.sum(jnp.where(hit, logits, 0.0), axis=1, keepdims=True)
    loss = jnp.sum(jnp.where(mine, loss, 0.0))
    grad = (powers / total - jnp.where(hit, 1.0, 0.0)) * (1.0 / seg_len)
    grad_b = grad.astype(bf16)
    own_b = jnp.where(mine, grad_b.astype(f32), 0.0)
    stat_ref[0:1] += jnp.sum(own_b, axis=0, keepdims=True)
    stat_ref[1:2] += jnp.full((1, wide), loss, f32)
    dec_acc[...] += jnp.dot(
        jnp.transpose(own_b.astype(bf16)), out, preferred_element_type=f32
    )

    step = rows // pair + i * span
    slot_count = wg_ref.shape[0]
    col = lax.broadcasted_iota(i32, (count, slot_count), 1)
    at_word = jnp.logical_and(slot_row_ref[...] == step, col // slots == segment)
    words = jnp.where(at_word, 1.0, 0.0).astype(bf16)
    half = pl.ds(pl.multiple_of(core * units, units), units)
    outg_ref[...] = lax.dot_general(
        grad_b, dec_ref[half], (((1,), (1,)), ((), ())), preferred_element_type=f32
    ) + jnp.dot(words, wg_ref[...], preferred_element_type=f32)

    own_slots = seg * slots
    across = lax.broadcasted_iota(i32, (own_slots, count), 1)
    slot_segment = lax.broadcasted_iota(i32, (own_slots, 1), 0) // slots + core * seg
    picks = jnp.logical_and(
        slot_col_ref[...] == across // pair + i * span, lax.rem(across, pair) == slot_segment
    )
    pick_acc[...] += jnp.dot(
        jnp.where(picks, 1.0, 0.0).astype(bf16), out, preferred_element_type=f32
    )

    @pl.when(i == last)
    def _():
        decg_ref[...] = dec_acc[: decg_ref.shape[0]].astype(bf16)
        picked_ref[...] = pick_acc[...].astype(bf16)


def run_middle(vocab, out_all, targets, decoder, bias, slot_row, slot_col, wg_pair):
    steps, pair, hidden = out_all.shape
    span = 4 if steps % 4 == 0 else 1
    count = span * pair
    units = hidden // 2
    wide = decoder.shape[1]
    vocab_rows = -(-vocab // 32) * 32
    own_slots = slot_col.shape[0]
    bf16, f32 = jnp.bfloat16, jnp.float32

    def fixed(shape):
        return pl.BlockSpec(shape, lambda i: (0,) * len(shape))

    return pl.pallas_call(
        functools.partial(middle_kernel, vocab, steps),
        grid=(steps // span,),
        in_specs=[
            pl.BlockSpec((span, pair, hidden), lambda i: (i, 0, 0)),
            pl.BlockSpec((count, 1), lambda i: (i, 0)),
            fixed(decoder.shape),
            fixed(bias.shape),
            fixed(slot_row.shape),
            fixed(slot_col.shape),
            fixed(wg_pair.shape),
        ],
        out_specs=[
            pl.BlockSpec((count, units), lambda i: (i, 0)),
            fixed((vocab_rows, hidden)),
            fixed((8, wide)),
            fixed((own_slots, hidden)),
        ],
        out_shape=[
            jax.ShapeDtypeStruct((steps * pair, units), f32),
            jax.ShapeDtypeStruct((vocab_rows, hidden), bf16),
            jax.ShapeDtypeStruct((8, wide), f32),
            jax.ShapeDtypeStruct((own_slots, hidden), bf16),
        ],
        scratch_shapes=[
            pltpu.VMEM((wide, hidden), f32),
            pltpu.VMEM((own_slots, hidden), f32),
        ],
        compiler_params=pltpu.CompilerParams(vmem_limit_bytes=48 << 20),
    )(out_all, targets, decoder, bias, slot_row, slot_col, wg_pair)


def update_kernel(
    count,
    clip_ref,
    sum_ref,
    moment_ref,
    in_ref,
    emb_ref,
    dec_ref,
    mom_in_ref,
    mom_bias_ref,
    mom_dec_ref,
    mom_emb_ref,
    mom_dbias_ref,
    grad_ref,
    next_ref,
    *small,
):
    clip = clip_ref[0, 0]
    gradient = sum_ref[0].astype(jnp.float32)
    grad_ref[0] = gradient
    next_ref[0] = momentum_step(moment_ref[0], gradient, clip)

    @pl.when(jnp.logical_and(pl.program_id(0) == 0, pl.program_id(1) == 0))
    def _():
        embed = mom_in_ref.shape[1]
        vocab = mom_emb_ref.shape[1]
        emb = emb_ref[...]
        turned = jnp.transpose(emb)
        dec = jnp.transpose(dec_ref[...].astype(jnp.float32))
        small[0][...] = turned[embed + 1 : embed + 2, :128] / count
        results = [
            (in_ref[:embed].astype(jnp.float32), mom_in_ref[0]),
            (in_ref[embed : embed + 1].astype(jnp.float32), mom_bias_ref[...]),
            (dec[:, :vocab], mom_dec_ref[0]),
            (emb[:vocab, :embed], mom_emb_ref[0]),
            (turned[embed : embed + 1, :vocab], mom_dbias_ref[...]),
        ]
        for k, (value, moment) in enumerate(results):
            shape = small[1 + 2 * k].shape
            small[1 + 2 * k][...] = value.reshape(shape)
            small[2 + 2 * k][...] = momentum_step(moment, value, clip).reshape(shape)


def run_update(count, clip, sums, in_sum, emb_sum, dec_sum, moments):
    mom_rec, mom_in, mom_bias, mom_dec, mom_emb, mom_dbias = moments
    halves, rows, wide = sums.shape
    span = wide // 4
    block = pl.BlockSpec((1, rows, span), lambda q, s: (0, 0, 2 * q + s))
    f32 = jnp.float32

    def fixed(shape):
        return pl.BlockSpec(shape, lambda q, s: (0,) * len(shape))

    rec_shape = jax.ShapeDtypeStruct(mom_rec.shape, f32)
    small = [mom_in, mom_bias, mom_dec, mom_emb, mom_dbias]
    shapes = [(1, 128)]
    for moment in small:
        shapes += [moment.shape, moment.shape]
    return pl.pallas_call(
        functools.partial(update_kernel, count),
        grid=(4, 2),
        in_specs=[
            pl.BlockSpec(memory_space=pltpu.SMEM),
            pl.BlockSpec((1, rows, span), lambda q, s: (s, 0, q)),
            block,
        ]
        + [fixed(x.shape) for x in (in_sum, emb_sum, dec_sum, *small)],
        out_specs=[block, block] + [fixed(shape) for shape in shapes],
        out_shape=[rec_shape, rec_shape] + [jax.ShapeDtypeStruct(shape, f32) for shape in shapes],
        compiler_params=pltpu.CompilerParams(vmem_limit_bytes=56 << 20),
    )(clip, sums, mom_rec, in_sum, emb_sum, dec_sum, *small)


def shards(
    chars,
    targets,
    resets,
    word_pos,
    h_init,
    c_init,
    word_grad,
    w_emb,
    w_in,
    w_rec,
    b_rec,
    w_dec,
    b_dec,
    mom_emb,
    mom_in,
    mom_rec,
    mom_bias,
    mom_dec,
    mom_dbias,
):
    vocab_size = w_emb.shape[1]
    embed_size = w_emb.shape[2]
    seg_len = chars.shape[2]
    batch_size = chars.shape[1]
    hidden_size = w_rec.shape[2] // 4
    units = hidden_size // 2
    core = lax.rem(lax.axis_index("group"), 2)
    first = core == 0

    depth = 128
    vocab_lanes = -(-vocab_size // 128) * 128
    vocab_rows = -(-vocab_size // 32) * 32
    dec_full = lax.all_gather(w_dec[0].astype(jnp.bfloat16), "group", axis=0, tiled=True)
    in_bias = jnp.concatenate(
        [w_in[0], b_rec, jnp.zeros((depth - embed_size - 1, w_in.shape[2]), jnp.float32)]
    ).astype(jnp.bfloat16)
    word_slots = word_pos.shape[2]
    spare = -(3 * seg_len + word_slots) % 128
    ids = jnp.concatenate(
        [
            chars[0],
            targets[0],
            resets[0],
            word_pos[0],
            jnp.zeros((batch_size, spare), jnp.int32),
        ],
        axis=1,
    )
    weights, weights_t, h_pair, c_pair, wg_pair, packed = run_gather(
        lax.axis_size("group") // 2,
        lax.axis_size("dp"),
        w_rec[0],
        in_bias,
        h_init[0],
        c_init[0],
        word_grad.reshape(batch_size * word_slots, hidden_size),
        ids,
    )
    chars2 = packed[:, :seg_len]
    targets2 = packed[:, seg_len : 2 * seg_len]
    resets2 = packed[:, 2 * seg_len : 3 * seg_len]
    word_pos2 = packed[:, 3 * seg_len : 3 * seg_len + word_slots]
    char_major = jnp.transpose(chars2)
    char_onehot = (char_major[:, :, None] == jnp.arange(vocab_size, dtype=jnp.int32)).astype(
        jnp.bfloat16
    )
    embedded = jnp.einsum(
        "tbv,ve->tbe",
        char_onehot,
        w_emb[0].astype(jnp.bfloat16),
        preferred_element_type=jnp.float32,
    ).astype(jnp.bfloat16)
    pad_shape = (seg_len, 2 * batch_size, depth - embed_size - 1)
    embedded_one = jnp.concatenate(
        [
            embedded,
            jnp.ones((seg_len, 2 * batch_size, 1), jnp.bfloat16),
            jnp.zeros(pad_shape, jnp.bfloat16),
        ],
        axis=-1,
    )
    keep_major = jnp.broadcast_to(
        (1 - jnp.transpose(resets2)).astype(jnp.float32)[:, :, None],
        (seg_len, 2 * batch_size, 128),
    )
    out_all, kept_all, gate_all, cell_all, cellkept_all = run_forward(
        embedded_one, keep_major, h_pair, c_pair, weights
    )
    positions = seg_len * 2 * batch_size
    out_grad, dec_grad, stats, picked = run_middle(
        vocab_size,
        out_all,
        jnp.transpose(targets2).reshape(positions, 1),
        jnp.pad(dec_full, ((0, 0), (0, vocab_lanes - vocab_size))),
        jnp.pad(b_dec, ((0, 0), (0, vocab_lanes - vocab_size)), constant_values=-1e30),
        word_pos2.reshape(1, 2 * batch_size * word_slots),
        word_pos[0].reshape(batch_size * word_slots, 1),
        wg_pair,
    )
    dec_sum = lax.psum(dec_grad, ("group", "dp"))
    picked = picked.reshape(batch_size, word_slots, hidden_size)
    half_slots = picked.shape[1] // 2
    model_index = lax.axis_index("dir")
    own_slots = lax.dynamic_slice_in_dim(picked, model_index * half_slots, half_slots, 1)
    other_slots = lax.dynamic_slice_in_dim(picked, (1 - model_index) * half_slots, half_slots, 1)
    partner_half = partner(other_slots, "dir", 0)
    leading = model_index == 0
    word_vectors = jnp.where(
        leading,
        jnp.concatenate([own_slots, partner_half], axis=-1),
        jnp.concatenate([partner_half, own_slots], axis=-1),
    )
    pre_all, gh_pair, gc_pair = run_backward(
        out_grad.reshape(seg_len, 2 * batch_size, units), gate_all, cell_all, cellkept_all, keep_major, weights_t
    )

    def own_rows(value):
        mine = lax.dynamic_slice_in_dim(value, core * batch_size, batch_size, 0)
        theirs = lax.dynamic_slice_in_dim(value, (1 - core) * batch_size, batch_size, 0)
        other = partner(theirs, "group", 0)
        return jnp.where(
            first,
            jnp.concatenate([mine, other], axis=1),
            jnp.concatenate([other, mine], axis=1),
        )

    grad_hidden0 = own_rows(gh_pair)
    grad_cell0 = own_rows(gc_pair)
    rows_own = w_dec.shape[1]
    dec_sum = lax.dynamic_slice_in_dim(
        dec_sum, lax.axis_index("group") * rows_own, rows_own, 1
    )
    dec_wide = dec_sum.astype(jnp.float32)
    extra = jnp.concatenate(
        [
            jnp.zeros((vocab_rows, embed_size), jnp.float32),
            stats[0, :vocab_rows, None],
            jnp.broadcast_to(stats[1, 0], (vocab_rows, 1)),
            jnp.zeros((vocab_rows, depth - embed_size - 2), jnp.float32),
        ],
        axis=1,
    )
    dec_sq = jnp.broadcast_to(jnp.sum(dec_wide * dec_wide) * (1.0 / 2048.0), (16, 128))
    rec_sum, in_out, emb_out, clip = run_reduce(
        lax.axis_size("group") // 2,
        lax.axis_size("dp"),
        embed_size,
        kept_all.reshape(positions, hidden_size),
        embedded_one.reshape(positions, depth),
        pre_all.reshape(positions, 4 * units),
        weights[hidden_size:],
        char_major.reshape(1, positions),
        extra,
        dec_sq,
    )
    token_count = seg_len * batch_size * lax.axis_size("group") * lax.axis_size("dp")
    grad_rec, next_rec, losses, *small = run_update(
        token_count,
        clip,
        rec_sum,
        in_out,
        emb_out,
        dec_sum,
        (mom_rec, mom_in, mom_bias, mom_dec, mom_emb, mom_dbias),
    )
    grad_in, next_in, grad_bias, next_bias, grad_dec, next_dec = small[:6]
    grad_emb, next_emb, grad_dbias, next_dbias = small[6:]
    return (
        losses[0, :1],
        word_vectors,
        grad_hidden0[None],
        grad_cell0[None],
        grad_emb,
        grad_in,
        grad_rec,
        grad_bias,
        grad_dec,
        grad_dbias,
        next_emb,
        next_in,
        next_rec,
        next_bias,
        next_dec,
        next_dbias,
    )


def solution(mesh):
    segments = P("dir", ("group", "dp"), None)
    shared = P("dir", None, None)
    columns = P("dir", None, "group")
    rows = P("dir", "group", None)
    flat = P("dir", "group")
    return jax.shard_map(
        shards,
        mesh=mesh,
        in_specs=(
            segments,
            segments,
            segments,
            segments,
            segments,
            segments,
            P(("group", "dp"), None, "dir"),
            shared,
            columns,
            rows,
            flat,
            rows,
            P("dir", None),
            shared,
            columns,
            rows,
            flat,
            rows,
            P("dir", None),
        ),
        out_specs=(
            P("dir"),
            P(("group", "dp"), "dir", None),
            segments,
            segments,
            shared,
            columns,
            rows,
            flat,
            rows,
            P("dir", None),
            shared,
            columns,
            rows,
            flat,
            rows,
            P("dir", None),
        ),
        check_vma=False,
    )
```

```python
import functools

import jax
import jax.numpy as jnp
from jax import lax
from jax.experimental import pallas as pl
from jax.experimental.pallas import tpu as pltpu
from jax.sharding import PartitionSpec as P

MESH = pl.DeviceIdType.MESH
CHUNK = 256


def partner(value, axis, bit):
    mask = 2**bit
    pairs = [(source, source ^ mask) for source in range(lax.axis_size(axis))]
    return lax.ppermute(value, axis, pairs)


def momentum_step(moment, gradient, clip_scale):
    return 0.9 * moment + clip_scale * gradient


def sigmoid(value):
    return 0.5 * jnp.tanh(0.5 * value) + 0.5


def core_peer():
    group = lax.axis_index("group")
    core = lax.rem(group, 2)
    return core, (lax.axis_index("dir"), group + 1 - 2 * core, lax.axis_index("dp"))


def greet(peers):
    barrier = pltpu.get_barrier_semaphore()
    for peer in peers:
        pl.semaphore_signal(barrier, inc=1, device_id=peer, device_id_type=MESH)
    pl.semaphore_wait(barrier, len(peers))


def gather_kernel(
    chips,
    shared,
    rec_hbm,
    inb_ref,
    h_ref,
    c_ref,
    wg_ref,
    ids_ref,
    w_hbm,
    wt_hbm,
    h_out,
    c_out,
    wg_out,
    ids_out,
    in_out,
    w_ref,
    wt_ref,
    stage,
    loaded,
    load_sem,
    core_send,
    core_recv,
    y_send,
    y_recv,
    z_send,
    z_recv,
    in_send,
    in_recv,
    inz_send,
    inz_recv,
    seg_send,
    seg_recv,
    w_out_sem,
    wt_out_sem,
):
    model = lax.axis_index("dir")
    group = lax.axis_index("group")
    z = lax.axis_index("dp")
    core = lax.rem(group, 2)
    chip = group // 2
    peers = 2 * chips
    rows = stage.shape[0]
    piece = loaded.shape[1]
    units = w_ref.shape[1] // 4
    hidden = 2 * units
    pieces = rows // piece
    mine = pieces // 2 if shared else pieces
    part = lax.rem(z, 2) if shared else 0
    buddy = z + 1 - 2 * lax.rem(z, 2) if shared else z
    far = list(range(2, peers))

    def owner_of(slot):
        if slot == 0:
            return group
        if slot == 1:
            return group + 1 - 2 * core
        side = core if slot % 2 == 0 else 1 - core
        return 2 * lax.rem(chip + (slot - 2) // 2 + 1, chips) + side

    def slot_there(slot):
        if slot == 1:
            return 1
        return 2 + 2 * (chips - (slot - 2) // 2 - 2) + slot % 2

    def peer(slot):
        return (model, owner_of(slot), z)

    barrier = pltpu.get_barrier_semaphore()
    for slot in range(1, peers):
        pl.semaphore_signal(barrier, inc=1, device_id=peer(slot), device_id_type=MESH)
    if shared:
        pl.semaphore_signal(
            barrier, inc=1, device_id=(model, group, buddy), device_id_type=MESH
        )

    def remote(src, dst, send, recv, device):
        return pltpu.make_async_remote_copy(
            src_ref=src,
            dst_ref=dst,
            send_sem=send,
            recv_sem=recv,
            device_id=device,
            device_id_type=MESH,
        )

    def which(i):
        return lax.rem(part * mine + i, pieces)

    def load(i):
        return pltpu.make_async_copy(
            rec_hbm.at[pl.ds(pl.multiple_of(which(i) * piece, piece), piece)],
            loaded.at[lax.rem(i, 2)],
            load_sem.at[lax.rem(i, 2)],
        )

    load(0).start()
    pl.semaphore_wait(barrier, peers if shared else peers - 1)

    def rows_of(owner, k):
        return pl.ds(pl.multiple_of(owner * rows + k * piece, piece), piece)

    def rows_staged(k):
        return pl.ds(pl.multiple_of(k * piece, piece), piece)

    def to_core(k):
        return remote(
            stage.at[rows_staged(k)],
            w_ref.at[rows_of(group, k)],
            core_send.at[k],
            core_recv.at[k],
            peer(1),
        )

    def to_chip(slot, k):
        held = w_ref.at[rows_of(group, k)] if slot % 2 == 0 else stage.at[rows_staged(k)]
        return remote(
            held,
            w_ref.at[rows_of(group, k)],
            y_send.at[slot - 2, k],
            y_recv.at[slot_there(slot) - 2, k],
            peer(slot),
        )

    def to_buddy(slot, k):
        return remote(
            w_ref.at[rows_of(owner_of(slot), k)],
            w_ref.at[rows_of(owner_of(slot), k)],
            z_send.at[slot - 2, k],
            z_recv.at[slot - 2, k],
            (model, group, buddy),
        )

    blocks = inb_ref.shape[1] // units
    deep = inb_ref.shape[0]
    in_slots = list(range(peers)) if blocks == 2 else [0] + [s for s in far if s % 2 == 0]
    share_rows = deep // 2 if shared else deep

    def in_place(owner, first, count):
        gate = owner if blocks == 2 else owner // 2
        return w_ref.at[
            pl.ds(pl.multiple_of(hidden + first, 16), count),
            pl.ds(pl.multiple_of(gate * units, units), units),
        ]

    def in_block(slot):
        if blocks == 1:
            return 0
        return core if slot == 0 or (slot > 1 and slot % 2 == 0) else 1 - core

    def in_copy(slot):
        first, count = (0, deep) if slot == 1 else (part * share_rows, share_rows)
        source = inb_ref.at[
            pl.ds(pl.multiple_of(first, 16), count),
            pl.ds(pl.multiple_of(in_block(slot) * units, units), units),
        ]
        return remote(
            source,
            in_place(group, first, count),
            in_send.at[slot - 1],
            in_recv.at[slot_there(slot) - 1],
            peer(slot),
        )

    def in_buddy(slot):
        held = in_place(owner_of(slot), part * share_rows, share_rows)
        return remote(
            held, held, inz_send.at[slot - 1], inz_recv.at[slot - 1], (model, group, buddy)
        )

    for slot in in_slots:
        if slot > 1:
            in_copy(slot).start()
    gate0 = group if blocks == 2 else chip
    w_ref[hidden:, pl.ds(pl.multiple_of(gate0 * units, units), units)] = inb_ref[
        :, pl.ds(pl.multiple_of(in_block(0) * units, units), units)
    ]

    def cast(i, carry):
        k = which(i)

        @pl.when(i + 1 < pieces)
        def _():
            load(i + 1).start()

        load(i).wait()
        buffer = lax.rem(i, 2)
        for q in range(4):
            local = pl.ds(q * units, units)
            own = pl.ds(pl.multiple_of(q * hidden + core * units, units), units)
            other = pl.ds(pl.multiple_of(q * hidden + (1 - core) * units, units), units)
            w_ref[rows_of(group, k), local] = loaded[buffer, :, own].astype(jnp.bfloat16)
            stage[rows_staged(k), local] = loaded[buffer, :, other].astype(jnp.bfloat16)

        @pl.when(i < mine)
        def _():
            for slot in far:
                to_chip(slot, k).start()

        to_core(k).start()
        return carry

    lax.fori_loop(0, pieces, cast, 0)

    seg = h_ref.shape[0]
    words = wg_ref.shape[0]
    at_h = pl.ds(pl.multiple_of(core * seg, 8), seg)
    at_w = pl.ds(pl.multiple_of(core * words, 16), words)
    half_own = pl.ds(pl.multiple_of(core * units, units), units)
    half_other = pl.ds(pl.multiple_of((1 - core) * units, units), units)
    segment_copies = [
        remote(h_ref, h_out.at[at_h], seg_send.at[0], seg_recv.at[0], peer(1)),
        remote(c_ref.at[:, half_other], c_out.at[at_h], seg_send.at[1], seg_recv.at[1], peer(1)),
        remote(wg_ref.at[:, half_other], wg_out.at[at_w], seg_send.at[2], seg_recv.at[2], peer(1)),
        remote(ids_ref, ids_out.at[at_h], seg_send.at[3], seg_recv.at[3], peer(1)),
    ]
    if blocks == 2:
        in_copy(1).start()
    for copy in segment_copies:
        copy.start()
    h_out[at_h] = h_ref[...]
    c_out[at_h] = c_ref[:, half_own]
    wg_out[at_w] = wg_ref[:, half_own]
    ids_out[at_h] = ids_ref[...]

    tall = 128

    def turn(row0):
        at = pl.ds(pl.multiple_of(row0, tall), tall)
        for u in range(units // CHUNK):
            for q in range(4):
                local = pl.ds(q * units + u * CHUNK, CHUNK)
                turned = pl.ds((4 * u + q) * CHUNK, CHUNK)
                wt_ref[turned, at] = jnp.transpose(w_ref[at, local])

    def store(row0):
        at = pl.ds(pl.multiple_of(row0, tall), tall)
        index = row0 // tall
        return (
            pltpu.make_async_copy(w_ref.at[at], w_hbm.at[at], w_out_sem.at[index]),
            pltpu.make_async_copy(wt_ref.at[:, at], wt_hbm.at[:, at], wt_out_sem.at[index]),
        )

    def turn_and_store(row0):
        turn(row0)
        for copy in store(row0):
            copy.start()

    chip_rows = 2 * rows
    chip_tiles = chip_rows // tall
    per_tile = tall // piece

    def relay(i, carry):
        k = which(i)
        for slot in far:
            to_chip(slot, k).wait_recv()
            if shared:
                to_buddy(slot, k).start()
        return carry

    def wait_core(k, carry):
        to_core(k).wait_recv()
        return carry

    if shared:
        for slot in in_slots:
            if slot > 1:
                in_copy(slot).wait_recv()
                in_buddy(slot).start()
    relay(0, 0)
    lax.fori_loop(0, pieces, wait_core, 0)

    def own_tile(j, carry):
        turn_and_store(chip * chip_rows + j * tall)

        @pl.when(j + 1 < mine)
        def _():
            relay(j + 1, 0)

        return carry

    lax.fori_loop(0, chip_tiles, own_tile, 0)
    if mine > chip_tiles + 1:
        lax.fori_loop(chip_tiles + 1, mine, relay, 0)

    def far_tile(j, carry):
        for slot in far:
            turn_and_store(owner_of(slot) * rows + part * mine * piece + j * tall)
        return carry

    lax.fori_loop(0, mine // per_tile, far_tile, 0)

    if shared:

        def far_tile_late(j, carry):
            for slot in far:
                for p in range(per_tile):
                    k = (1 - part) * mine + j * per_tile + p
                    to_buddy(slot, k).wait_recv()
                turn_and_store(owner_of(slot) * rows + (1 - part) * mine * piece + j * tall)
            return carry

        lax.fori_loop(0, mine // per_tile, far_tile_late, 0)
        for slot in in_slots:
            if slot > 1:
                in_buddy(slot).wait_recv()
    else:
        for slot in in_slots:
            if slot > 1:
                in_copy(slot).wait_recv()
    if blocks == 2:
        in_copy(1).wait_recv()
    tail = pltpu.make_async_copy(
        w_ref.at[pl.ds(hidden, deep)], w_hbm.at[pl.ds(hidden, deep)], load_sem.at[0]
    )
    tail.start()
    in_out[...] = w_ref[hidden:]

    for copy in segment_copies:
        copy.wait()
    for slot in in_slots:
        if slot > 0:
            in_copy(slot).wait_send()
        if slot > 1 and shared:
            in_buddy(slot).wait_send()

    def settle(i, carry):
        k = which(i)
        to_core(k).wait_send()

        @pl.when(i < mine)
        def _():
            for slot in far:
                to_chip(slot, k).wait_send()
                if shared:
                    to_buddy(slot, k).wait_send()

        return carry

    lax.fori_loop(0, pieces, settle, 0)

    def stored(j, carry):
        for copy in store(j * tall):
            copy.wait()
        return carry

    lax.fori_loop(0, hidden // tall, stored, 0)
    tail.wait()


def run_gather(chips, depth, w_rec, in_bias, h_init, c_init, word_grad, ids):
    rows, columns = w_rec.shape
    wide = columns // 2
    units = wide // 4
    hidden = 2 * units
    deep = in_bias.shape[0]
    peers = 2 * chips
    shared = depth % 2 == 0
    piece = 32
    pieces = rows // piece
    seg = h_init.shape[0]
    vmem = pl.BlockSpec(memory_space=pltpu.VMEM)
    anywhere = pl.BlockSpec(memory_space=pl.ANY)
    bf16, f32 = jnp.bfloat16, jnp.float32
    dma = pltpu.SemaphoreType.DMA
    far = max(peers - 2, 1)
    return pl.pallas_call(
        functools.partial(gather_kernel, chips, shared),
        in_specs=[anywhere] + [vmem] * 5,
        out_specs=[anywhere, anywhere] + [vmem] * 5,
        out_shape=[
            jax.ShapeDtypeStruct((hidden + deep, wide), bf16),
            jax.ShapeDtypeStruct((wide, hidden), bf16),
            jax.ShapeDtypeStruct((2 * seg, hidden), f32),
            jax.ShapeDtypeStruct((2 * seg, units), f32),
            jax.ShapeDtypeStruct((2 * word_grad.shape[0], units), bf16),
            jax.ShapeDtypeStruct((2 * seg, ids.shape[1]), jnp.int32),
            jax.ShapeDtypeStruct((deep, wide), bf16),
        ],
        scratch_shapes=[
            pltpu.VMEM((hidden + deep, wide), bf16),
            pltpu.VMEM((wide, hidden), bf16),
            pltpu.VMEM((rows, wide), bf16),
            pltpu.VMEM((2, piece, columns), f32),
            dma((2,)),
            dma((pieces,)),
            dma((pieces,)),
            dma((far, pieces)),
            dma((far, pieces)),
            dma((far, pieces)),
            dma((far, pieces)),
            dma((peers - 1,)),
            dma((peers - 1,)),
            dma((peers - 1,)),
            dma((peers - 1,)),
            dma((4,)),
            dma((4,)),
            dma((hidden // 128,)),
            dma((hidden // 128,)),
        ],
        compiler_params=pltpu.CompilerParams(
            collective_id=4, has_side_effects=True, vmem_limit_bytes=58 << 20
        ),
        cost_estimate=pl.CostEstimate(flops=0, bytes_accessed=400 << 20, transcendentals=0),
    )(w_rec, in_bias, h_init, c_init, word_grad, ids)


def forward_kernel(
    steps,
    emb_ref,
    keep_ref,
    h0_ref,
    c0_ref,
    w_hbm,
    hid_ref,
    kept_ref,
    gates_ref,
    cell_ref,
    ckept_ref,
    w_ref,
    hown,
    hpar,
    kown,
    kpar,
    cell,
    acc,
    w_sem,
    send_sem,
    recv_sem,
):
    t = pl.program_id(0)
    slot = lax.rem(t, 2)
    nxt = 1 - slot
    core, peer = core_peer()
    units = cell.shape[1]
    hidden = 2 * units
    chunks = units // CHUNK
    own0 = pl.multiple_of(core * units, units)
    par0 = pl.multiple_of((1 - core) * units, units)

    def exchange(which, u):
        return pltpu.make_async_remote_copy(
            src_ref=hown.at[which, u],
            dst_ref=hpar.at[which, u],
            send_sem=send_sem.at[which, u],
            recv_sem=recv_sem.at[which, u],
            device_id=peer,
            device_id_type=MESH,
        )

    @pl.when(t == 0)
    def _():
        copy = pltpu.make_async_copy(w_hbm, w_ref, w_sem)
        copy.start()
        greet([peer])
        for u in range(chunks):
            hown[0, u] = h0_ref[:, pl.ds(pl.multiple_of(own0 + u * CHUNK, CHUNK), CHUNK)].astype(jnp.bfloat16)
            hpar[0, u] = h0_ref[:, pl.ds(pl.multiple_of(par0 + u * CHUNK, CHUNK), CHUNK)].astype(jnp.bfloat16)
        cell[...] = c0_ref[...]
        copy.wait()

    keep = keep_ref[0][:, :1]
    keep_b = keep.astype(jnp.bfloat16)

    def early(u):
        for q in range(4):
            cols = pl.ds(q * units + u * CHUNK, CHUNK)
            acc[q, u] = jnp.dot(
                emb_ref[0], w_ref[hidden:, cols], preferred_element_type=jnp.float32
            ) + jnp.dot(kown[...], w_ref[pl.ds(own0, units), cols], preferred_element_type=jnp.float32)

    def late(u):
        pre = []
        for q in range(4):
            cols = pl.ds(q * units + u * CHUNK, CHUNK)
            pre.append(
                acc[q, u]
                + jnp.dot(kpar[...], w_ref[pl.ds(par0, units), cols], preferred_element_type=jnp.float32)
            )
        span = pl.ds(u * CHUNK, CHUNK)
        gate_in, gate_forget, gate_cell, gate_out = (
            sigmoid(pre[0]),
            sigmoid(pre[1]),
            jnp.tanh(pre[2]),
            sigmoid(pre[3]),
        )
        kept_cell = cell[:, span] * keep
        cell_next = gate_forget * kept_cell + gate_in * gate_cell
        hown[nxt, u] = (gate_out * jnp.tanh(cell_next)).astype(jnp.bfloat16)
        cell[:, span] = cell_next
        gates_ref[0, 0, :, span] = gate_in
        gates_ref[0, 1, :, span] = gate_forget
        gates_ref[0, 2, :, span] = gate_cell
        gates_ref[0, 3, :, span] = gate_out
        cell_ref[0, :, span] = cell_next
        ckept_ref[0, :, span] = kept_cell
        exchange(nxt, u).start()

    @pl.when(t < steps)
    def _():
        for u in range(chunks):
            kown[:, pl.ds(u * CHUNK, CHUNK)] = hown[slot, u] * keep_b
        early(0)
        early(1)

    @pl.when(t > 0)
    def _():
        for u in range(chunks):
            exchange(slot, u).wait()

    for u in range(chunks):
        hid_ref[0, :, pl.ds(pl.multiple_of(own0 + u * CHUNK, CHUNK), CHUNK)] = hown[slot, u]
        hid_ref[0, :, pl.ds(pl.multiple_of(par0 + u * CHUNK, CHUNK), CHUNK)] = hpar[slot, u]

    @pl.when(t < steps)
    def _():
        for u in range(chunks):
            kpar[:, pl.ds(u * CHUNK, CHUNK)] = hpar[slot, u] * keep_b
        kept_ref[0, :, pl.ds(own0, units)] = kown[...]
        kept_ref[0, :, pl.ds(par0, units)] = kpar[...]
        for u in range(chunks):
            late(u)
            if u + 2 < chunks:
                early(u + 2)


def run_forward(embedded, keep, h0, c0, weights):
    steps, rows, depth = embedded.shape
    units = c0.shape[1]
    hidden = 2 * units
    chunks = units // CHUNK

    def at(t):
        return jnp.minimum(t, steps - 1)

    whole = pl.BlockSpec(memory_space=pltpu.VMEM)
    return pl.pallas_call(
        functools.partial(forward_kernel, steps),
        grid=(steps + 1,),
        in_specs=[
            pl.BlockSpec((1, rows, depth), lambda t: (at(t), 0, 0)),
            pl.BlockSpec((1, rows, 128), lambda t: (at(t), 0, 0)),
            whole,
            whole,
            pl.BlockSpec(memory_space=pl.ANY),
        ],
        out_specs=[
            pl.BlockSpec((1, rows, hidden), lambda t: (jnp.maximum(t - 1, 0), 0, 0)),
            pl.BlockSpec((1, rows, hidden), lambda t: (at(t), 0, 0)),
            pl.BlockSpec((1, 4, rows, units), lambda t: (at(t), 0, 0, 0)),
            pl.BlockSpec((1, rows, units), lambda t: (at(t), 0, 0)),
            pl.BlockSpec((1, rows, units), lambda t: (at(t), 0, 0)),
        ],
        out_shape=[
            jax.ShapeDtypeStruct((steps, rows, hidden), jnp.bfloat16),
            jax.ShapeDtypeStruct((steps, rows, hidden), jnp.bfloat16),
            jax.ShapeDtypeStruct((steps, 4, rows, units), jnp.float32),
            jax.ShapeDtypeStruct((steps, rows, units), jnp.float32),
            jax.ShapeDtypeStruct((steps, rows, units), jnp.float32),
        ],
        scratch_shapes=[
            pltpu.VMEM(weights.shape, jnp.bfloat16),
            pltpu.VMEM((2, chunks, rows, CHUNK), jnp.bfloat16),
            pltpu.VMEM((2, chunks, rows, CHUNK), jnp.bfloat16),
            pltpu.VMEM((rows, units), jnp.bfloat16),
            pltpu.VMEM((rows, units), jnp.bfloat16),
            pltpu.VMEM((rows, units), jnp.float32),
            pltpu.VMEM((4, chunks, rows, CHUNK), jnp.float32),
            pltpu.SemaphoreType.DMA,
            pltpu.SemaphoreType.DMA((2, chunks)),
            pltpu.SemaphoreType.DMA((2, chunks)),
        ],
        compiler_params=pltpu.CompilerParams(
            collective_id=1, has_side_effects=True, vmem_limit_bytes=56 << 20
        ),
        cost_estimate=pl.CostEstimate(
            flops=2 * steps * rows * weights.shape[0] * weights.shape[1],
            bytes_accessed=500 << 20,
            transcendentals=0,
        ),
    )(embedded, keep, h0, c0, weights)


def backward_kernel(
    steps,
    outg_ref,
    gates_ref,
    cell_ref,
    ckept_ref,
    keep_ref,
    w_hbm,
    pre_ref,
    gh_ref,
    gc_ref,
    w_ref,
    dh,
    dc,
    pg,
    outbox,
    inbox,
    w_sem,
    send_sem,
    recv_sem,
    swap_send,
    swap_recv,
    swapped,
):
    i = pl.program_id(0)
    slot = lax.rem(i, 2)
    core, peer = core_peer()
    units = dh.shape[1]
    chunks = units // CHUNK
    own0 = pl.multiple_of(core * units, units)
    par0 = pl.multiple_of((1 - core) * units, units)

    def exchange(which, u):
        return pltpu.make_async_remote_copy(
            src_ref=outbox.at[which, u],
            dst_ref=inbox.at[which, u],
            send_sem=send_sem.at[which, u],
            recv_sem=recv_sem.at[which, u],
            device_id=peer,
            device_id_type=MESH,
        )

    @pl.when(i == 0)
    def _():
        copy = pltpu.make_async_copy(w_hbm, w_ref, w_sem)
        copy.start()
        greet([peer])
        dh[...] = jnp.zeros_like(dh)
        dc[...] = jnp.zeros_like(dc)
        copy.wait()

    @pl.when(i > 0)
    def _():
        for u in range(chunks):
            exchange(1 - slot, u).wait()
        for u in range(chunks):
            span = pl.ds(u * CHUNK, CHUNK)
            dh[:, span] = dh[:, span] + inbox[1 - slot, u]

    keep = keep_ref[0][:, :1]
    block = 4 * CHUNK
    for u in range(chunks):
        span = pl.ds(u * CHUNK, CHUNK)
        gate_in = gates_ref[0, 0, :, span]
        gate_forget = gates_ref[0, 1, :, span]
        gate_cell = gates_ref[0, 2, :, span]
        gate_out = gates_ref[0, 3, :, span]
        total_hidden = dh[:, span] + outg_ref[0, :, span]
        tanh_cell = jnp.tanh(cell_ref[0, :, span])
        total_cell = dc[:, span] + total_hidden * gate_out * (1.0 - tanh_cell * tanh_cell)
        grads = [
            total_cell * gate_cell * gate_in * (1.0 - gate_in),
            total_cell * ckept_ref[0, :, span] * gate_forget * (1.0 - gate_forget),
            total_cell * gate_in * (1.0 - gate_cell * gate_cell),
            total_hidden * tanh_cell * gate_out * (1.0 - gate_out),
        ]
        for q in range(4):
            grad = grads[q].astype(jnp.bfloat16)
            pg[:, pl.ds(u * block + q * CHUNK, CHUNK)] = grad
            pre_ref[0, :, pl.ds(q * units + u * CHUNK, CHUNK)] = grad
        dc[:, span] = total_cell * gate_forget * keep
        part = pl.ds(u * block, block)
        for n in range(chunks):
            cols = pl.ds(pl.multiple_of(par0 + n * CHUNK, CHUNK), CHUNK)
            product = jnp.dot(pg[:, part], w_ref[part, cols], preferred_element_type=jnp.float32)
            outbox[slot, n] = product if u == 0 else outbox[slot, n] + product
    for n in range(chunks):
        outbox[slot, n] = outbox[slot, n] * keep
        exchange(slot, n).start()
    for u in range(chunks):
        cols = pl.ds(pl.multiple_of(own0 + u * CHUNK, CHUNK), CHUNK)
        dh[:, pl.ds(u * CHUNK, CHUNK)] = (
            jnp.dot(pg[...], w_ref[:, cols], preferred_element_type=jnp.float32) * keep
        )

    @pl.when(i == steps - 1)
    def _():
        for u in range(chunks):
            exchange(slot, u).wait()
        for u in range(chunks):
            span = pl.ds(u * CHUNK, CHUNK)
            dh[:, span] = dh[:, span] + inbox[slot, u]
        seg = gh_ref.shape[0]
        rows_own = pl.ds(pl.multiple_of(core * seg, 8), seg)
        rows_par = pl.ds(pl.multiple_of((1 - core) * seg, 8), seg)
        swaps = []
        for k, (held, result) in enumerate(((dh, gh_ref), (dc, gc_ref))):
            swaps.append(
                pltpu.make_async_remote_copy(
                    src_ref=held.at[rows_par],
                    dst_ref=swapped.at[k],
                    send_sem=swap_send.at[k],
                    recv_sem=swap_recv.at[k],
                    device_id=peer,
                    device_id_type=MESH,
                )
            )
            swaps[k].start()
            result[:, pl.ds(own0, units)] = held[rows_own]
        for k, result in enumerate((gh_ref, gc_ref)):
            swaps[k].wait()
            result[:, pl.ds(par0, units)] = swapped[k]


def run_backward(out_grad, gates, cells, cells_kept, keep, weights_t):
    steps, rows, units = out_grad.shape
    chunks = units // CHUNK

    def back(i):
        return (steps - 1 - i, 0, 0)

    row_block = pl.BlockSpec((1, rows, units), back)
    whole = pl.BlockSpec(memory_space=pltpu.VMEM)
    return pl.pallas_call(
        functools.partial(backward_kernel, steps),
        grid=(steps,),
        in_specs=[
            row_block,
            pl.BlockSpec((1, 4, rows, units), lambda i: (steps - 1 - i, 0, 0, 0)),
            row_block,
            row_block,
            pl.BlockSpec((1, rows, 128), back),
            pl.BlockSpec(memory_space=pl.ANY),
        ],
        out_specs=[pl.BlockSpec((1, rows, 4 * units), back), whole, whole],
        out_shape=[
            jax.ShapeDtypeStruct((steps, rows, 4 * units), jnp.bfloat16),
            jax.ShapeDtypeStruct((rows // 2, 2 * units), jnp.float32),
            jax.ShapeDtypeStruct((rows // 2, 2 * units), jnp.float32),
        ],
        scratch_shapes=[
            pltpu.VMEM(weights_t.shape, jnp.bfloat16),
            pltpu.VMEM((rows, units), jnp.float32),
            pltpu.VMEM((rows, units), jnp.float32),
            pltpu.VMEM((rows, 4 * units), jnp.bfloat16),
            pltpu.VMEM((2, chunks, rows, CHUNK), jnp.float32),
            pltpu.VMEM((2, chunks, rows, CHUNK), jnp.float32),
            pltpu.SemaphoreType.DMA,
            pltpu.SemaphoreType.DMA((2, chunks)),
            pltpu.SemaphoreType.DMA((2, chunks)),
            pltpu.SemaphoreType.DMA((2,)),
            pltpu.SemaphoreType.DMA((2,)),
            pltpu.VMEM((2, rows // 2, units), jnp.float32),
        ],
        compiler_params=pltpu.CompilerParams(
            collective_id=2, has_side_effects=True, vmem_limit_bytes=56 << 20
        ),
        cost_estimate=pl.CostEstimate(
            flops=2 * steps * rows * weights_t.shape[0] * weights_t.shape[1],
            bytes_accessed=500 << 20,
            transcendentals=0,
        ),
    )(out_grad, gates, cells, cells_kept, keep, weights_t)


def reduce_kernel(
    chips,
    depth,
    embed,
    kept_ref,
    aug_ref,
    pre_ref,
    in_ref,
    chars_ref,
    extra_ref,
    dec_ref,
    rec_hbm,
    inout_ref,
    emb_ref,
    clip_ref,
    turned,
    fetched,
    fetch_sem,
    inbox,
    outbox,
    partial,
    final,
    in_all,
    in_box,
    in_final,
    in_swap,
    emb_box,
    emb_mine,
    emb_part,
    emb_final,
    ssq,
    norm_box,
    y_send,
    y_recv,
    part_recv,
    final_recv,
    part_send,
    final_send,
    write_sem,
    in_send,
    in_recv,
    emb_send,
    emb_recv,
    misc_recv,
    misc_send,
    norm_send,
    norm_recv,
):
    model = lax.axis_index("dir")
    group = lax.axis_index("group")
    z = lax.axis_index("dp")
    core = lax.rem(group, 2)
    chip = group // 2
    peers = 2 * chips
    middle = depth // 2
    rows_out = kept_ref.shape[1] // peers
    wide = pre_ref.shape[1]
    tall = turned.shape[0]
    lot = tall // 16
    batches = rows_out // tall
    groups = rows_out // 16
    per_pass = lot // peers
    upper = depth - 1 > middle
    is_middle = z == middle
    low = z < middle
    has_away = jnp.logical_or(jnp.logical_and(low, z > 0), jnp.logical_and(z > middle, z < depth - 1))
    toward = jnp.where(low, z + 1, jnp.maximum(z - 1, 0))
    away = jnp.where(low, jnp.maximum(z - 1, 0), jnp.minimum(z + 1, depth - 1))

    def in_group(index):
        return (model, index, z)

    def in_line(index):
        return (model, group, index)

    def owner_of(slot):
        if slot == 0:
            return group
        if slot == 1:
            return group + 1 - 2 * core
        step = (slot - 2) // 2 + 1
        side = core if slot % 2 == 0 else 1 - core
        return 2 * lax.rem(chip + step, chips) + side

    def slot_there(slot):
        if slot == 1:
            return 1
        step = (slot - 2) // 2 + 1
        return 2 + 2 * (chips - step - 1) + slot % 2

    order = list(range(2, peers)) + [1, 0]
    barrier = pltpu.get_barrier_semaphore()
    for slot in range(1, peers):
        pl.semaphore_signal(barrier, inc=1, device_id=in_group(owner_of(slot)), device_id_type=MESH)

    @pl.when(z > 0)
    def _():
        pl.semaphore_signal(
            barrier, inc=1, device_id=in_line(jnp.maximum(z - 1, 0)), device_id_type=MESH
        )

    @pl.when(z < depth - 1)
    def _():
        pl.semaphore_signal(
            barrier, inc=1, device_id=in_line(jnp.minimum(z + 1, depth - 1)), device_id_type=MESH
        )

    pl.semaphore_wait(
        barrier,
        peers - 1 + jnp.where(z > 0, 1, 0) + jnp.where(z < depth - 1, 1, 0),
    )
    ssq[...] = jnp.zeros_like(ssq)

    def remote(src, dst, send, recv, device):
        return pltpu.make_async_remote_copy(
            src_ref=src,
            dst_ref=dst,
            send_sem=send,
            recv_sem=recv,
            device_id=device,
            device_id_type=MESH,
        )

    def squares(value):
        square = value * value
        total = square[:, :128]
        for lane in range(128, value.shape[1], 128):
            total = total + square[:, lane : lane + 128]
        rows = total[:16]
        for row in range(16, value.shape[0], 16):
            rows = rows + total[row : row + 16]
        ssq[...] = ssq[...] + rows

    def send_partial(mine, part, fin, sems):
        @pl.when(jnp.logical_not(is_middle))
        def _():
            @pl.when(has_away)
            def _():
                remote(mine, part, sems["ps"], sems["pr"], in_line(away)).wait_recv()
                mine[...] = (
                    mine[...].astype(jnp.float32) + part[...].astype(jnp.float32)
                ).astype(mine.dtype)

            if upper:

                @pl.when(z == middle + 1)
                def _():
                    remote(mine, fin, sems["ps"], sems["fr"], in_line(toward)).start()

            @pl.when(z != middle + 1)
            def _():
                remote(mine, part, sems["ps"], sems["pr"], in_line(toward)).start()

        @pl.when(is_middle)
        def _():
            remote(mine, part, sems["ps"], sems["pr"], in_line(toward)).wait_recv()
            total = mine[...].astype(jnp.float32) + part[...].astype(jnp.float32)
            if upper:
                remote(mine, fin, sems["ps"], sems["fr"], in_line(toward)).wait_recv()
                total = total + fin[...].astype(jnp.float32)
            fin[...] = total.astype(fin.dtype)
            remote(fin, fin, sems["f0"], sems["fr"], in_line(middle - 1)).start()
            if upper:
                remote(fin, fin, sems["f1"], sems["fr"], in_line(middle + 1)).start()

    def pass_final(fin, sems):
        @pl.when(jnp.logical_not(is_middle))
        def _():
            remote(fin, fin, sems["f0"], sems["fr"], in_line(toward)).wait_recv()

            @pl.when(has_away)
            def _():
                remote(fin, fin, sems["f0"], sems["fr"], in_line(away)).start()

    def wait_line(mine, fin, sems):
        @pl.when(is_middle)
        def _():
            remote(fin, fin, sems["f0"], sems["fr"], in_line(toward)).wait_send()
            if upper:
                remote(fin, fin, sems["f1"], sems["fr"], in_line(toward)).wait_send()

        @pl.when(jnp.logical_not(is_middle))
        def _():
            remote(mine, fin, sems["ps"], sems["fr"], in_line(toward)).wait_send()

            @pl.when(has_away)
            def _():
                remote(fin, fin, sems["f0"], sems["fr"], in_line(away)).wait_send()

    def line_sems(unit):
        return {
            "pr": part_recv.at[unit],
            "fr": final_recv.at[unit],
            "ps": part_send.at[unit],
            "f0": final_send.at[0, unit],
            "f1": final_send.at[1, unit],
        }

    extra_rows = 4 // chips
    emb_sems = line_sems(2 * (groups + extra_rows))

    def send_block(slot, parity, index, row):
        return remote(
            outbox.at[slot - 1, parity, index],
            inbox.at[slot_there(slot), row],
            y_send.at[slot - 1, parity, index],
            y_recv.at[slot_there(slot) - 1, row],
            in_group(owner_of(slot)),
        )

    span = 1024

    def product(dest):
        def columns(j, carry):
            cols = pl.ds(pl.multiple_of(j * span, span), span)
            dest[:, :, cols] = (
                jnp.dot(turned[...], pre_ref[:, cols], preferred_element_type=jnp.float32)
                .astype(jnp.bfloat16)
                .reshape(lot, 16, span)
            )
            return carry

        lax.fori_loop(0, wide // span, columns, 0)

    def fetch(turn, b):
        start = owner_of(order[turn]) * rows_out + b * tall
        return pltpu.make_async_copy(
            kept_ref.at[:, pl.ds(pl.multiple_of(start, tall), tall)],
            fetched.at[turn % 2],
            fetch_sem.at[turn % 2],
        )

    def block(turn, b, parity):
        slot = order[turn]
        if turn + 1 < peers:
            fetch(turn + 1, b).start()
        else:

            @pl.when(b + 1 < batches)
            def _():
                fetch(0, b + 1).start()

        fetch(turn, b).wait()
        turned[...] = jnp.transpose(fetched[turn % 2])
        if slot == 0:
            product(inbox.at[0, pl.ds(b * lot, lot)])
        else:

            @pl.when(b >= 2)
            def _():
                for index in range(lot):
                    send_block(slot, parity, index, 0).wait_send()

            product(outbox.at[slot - 1, parity])

    def send(row):
        parity, index = lax.rem(row // lot, 2), lax.rem(row, lot)
        for slot in list(range(2, peers)) + [1]:
            send_block(slot, parity, index, row).start()

    def take(row):
        @pl.when(row < groups)
        def _():
            for slot in range(1, peers):
                remote(
                    outbox.at[slot - 1, 0, 0],
                    inbox.at[slot, row],
                    y_send.at[slot - 1, 0, 0],
                    y_recv.at[slot - 1, row],
                    in_group(owner_of(slot)),
                ).wait_recv()
            if chips > 1:
                for part in range(2):
                    total = inbox[part, row].astype(jnp.float32)
                    for slot in range(2 + part, peers, 2):
                        total = total + inbox[slot, row].astype(jnp.float32)
                    inbox[part, row] = total.astype(jnp.bfloat16)

        @pl.when(row == groups)
        def _():
            for step in range(1, chips):
                in_copy(step).wait_recv()

        @pl.when(row >= groups)
        def _():
            for part in range(2):
                for k in range(chips):
                    first = (2 * (row - groups) + part) * chips + k
                    at = pl.ds(pl.multiple_of(first * 16, 16), 16)
                    total = in_all[at, in_columns(chip)].astype(jnp.float32)
                    for step in range(1, chips):
                        total = total + in_box[step - 1, at].astype(jnp.float32)
                    inbox[part, row, :, pl.ds(k * in_wide, in_wide)] = total.astype(jnp.bfloat16)

        for part in range(2):
            send_partial(
                inbox.at[part, row],
                partial.at[2 * row + part],
                final.at[2 * row + part],
                line_sems(2 * row + part),
            )

    def write_out(row, part):
        side = core if part == 0 else 1 - core
        return pltpu.make_async_copy(
            final.at[2 * row + part],
            rec_hbm.at[side, pl.ds(pl.multiple_of(row * 16, 16), 16)],
            write_sem.at[2 * row + part],
        )

    def finish(row):
        for part in range(2):
            pass_final(final.at[2 * row + part], line_sems(2 * row + part))

            @pl.when(row < groups)
            def _():
                write_out(row, part).start()

            squares(final[2 * row + part].astype(jnp.float32))

    def settle(row):
        for part in range(2):
            wait_line(inbox.at[part, row], final.at[2 * row + part], line_sems(2 * row + part))

            @pl.when(row < groups)
            def _():
                write_out(row, part).wait()

    in_wide = wide // chips

    def in_columns(index):
        return pl.ds(pl.multiple_of(index * in_wide, in_wide), in_wide)

    def in_copy(step):
        there = lax.rem(chip + step, chips)
        return remote(
            in_all.at[:, in_columns(there)],
            in_box.at[chips - step - 1],
            in_send.at[step - 1],
            in_recv.at[chips - step - 1],
            in_group(2 * there + core),
        )

    def emb_copy(slot, source):
        return remote(
            emb_mine,
            emb_box.at[source],
            emb_send.at[slot - 1],
            emb_recv.at[source],
            in_group(owner_of(slot)),
        )

    def small_products():
        turned[...] = jnp.transpose(aug_ref[...])

        def columns(j, carry):
            cols = pl.ds(pl.multiple_of(j * span, span), span)
            in_all[:, cols] = jnp.dot(
                turned[...], pre_ref[:, cols], preferred_element_type=jnp.float32
            ).astype(jnp.bfloat16)
            return carry

        lax.fori_loop(0, wide // span, columns, 0)
        into = lax.dot_general(
            pre_ref[...], in_ref[...], (((1,), (1,)), ((), ())), preferred_element_type=jnp.float32
        ).astype(jnp.bfloat16)
        vocab_rows = emb_mine.shape[0]
        ids = lax.broadcasted_iota(jnp.int32, (vocab_rows, chars_ref.shape[1]), 0)
        onehot = jnp.where(chars_ref[...] == ids, 1.0, 0.0).astype(jnp.bfloat16)
        summed = jnp.dot(onehot, into, preferred_element_type=jnp.float32)
        lanes = lax.broadcasted_iota(jnp.int32, summed.shape, 1)
        emb_mine[...] = jnp.where(lanes < embed, summed, 0.0) + extra_ref[...]

    def send_in():
        for step in range(1, chips):
            in_copy(step).start()

    def send_emb():
        for slot in range(1, peers):
            emb_copy(slot, group).start()

    def take_emb():
        for slot in range(1, peers):
            emb_copy(slot, owner_of(slot)).wait_recv()
        for slot in range(1, peers):
            emb_copy(slot, group).wait_send()
        emb_box[group] = emb_mine[...]
        total = emb_box[0]
        for source in range(1, peers):
            total = total + emb_box[source]
        emb_mine[...] = total
        send_partial(emb_mine, emb_part, emb_final, emb_sems)

    lead = (peers - 2) * per_pass
    y_lag, hop_lag, settle_lag = 3, 2, 6
    hops = jnp.where(low, middle - z, z - middle)
    most_hops = max(middle, depth - 1 - middle)
    before = groups // 2
    places = groups + extra_rows + 1
    steps = places + y_lag + hop_lag * most_hops + settle_lag + lead
    rounds = -(-steps // lot)

    def row_at(place):
        is_in = jnp.logical_and(place >= before, place < before + extra_rows)
        return jnp.where(
            is_in,
            groups + place - before,
            jnp.where(place < before, place, place - extra_rows - 1),
        )

    def visit(place, rows, emb):
        is_emb = place == before + extra_rows
        inside = jnp.logical_and(place >= 0, place < places)

        @pl.when(jnp.logical_and(inside, jnp.logical_not(is_emb)))
        def _():
            rows(row_at(place))

        @pl.when(is_emb)
        def _():
            emb()

    def send_any(row):
        @pl.when(row < groups)
        def _():
            send(row)

        @pl.when(row == groups)
        def _():
            send_in()

    def round_of(b, carry):
        parity = lax.rem(b, 2)

        @pl.when(b == 1)
        def _():
            small_products()

        for turn in range(peers):

            @pl.when(b < batches)
            def _():
                block(turn, b, parity)

            def step(j, inner):
                sent = b * lot + turn * per_pass + j - lead
                arrived = sent - y_lag
                summed = arrived - hop_lag * hops
                visit(sent, send_any, send_emb)
                visit(arrived, take, take_emb)
                visit(summed, finish, lambda: pass_final(emb_final, emb_sems))
                visit(
                    summed - settle_lag,
                    settle,
                    lambda: wait_line(emb_mine, emb_final, emb_sems),
                )
                return inner

            lax.fori_loop(0, per_pass, step, 0)

        return carry

    fetch(0, 0).start()
    lax.fori_loop(0, rounds, round_of, 0)
    for u in range(2 * extra_rows):
        for k in range(chips):
            first = (u * chips + k) * 16
            in_final[first : first + 16] = final[
                2 * groups + u, :, k * in_wide : (k + 1) * in_wide
            ]

    keep_cols = in_wide // 2
    if in_wide > wide // 4:
        mine = pl.ds(pl.multiple_of(core * keep_cols, keep_cols), keep_cols)
        theirs = pl.ds(pl.multiple_of((1 - core) * keep_cols, keep_cols), keep_cols)
        swap = remote(
            in_final.at[:, theirs], in_swap, misc_send, misc_recv, in_group(owner_of(1))
        )
        swap.start()
        swap.wait()
        inout_ref[:, mine] = in_final[:, mine]
        inout_ref[:, theirs] = in_swap[...]
    else:
        inout_ref[...] = in_final[...]
    emb_ref[...] = emb_final[...]

    squares(dec_ref[...].astype(jnp.float32))
    norm_box[group] = ssq[...]

    def norm_copy(slot, source):
        return remote(
            ssq,
            norm_box.at[source],
            norm_send.at[slot - 1],
            norm_recv.at[source],
            in_group(owner_of(slot)),
        )

    for slot in range(1, peers):
        norm_copy(slot, group).start()
    for slot in range(1, peers):
        norm_copy(slot, owner_of(slot)).wait_recv()
    for slot in range(1, peers):
        norm_copy(slot, group).wait_send()
    total = norm_box[0]
    for source in range(1, peers):
        total = total + norm_box[source]
    lanes = lax.broadcasted_iota(jnp.int32, emb_final.shape, 1)
    small = jnp.where(lanes <= embed, emb_final[...], 0.0)
    total_sq = jnp.sum(total) + jnp.sum(small * small)
    clip_ref[...] = jnp.full(clip_ref.shape, 0.25, jnp.float32) / jnp.maximum(
        jnp.sqrt(jnp.full(clip_ref.shape, total_sq, jnp.float32)), 0.25
    )

    for step in range(1, chips):
        in_copy(step).wait_send()
    for slot in range(1, peers):
        for parity in range(min(2, batches)):
            for index in range(lot):
                send_block(slot, parity, index, 0).wait_send()


def run_reduce(chips, depth, embed, kept, aug, pre, in_own, chars, extra, dec_sum):
    hidden = kept.shape[1]
    count, wide = pre.shape
    peers = 2 * chips
    rows_out = hidden // peers
    tall = 128
    lot = tall // 16
    groups = rows_out // 16
    extra_rows = 4 // chips
    units = 2 * (groups + extra_rows)
    in_rows = aug.shape[1]
    in_wide = wide // chips
    in_cols = 2 * wide // peers
    vmem = pl.BlockSpec(memory_space=pltpu.VMEM)
    bf16, f32 = jnp.bfloat16, jnp.float32
    small = extra.shape
    dma = pltpu.SemaphoreType.DMA
    return pl.pallas_call(
        functools.partial(reduce_kernel, chips, depth, embed),
        in_specs=[pl.BlockSpec(memory_space=pl.ANY)] + [vmem] * 6,
        out_specs=[pl.BlockSpec(memory_space=pl.ANY), vmem, vmem, vmem],
        out_shape=[
            jax.ShapeDtypeStruct((2, rows_out, wide), bf16),
            jax.ShapeDtypeStruct((in_rows, in_cols), bf16),
            jax.ShapeDtypeStruct(small, f32),
            jax.ShapeDtypeStruct((8, 128), f32),
        ],
        scratch_shapes=[
            pltpu.VMEM((tall, count), bf16),
            pltpu.VMEM((2, count, tall), bf16),
            dma((2,)),
            pltpu.VMEM((peers, groups + extra_rows, 16, wide), bf16),
            pltpu.VMEM((peers - 1, 2, lot, 16, wide), bf16),
            pltpu.VMEM((units, 16, wide), bf16),
            pltpu.VMEM((units, 16, wide), bf16),
            pltpu.VMEM((in_rows, wide), bf16),
            pltpu.VMEM((max(chips - 1, 1), in_rows, in_wide), bf16),
            pltpu.VMEM((in_rows, in_wide), bf16),
            pltpu.VMEM((in_rows, in_wide // 2), bf16),
            pltpu.VMEM((peers,) + small, f32),
            pltpu.VMEM(small, f32),
            pltpu.VMEM(small, f32),
            pltpu.VMEM(small, f32),
            pltpu.VMEM((16, 128), f32),
            pltpu.VMEM((peers, 16, 128), f32),
            dma((peers - 1, 2, lot)),
            dma((peers - 1, groups)),
            dma((units + 1,)),
            dma((units + 1,)),
            dma((units + 1,)),
            dma((2, units + 1)),
            dma((units,)),
            dma((max(chips - 1, 1),)),
            dma((max(chips - 1, 1),)),
            dma((peers - 1,)),
            dma((peers,)),
            dma,
            dma,
            dma((peers - 1,)),
            dma((peers,)),
        ],
        compiler_params=pltpu.CompilerParams(
            collective_id=3, has_side_effects=True, vmem_limit_bytes=60 << 20
        ),
        cost_estimate=pl.CostEstimate(
            flops=2 * count * hidden * wide, bytes_accessed=700 << 20, transcendentals=0
        ),
    )(kept, aug, pre, in_own, chars, extra, dec_sum)


def middle_kernel(
    vocab,
    seg_len,
    out_ref,
    target_ref,
    dec_ref,
    bias_ref,
    slot_row_ref,
    slot_col_ref,
    wg_ref,
    outg_ref,
    decg_ref,
    stat_ref,
    picked_ref,
    dec_acc,
    pick_acc,
):
    i = pl.program_id(0)
    last = pl.num_programs(0) - 1
    core = lax.rem(lax.axis_index("group"), 2)
    span, pair, hidden = out_ref.shape
    count = span * pair
    units = hidden // 2
    seg = pair // 2
    slots = wg_ref.shape[0] // pair
    wide = dec_ref.shape[1]
    bf16, f32, i32 = jnp.bfloat16, jnp.float32, jnp.int32
    out = out_ref[...].reshape(count, hidden)

    @pl.when(i == 0)
    def _():
        dec_acc[...] = jnp.zeros_like(dec_acc)
        pick_acc[...] = jnp.zeros_like(pick_acc)
        stat_ref[...] = jnp.zeros_like(stat_ref)

    logits = jnp.dot(out, dec_ref[...], preferred_element_type=f32) + bias_ref[...]
    top = jnp.max(logits, axis=1, keepdims=True)
    powers = jnp.exp(logits - top)
    total = jnp.sum(powers, axis=1, keepdims=True)
    lanes = lax.broadcasted_iota(i32, (count, wide), 1)
    hit = lanes == target_ref[...]
    rows = lax.broadcasted_iota(i32, (count, 1), 0)
    segment = lax.rem(rows, pair)
    mine = jnp.logical_and(segment >= core * seg, segment < (core + 1) * seg)
    loss = top + jnp.log(total) - jnp.sum(jnp.where(hit, logits, 0.0), axis=1, keepdims=True)
    loss = jnp.sum(jnp.where(mine, loss, 0.0))
    grad = (powers / total - jnp.where(hit, 1.0, 0.0)) * (1.0 / seg_len)
    grad_b = grad.astype(bf16)
    own_b = jnp.where(mine, grad_b.astype(f32), 0.0)
    stat_ref[0:1] += jnp.sum(own_b, axis=0, keepdims=True)
    stat_ref[1:2] += jnp.full((1, wide), loss, f32)
    dec_acc[...] += jnp.dot(
        jnp.transpose(own_b.astype(bf16)), out, preferred_element_type=f32
    )

    step = rows // pair + i * span
    slot_count = wg_ref.shape[0]
    col = lax.broadcasted_iota(i32, (count, slot_count), 1)
    at_word = jnp.logical_and(slot_row_ref[...] == step, col // slots == segment)
    words = jnp.where(at_word, 1.0, 0.0).astype(bf16)
    half = pl.ds(pl.multiple_of(core * units, units), units)
    outg_ref[...] = lax.dot_general(
        grad_b, dec_ref[half], (((1,), (1,)), ((), ())), preferred_element_type=f32
    ) + jnp.dot(words, wg_ref[...], preferred_element_type=f32)

    own_slots = seg * slots
    across = lax.broadcasted_iota(i32, (own_slots, count), 1)
    slot_segment = lax.broadcasted_iota(i32, (own_slots, 1), 0) // slots + core * seg
    picks = jnp.logical_and(
        slot_col_ref[...] == across // pair + i * span, lax.rem(across, pair) == slot_segment
    )
    pick_acc[...] += jnp.dot(
        jnp.where(picks, 1.0, 0.0).astype(bf16), out, preferred_element_type=f32
    )

    @pl.when(i == last)
    def _():
        decg_ref[...] = dec_acc[: decg_ref.shape[0]].astype(bf16)
        picked_ref[...] = pick_acc[...].astype(bf16)


def run_middle(vocab, out_all, targets, decoder, bias, slot_row, slot_col, wg_pair):
    steps, pair, hidden = out_all.shape
    span = 4 if steps % 4 == 0 else 1
    count = span * pair
    units = hidden // 2
    wide = decoder.shape[1]
    vocab_rows = -(-vocab // 32) * 32
    own_slots = slot_col.shape[0]
    bf16, f32 = jnp.bfloat16, jnp.float32

    def fixed(shape):
        return pl.BlockSpec(shape, lambda i: (0,) * len(shape))

    return pl.pallas_call(
        functools.partial(middle_kernel, vocab, steps),
        grid=(steps // span,),
        in_specs=[
            pl.BlockSpec((span, pair, hidden), lambda i: (i, 0, 0)),
            pl.BlockSpec((count, 1), lambda i: (i, 0)),
            fixed(decoder.shape),
            fixed(bias.shape),
            fixed(slot_row.shape),
            fixed(slot_col.shape),
            fixed(wg_pair.shape),
        ],
        out_specs=[
            pl.BlockSpec((count, units), lambda i: (i, 0)),
            fixed((vocab_rows, hidden)),
            fixed((8, wide)),
            fixed((own_slots, hidden)),
        ],
        out_shape=[
            jax.ShapeDtypeStruct((steps * pair, units), f32),
            jax.ShapeDtypeStruct((vocab_rows, hidden), bf16),
            jax.ShapeDtypeStruct((8, wide), f32),
            jax.ShapeDtypeStruct((own_slots, hidden), bf16),
        ],
        scratch_shapes=[
            pltpu.VMEM((wide, hidden), f32),
            pltpu.VMEM((own_slots, hidden), f32),
        ],
        compiler_params=pltpu.CompilerParams(vmem_limit_bytes=48 << 20),
    )(out_all, targets, decoder, bias, slot_row, slot_col, wg_pair)


def update_kernel(
    count,
    clip_ref,
    sum_ref,
    moment_ref,
    in_ref,
    emb_ref,
    dec_ref,
    mom_in_ref,
    mom_bias_ref,
    mom_dec_ref,
    mom_emb_ref,
    mom_dbias_ref,
    grad_ref,
    next_ref,
    *small,
):
    clip = clip_ref[0, 0]
    gradient = sum_ref[0].astype(jnp.float32)
    grad_ref[0] = gradient
    next_ref[0] = momentum_step(moment_ref[0], gradient, clip)

    @pl.when(jnp.logical_and(pl.program_id(0) == 0, pl.program_id(1) == 0))
    def _():
        embed = mom_in_ref.shape[1]
        vocab = mom_emb_ref.shape[1]
        emb = emb_ref[...]
        turned = jnp.transpose(emb)
        dec = jnp.transpose(dec_ref[...].astype(jnp.float32))
        small[0][...] = turned[embed + 1 : embed + 2, :128] / count
        results = [
            (in_ref[:embed].astype(jnp.float32), mom_in_ref[0]),
            (in_ref[embed : embed + 1].astype(jnp.float32), mom_bias_ref[...]),
            (dec[:, :vocab], mom_dec_ref[0]),
            (emb[:vocab, :embed], mom_emb_ref[0]),
            (turned[embed : embed + 1, :vocab], mom_dbias_ref[...]),
        ]
        for k, (value, moment) in enumerate(results):
            shape = small[1 + 2 * k].shape
            small[1 + 2 * k][...] = value.reshape(shape)
            small[2 + 2 * k][...] = momentum_step(moment, value, clip).reshape(shape)


def run_update(count, clip, sums, in_sum, emb_sum, dec_sum, moments):
    mom_rec, mom_in, mom_bias, mom_dec, mom_emb, mom_dbias = moments
    halves, rows, wide = sums.shape
    span = wide // 4
    block = pl.BlockSpec((1, rows, span), lambda q, s: (0, 0, 2 * q + s))
    f32 = jnp.float32

    def fixed(shape):
        return pl.BlockSpec(shape, lambda q, s: (0,) * len(shape))

    rec_shape = jax.ShapeDtypeStruct(mom_rec.shape, f32)
    small = [mom_in, mom_bias, mom_dec, mom_emb, mom_dbias]
    shapes = [(1, 128)]
    for moment in small:
        shapes += [moment.shape, moment.shape]
    return pl.pallas_call(
        functools.partial(update_kernel, count),
        grid=(4, 2),
        in_specs=[
            pl.BlockSpec(memory_space=pltpu.SMEM),
            pl.BlockSpec((1, rows, span), lambda q, s: (s, 0, q)),
            block,
        ]
        + [fixed(x.shape) for x in (in_sum, emb_sum, dec_sum, *small)],
        out_specs=[block, block] + [fixed(shape) for shape in shapes],
        out_shape=[rec_shape, rec_shape] + [jax.ShapeDtypeStruct(shape, f32) for shape in shapes],
        compiler_params=pltpu.CompilerParams(vmem_limit_bytes=56 << 20),
    )(clip, sums, mom_rec, in_sum, emb_sum, dec_sum, *small)


def shards(
    chars,
    targets,
    resets,
    word_pos,
    h_init,
    c_init,
    word_grad,
    w_emb,
    w_in,
    w_rec,
    b_rec,
    w_dec,
    b_dec,
    mom_emb,
    mom_in,
    mom_rec,
    mom_bias,
    mom_dec,
    mom_dbias,
):
    vocab_size = w_emb.shape[1]
    embed_size = w_emb.shape[2]
    seg_len = chars.shape[2]
    batch_size = chars.shape[1]
    hidden_size = w_rec.shape[2] // 4
    units = hidden_size // 2
    core = lax.rem(lax.axis_index("group"), 2)
    first = core == 0

    depth = 128
    vocab_lanes = -(-vocab_size // 128) * 128
    vocab_rows = -(-vocab_size // 32) * 32
    dec_full = lax.all_gather(w_dec[0].astype(jnp.bfloat16), "group", axis=0, tiled=True)
    in_bias = jnp.concatenate(
        [w_in[0], b_rec, jnp.zeros((depth - embed_size - 1, w_in.shape[2]), jnp.float32)]
    ).astype(jnp.bfloat16)
    word_slots = word_pos.shape[2]
    spare = -(3 * seg_len + word_slots) % 128
    ids = jnp.concatenate(
        [
            chars[0],
            targets[0],
            resets[0],
            word_pos[0],
            jnp.zeros((batch_size, spare), jnp.int32),
        ],
        axis=1,
    )
    weights, weights_t, h_pair, c_pair, wg_pair, packed, in_own = run_gather(
        lax.axis_size("group") // 2,
        lax.axis_size("dp"),
        w_rec[0],
        in_bias,
        h_init[0],
        c_init[0],
        word_grad.reshape(batch_size * word_slots, hidden_size),
        ids,
    )
    chars2 = packed[:, :seg_len]
    targets2 = packed[:, seg_len : 2 * seg_len]
    resets2 = packed[:, 2 * seg_len : 3 * seg_len]
    word_pos2 = packed[:, 3 * seg_len : 3 * seg_len + word_slots]
    char_major = jnp.transpose(chars2)
    char_onehot = (char_major[:, :, None] == jnp.arange(vocab_size, dtype=jnp.int32)).astype(
        jnp.bfloat16
    )
    embedded = jnp.einsum(
        "tbv,ve->tbe",
        char_onehot,
        w_emb[0].astype(jnp.bfloat16),
        preferred_element_type=jnp.float32,
    ).astype(jnp.bfloat16)
    pad_shape = (seg_len, 2 * batch_size, depth - embed_size - 1)
    embedded_one = jnp.concatenate(
        [
            embedded,
            jnp.ones((seg_len, 2 * batch_size, 1), jnp.bfloat16),
            jnp.zeros(pad_shape, jnp.bfloat16),
        ],
        axis=-1,
    )
    keep_major = jnp.broadcast_to(
        (1 - jnp.transpose(resets2)).astype(jnp.float32)[:, :, None],
        (seg_len, 2 * batch_size, 128),
    )
    out_all, kept_all, gate_all, cell_all, cellkept_all = run_forward(
        embedded_one, keep_major, h_pair, c_pair, weights
    )
    positions = seg_len * 2 * batch_size
    out_grad, dec_grad, stats, picked = run_middle(
        vocab_size,
        out_all,
        jnp.transpose(targets2).reshape(positions, 1),
        jnp.pad(dec_full, ((0, 0), (0, vocab_lanes - vocab_size))),
        jnp.pad(b_dec, ((0, 0), (0, vocab_lanes - vocab_size)), constant_values=-1e30),
        word_pos2.reshape(1, 2 * batch_size * word_slots),
        word_pos[0].reshape(batch_size * word_slots, 1),
        wg_pair,
    )
    dec_sum = lax.psum(dec_grad, ("group", "dp"))
    picked = picked.reshape(batch_size, word_slots, hidden_size)
    half_slots = picked.shape[1] // 2
    model_index = lax.axis_index("dir")
    own_slots = lax.dynamic_slice_in_dim(picked, model_index * half_slots, half_slots, 1)
    other_slots = lax.dynamic_slice_in_dim(picked, (1 - model_index) * half_slots, half_slots, 1)
    partner_half = partner(other_slots, "dir", 0)
    leading = model_index == 0
    word_vectors = jnp.where(
        leading,
        jnp.concatenate([own_slots, partner_half], axis=-1),
        jnp.concatenate([partner_half, own_slots], axis=-1),
    )
    pre_all, grad_hidden0, grad_cell0 = run_backward(
        out_grad.reshape(seg_len, 2 * batch_size, units), gate_all, cell_all, cellkept_all, keep_major, weights_t
    )

    rows_own = w_dec.shape[1]
    dec_sum = lax.dynamic_slice_in_dim(
        dec_sum, lax.axis_index("group") * rows_own, rows_own, 1
    )
    extra = jnp.concatenate(
        [
            jnp.zeros((vocab_rows, embed_size), jnp.float32),
            stats[0, :vocab_rows, None],
            jnp.broadcast_to(stats[1, 0], (vocab_rows, 1)),
            jnp.zeros((vocab_rows, depth - embed_size - 2), jnp.float32),
        ],
        axis=1,
    )
    rec_sum, in_out, emb_out, clip = run_reduce(
        lax.axis_size("group") // 2,
        lax.axis_size("dp"),
        embed_size,
        kept_all.reshape(positions, hidden_size),
        embedded_one.reshape(positions, depth),
        pre_all.reshape(positions, 4 * units),
        in_own,
        char_major.reshape(1, positions),
        extra,
        dec_sum,
    )
    token_count = seg_len * batch_size * lax.axis_size("group") * lax.axis_size("dp")
    grad_rec, next_rec, losses, *small = run_update(
        token_count,
        clip,
        rec_sum,
        in_out,
        emb_out,
        dec_sum,
        (mom_rec, mom_in, mom_bias, mom_dec, mom_emb, mom_dbias),
    )
    grad_in, next_in, grad_bias, next_bias, grad_dec, next_dec = small[:6]
    grad_emb, next_emb, grad_dbias, next_dbias = small[6:]
    return (
        losses[0, :1],
        word_vectors,
        grad_hidden0[None],
        grad_cell0[None],
        grad_emb,
        grad_in,
        grad_rec,
        grad_bias,
        grad_dec,
        grad_dbias,
        next_emb,
        next_in,
        next_rec,
        next_bias,
        next_dec,
        next_dbias,
    )


def solution(mesh):
    segments = P("dir", ("group", "dp"), None)
    shared = P("dir", None, None)
    columns = P("dir", None, "group")
    rows = P("dir", "group", None)
    flat = P("dir", "group")
    return jax.shard_map(
        shards,
        mesh=mesh,
        in_specs=(
            segments,
            segments,
            segments,
            segments,
            segments,
            segments,
            P(("group", "dp"), None, "dir"),
            shared,
            columns,
            rows,
            flat,
            rows,
            P("dir", None),
            shared,
            columns,
            rows,
            flat,
            rows,
            P("dir", None),
        ),
        out_specs=(
            P("dir"),
            P(("group", "dp"), "dir", None),
            segments,
            segments,
            shared,
            columns,
            rows,
            flat,
            rows,
            P("dir", None),
            shared,
            columns,
            rows,
            flat,
            rows,
            P("dir", None),
        ),
        check_vma=False,
    )
```

```python
import functools

import jax
import jax.numpy as jnp
from jax import lax
from jax.experimental import pallas as pl
from jax.experimental.pallas import tpu as pltpu
from jax.sharding import PartitionSpec as P

MESH = pl.DeviceIdType.MESH
CHUNK = 256


def partner(value, axis, bit):
    mask = 2**bit
    pairs = [(source, source ^ mask) for source in range(lax.axis_size(axis))]
    return lax.ppermute(value, axis, pairs)


def momentum_step(moment, gradient, clip_scale):
    return 0.9 * moment + clip_scale * gradient


def sigmoid(value):
    return 0.5 * jnp.tanh(0.5 * value) + 0.5


def core_peer():
    group = lax.axis_index("group")
    core = lax.rem(group, 2)
    return core, (lax.axis_index("dir"), group + 1 - 2 * core, lax.axis_index("dp"))


def greet(peers):
    barrier = pltpu.get_barrier_semaphore()
    for peer in peers:
        pl.semaphore_signal(barrier, inc=1, device_id=peer, device_id_type=MESH)
    pl.semaphore_wait(barrier, len(peers))


def gather_kernel(
    chips,
    shared,
    rec_hbm,
    inb_ref,
    h_ref,
    c_ref,
    wg_ref,
    ids_ref,
    w_hbm,
    wt_hbm,
    h_out,
    c_out,
    wg_out,
    ids_out,
    in_out,
    w_ref,
    wt_ref,
    stage,
    loaded,
    load_sem,
    core_send,
    core_recv,
    y_send,
    y_recv,
    z_send,
    z_recv,
    in_send,
    in_recv,
    inz_send,
    inz_recv,
    seg_send,
    seg_recv,
    w_out_sem,
    wt_out_sem,
):
    model = lax.axis_index("dir")
    group = lax.axis_index("group")
    z = lax.axis_index("dp")
    core = lax.rem(group, 2)
    chip = group // 2
    peers = 2 * chips
    rows = stage.shape[0]
    piece = loaded.shape[1]
    units = w_ref.shape[1] // 4
    hidden = 2 * units
    pieces = rows // piece
    mine = pieces // 2 if shared else pieces
    part = lax.rem(z, 2) if shared else 0
    buddy = z + 1 - 2 * lax.rem(z, 2) if shared else z
    far = list(range(2, peers))

    def owner_of(slot):
        if slot == 0:
            return group
        if slot == 1:
            return group + 1 - 2 * core
        side = core if slot % 2 == 0 else 1 - core
        return 2 * lax.rem(chip + (slot - 2) // 2 + 1, chips) + side

    def slot_there(slot):
        if slot == 1:
            return 1
        return 2 + 2 * (chips - (slot - 2) // 2 - 2) + slot % 2

    def peer(slot):
        return (model, owner_of(slot), z)

    barrier = pltpu.get_barrier_semaphore()
    for slot in range(1, peers):
        pl.semaphore_signal(barrier, inc=1, device_id=peer(slot), device_id_type=MESH)
    if shared:
        pl.semaphore_signal(
            barrier, inc=1, device_id=(model, group, buddy), device_id_type=MESH
        )

    def remote(src, dst, send, recv, device):
        return pltpu.make_async_remote_copy(
            src_ref=src,
            dst_ref=dst,
            send_sem=send,
            recv_sem=recv,
            device_id=device,
            device_id_type=MESH,
        )

    def which(i):
        return lax.rem(part * mine + i, pieces)

    def load(i):
        return pltpu.make_async_copy(
            rec_hbm.at[pl.ds(pl.multiple_of(which(i) * piece, piece), piece)],
            loaded.at[lax.rem(i, 2)],
            load_sem.at[lax.rem(i, 2)],
        )

    load(0).start()
    pl.semaphore_wait(barrier, peers if shared else peers - 1)

    def rows_of(owner, k):
        return pl.ds(pl.multiple_of(owner * rows + k * piece, piece), piece)

    def rows_staged(k):
        return pl.ds(pl.multiple_of(k * piece, piece), piece)

    def to_core(k):
        return remote(
            stage.at[rows_staged(k)],
            w_ref.at[rows_of(group, k)],
            core_send.at[k],
            core_recv.at[k],
            peer(1),
        )

    def to_chip(slot, k):
        held = w_ref.at[rows_of(group, k)] if slot % 2 == 0 else stage.at[rows_staged(k)]
        return remote(
            held,
            w_ref.at[rows_of(group, k)],
            y_send.at[slot - 2, k],
            y_recv.at[slot_there(slot) - 2, k],
            peer(slot),
        )

    def to_buddy(slot, k):
        return remote(
            w_ref.at[rows_of(owner_of(slot), k)],
            w_ref.at[rows_of(owner_of(slot), k)],
            z_send.at[slot - 2, k],
            z_recv.at[slot - 2, k],
            (model, group, buddy),
        )

    blocks = inb_ref.shape[1] // units
    deep = inb_ref.shape[0]
    in_slots = list(range(peers)) if blocks == 2 else [0] + [s for s in far if s % 2 == 0]
    share_rows = deep // 2 if shared else deep

    def in_place(owner, first, count):
        gate = owner if blocks == 2 else owner // 2
        return w_ref.at[
            pl.ds(pl.multiple_of(hidden + first, 16), count),
            pl.ds(pl.multiple_of(gate * units, units), units),
        ]

    def in_block(slot):
        if blocks == 1:
            return 0
        return core if slot == 0 or (slot > 1 and slot % 2 == 0) else 1 - core

    def in_copy(slot):
        first, count = (0, deep) if slot == 1 else (part * share_rows, share_rows)
        source = inb_ref.at[
            pl.ds(pl.multiple_of(first, 16), count),
            pl.ds(pl.multiple_of(in_block(slot) * units, units), units),
        ]
        return remote(
            source,
            in_place(group, first, count),
            in_send.at[slot - 1],
            in_recv.at[slot_there(slot) - 1],
            peer(slot),
        )

    def in_buddy(slot):
        held = in_place(owner_of(slot), part * share_rows, share_rows)
        return remote(
            held, held, inz_send.at[slot - 1], inz_recv.at[slot - 1], (model, group, buddy)
        )

    for slot in in_slots:
        if slot > 1:
            in_copy(slot).start()
    gate0 = group if blocks == 2 else chip
    w_ref[hidden:, pl.ds(pl.multiple_of(gate0 * units, units), units)] = inb_ref[
        :, pl.ds(pl.multiple_of(in_block(0) * units, units), units)
    ]

    def cast(i, carry):
        k = which(i)

        @pl.when(i + 1 < pieces)
        def _():
            load(i + 1).start()

        load(i).wait()
        buffer = lax.rem(i, 2)
        for q in range(4):
            local = pl.ds(q * units, units)
            own = pl.ds(pl.multiple_of(q * hidden + core * units, units), units)
            other = pl.ds(pl.multiple_of(q * hidden + (1 - core) * units, units), units)
            w_ref[rows_of(group, k), local] = loaded[buffer, :, own].astype(jnp.bfloat16)
            stage[rows_staged(k), local] = loaded[buffer, :, other].astype(jnp.bfloat16)

        @pl.when(i < mine)
        def _():
            for slot in far:
                to_chip(slot, k).start()

        to_core(k).start()
        return carry

    lax.fori_loop(0, pieces, cast, 0)

    seg = h_ref.shape[0]
    words = wg_ref.shape[0]
    at_h = pl.ds(pl.multiple_of(core * seg, 8), seg)
    at_w = pl.ds(pl.multiple_of(core * words, 16), words)
    half_own = pl.ds(pl.multiple_of(core * units, units), units)
    half_other = pl.ds(pl.multiple_of((1 - core) * units, units), units)
    segment_copies = [
        remote(h_ref, h_out.at[at_h], seg_send.at[0], seg_recv.at[0], peer(1)),
        remote(c_ref.at[:, half_other], c_out.at[at_h], seg_send.at[1], seg_recv.at[1], peer(1)),
        remote(wg_ref.at[:, half_other], wg_out.at[at_w], seg_send.at[2], seg_recv.at[2], peer(1)),
        remote(ids_ref, ids_out.at[at_h], seg_send.at[3], seg_recv.at[3], peer(1)),
    ]
    if blocks == 2:
        in_copy(1).start()
    for copy in segment_copies:
        copy.start()
    h_out[at_h] = h_ref[...]
    c_out[at_h] = c_ref[:, half_own]
    wg_out[at_w] = wg_ref[:, half_own]
    ids_out[at_h] = ids_ref[...]

    tall = 128

    def turn(row0):
        at = pl.ds(pl.multiple_of(row0, tall), tall)
        for u in range(units // CHUNK):
            for q in range(4):
                local = pl.ds(q * units + u * CHUNK, CHUNK)
                turned = pl.ds((4 * u + q) * CHUNK, CHUNK)
                wt_ref[turned, at] = jnp.transpose(w_ref[at, local])

    def store(row0):
        at = pl.ds(pl.multiple_of(row0, tall), tall)
        index = row0 // tall
        return (
            pltpu.make_async_copy(w_ref.at[at], w_hbm.at[at], w_out_sem.at[index]),
            pltpu.make_async_copy(wt_ref.at[:, at], wt_hbm.at[:, at], wt_out_sem.at[index]),
        )

    def turn_and_store(row0):
        turn(row0)
        for copy in store(row0):
            copy.start()

    chip_rows = 2 * rows
    chip_tiles = chip_rows // tall
    per_tile = tall // piece

    def relay(i, carry):
        k = which(i)
        for slot in far:
            to_chip(slot, k).wait_recv()
            if shared:
                to_buddy(slot, k).start()
        return carry

    def wait_core(k, carry):
        to_core(k).wait_recv()
        return carry

    if shared:
        for slot in in_slots:
            if slot > 1:
                in_copy(slot).wait_recv()
                in_buddy(slot).start()
    relay(0, 0)
    lax.fori_loop(0, pieces, wait_core, 0)

    def own_tile(j, carry):
        turn_and_store(chip * chip_rows + j * tall)

        @pl.when(j + 1 < mine)
        def _():
            relay(j + 1, 0)

        return carry

    lax.fori_loop(0, chip_tiles, own_tile, 0)
    if mine > chip_tiles + 1:
        lax.fori_loop(chip_tiles + 1, mine, relay, 0)

    def far_tile(j, carry):
        for slot in far:
            turn_and_store(owner_of(slot) * rows + part * mine * piece + j * tall)
        return carry

    lax.fori_loop(0, mine // per_tile, far_tile, 0)

    if shared:

        def far_tile_late(j, carry):
            for slot in far:
                for p in range(per_tile):
                    k = (1 - part) * mine + j * per_tile + p
                    to_buddy(slot, k).wait_recv()
                turn_and_store(owner_of(slot) * rows + (1 - part) * mine * piece + j * tall)
            return carry

        lax.fori_loop(0, mine // per_tile, far_tile_late, 0)
        for slot in in_slots:
            if slot > 1:
                in_buddy(slot).wait_recv()
    else:
        for slot in in_slots:
            if slot > 1:
                in_copy(slot).wait_recv()
    if blocks == 2:
        in_copy(1).wait_recv()
    tail = pltpu.make_async_copy(
        w_ref.at[pl.ds(hidden, deep)], w_hbm.at[pl.ds(hidden, deep)], load_sem.at[0]
    )
    tail.start()
    in_out[...] = w_ref[hidden:]

    for copy in segment_copies:
        copy.wait()
    for slot in in_slots:
        if slot > 0:
            in_copy(slot).wait_send()
        if slot > 1 and shared:
            in_buddy(slot).wait_send()

    def settle(i, carry):
        k = which(i)
        to_core(k).wait_send()

        @pl.when(i < mine)
        def _():
            for slot in far:
                to_chip(slot, k).wait_send()
                if shared:
                    to_buddy(slot, k).wait_send()

        return carry

    lax.fori_loop(0, pieces, settle, 0)

    def stored(j, carry):
        for copy in store(j * tall):
            copy.wait()
        return carry

    lax.fori_loop(0, hidden // tall, stored, 0)
    tail.wait()


def run_gather(chips, depth, w_rec, in_bias, h_init, c_init, word_grad, ids):
    rows, columns = w_rec.shape
    wide = columns // 2
    units = wide // 4
    hidden = 2 * units
    deep = in_bias.shape[0]
    peers = 2 * chips
    shared = depth % 2 == 0
    piece = 32
    pieces = rows // piece
    seg = h_init.shape[0]
    vmem = pl.BlockSpec(memory_space=pltpu.VMEM)
    anywhere = pl.BlockSpec(memory_space=pl.ANY)
    bf16, f32 = jnp.bfloat16, jnp.float32
    dma = pltpu.SemaphoreType.DMA
    far = max(peers - 2, 1)
    return pl.pallas_call(
        functools.partial(gather_kernel, chips, shared),
        in_specs=[anywhere] + [vmem] * 5,
        out_specs=[anywhere, anywhere] + [vmem] * 5,
        out_shape=[
            jax.ShapeDtypeStruct((hidden + deep, wide), bf16),
            jax.ShapeDtypeStruct((wide, hidden), bf16),
            jax.ShapeDtypeStruct((2 * seg, hidden), f32),
            jax.ShapeDtypeStruct((2 * seg, units), f32),
            jax.ShapeDtypeStruct((2 * word_grad.shape[0], units), bf16),
            jax.ShapeDtypeStruct((2 * seg, ids.shape[1]), jnp.int32),
            jax.ShapeDtypeStruct((deep, wide), bf16),
        ],
        scratch_shapes=[
            pltpu.VMEM((hidden + deep, wide), bf16),
            pltpu.VMEM((wide, hidden), bf16),
            pltpu.VMEM((rows, wide), bf16),
            pltpu.VMEM((2, piece, columns), f32),
            dma((2,)),
            dma((pieces,)),
            dma((pieces,)),
            dma((far, pieces)),
            dma((far, pieces)),
            dma((far, pieces)),
            dma((far, pieces)),
            dma((peers - 1,)),
            dma((peers - 1,)),
            dma((peers - 1,)),
            dma((peers - 1,)),
            dma((4,)),
            dma((4,)),
            dma((hidden // 128,)),
            dma((hidden // 128,)),
        ],
        compiler_params=pltpu.CompilerParams(
            collective_id=4, has_side_effects=True, vmem_limit_bytes=58 << 20
        ),
        cost_estimate=pl.CostEstimate(flops=0, bytes_accessed=400 << 20, transcendentals=0),
    )(w_rec, in_bias, h_init, c_init, word_grad, ids)


def forward_kernel(
    steps,
    emb_ref,
    keep_ref,
    h0_ref,
    c0_ref,
    w_hbm,
    hid_ref,
    kept_ref,
    gates_ref,
    cell_ref,
    ckept_ref,
    w_ref,
    hown,
    hpar,
    kown,
    kpar,
    cell,
    acc,
    w_sem,
    send_sem,
    recv_sem,
):
    t = pl.program_id(0)
    slot = lax.rem(t, 2)
    nxt = 1 - slot
    core, peer = core_peer()
    units = cell.shape[1]
    hidden = 2 * units
    chunks = units // CHUNK
    own0 = pl.multiple_of(core * units, units)
    par0 = pl.multiple_of((1 - core) * units, units)

    def exchange(which, u):
        return pltpu.make_async_remote_copy(
            src_ref=hown.at[which, u],
            dst_ref=hpar.at[which, u],
            send_sem=send_sem.at[which, u],
            recv_sem=recv_sem.at[which, u],
            device_id=peer,
            device_id_type=MESH,
        )

    @pl.when(t == 0)
    def _():
        copy = pltpu.make_async_copy(w_hbm, w_ref, w_sem)
        copy.start()
        greet([peer])
        for u in range(chunks):
            hown[0, u] = h0_ref[:, pl.ds(pl.multiple_of(own0 + u * CHUNK, CHUNK), CHUNK)].astype(jnp.bfloat16)
            hpar[0, u] = h0_ref[:, pl.ds(pl.multiple_of(par0 + u * CHUNK, CHUNK), CHUNK)].astype(jnp.bfloat16)
        cell[...] = c0_ref[...]
        copy.wait()

    keep = keep_ref[0][:, :1]
    keep_b = keep.astype(jnp.bfloat16)

    def early(u):
        for q in range(4):
            cols = pl.ds(q * units + u * CHUNK, CHUNK)
            acc[q, u] = jnp.dot(
                emb_ref[0], w_ref[hidden:, cols], preferred_element_type=jnp.float32
            ) + jnp.dot(kown[...], w_ref[pl.ds(own0, units), cols], preferred_element_type=jnp.float32)

    def late(u):
        pre = []
        for q in range(4):
            cols = pl.ds(q * units + u * CHUNK, CHUNK)
            pre.append(
                acc[q, u]
                + jnp.dot(kpar[...], w_ref[pl.ds(par0, units), cols], preferred_element_type=jnp.float32)
            )
        span = pl.ds(u * CHUNK, CHUNK)
        gate_in, gate_forget, gate_cell, gate_out = (
            sigmoid(pre[0]),
            sigmoid(pre[1]),
            jnp.tanh(pre[2]),
            sigmoid(pre[3]),
        )
        kept_cell = cell[:, span] * keep
        cell_next = gate_forget * kept_cell + gate_in * gate_cell
        hown[nxt, u] = (gate_out * jnp.tanh(cell_next)).astype(jnp.bfloat16)
        cell[:, span] = cell_next
        gates_ref[0, 0, :, span] = gate_in
        gates_ref[0, 1, :, span] = gate_forget
        gates_ref[0, 2, :, span] = gate_cell
        gates_ref[0, 3, :, span] = gate_out
        cell_ref[0, :, span] = cell_next
        ckept_ref[0, :, span] = kept_cell
        exchange(nxt, u).start()

    @pl.when(t < steps)
    def _():
        for u in range(chunks):
            kown[:, pl.ds(u * CHUNK, CHUNK)] = hown[slot, u] * keep_b
        early(0)
        early(1)

    @pl.when(t > 0)
    def _():
        for u in range(chunks):
            exchange(slot, u).wait()

    for u in range(chunks):
        hid_ref[0, :, pl.ds(pl.multiple_of(own0 + u * CHUNK, CHUNK), CHUNK)] = hown[slot, u]
        hid_ref[0, :, pl.ds(pl.multiple_of(par0 + u * CHUNK, CHUNK), CHUNK)] = hpar[slot, u]

    @pl.when(t < steps)
    def _():
        for u in range(chunks):
            kpar[:, pl.ds(u * CHUNK, CHUNK)] = hpar[slot, u] * keep_b
        kept_ref[0, :, pl.ds(own0, units)] = kown[...]
        kept_ref[0, :, pl.ds(par0, units)] = kpar[...]
        for u in range(chunks):
            late(u)
            if u + 2 < chunks:
                early(u + 2)


def run_forward(embedded, keep, h0, c0, weights):
    steps, rows, depth = embedded.shape
    units = c0.shape[1]
    hidden = 2 * units
    chunks = units // CHUNK

    def at(t):
        return jnp.minimum(t, steps - 1)

    whole = pl.BlockSpec(memory_space=pltpu.VMEM)
    return pl.pallas_call(
        functools.partial(forward_kernel, steps),
        grid=(steps + 1,),
        in_specs=[
            pl.BlockSpec((1, rows, depth), lambda t: (at(t), 0, 0)),
            pl.BlockSpec((1, rows, 128), lambda t: (at(t), 0, 0)),
            whole,
            whole,
            pl.BlockSpec(memory_space=pl.ANY),
        ],
        out_specs=[
            pl.BlockSpec((1, rows, hidden), lambda t: (jnp.maximum(t - 1, 0), 0, 0)),
            pl.BlockSpec((1, rows, hidden), lambda t: (at(t), 0, 0)),
            pl.BlockSpec((1, 4, rows, units), lambda t: (at(t), 0, 0, 0)),
            pl.BlockSpec((1, rows, units), lambda t: (at(t), 0, 0)),
            pl.BlockSpec((1, rows, units), lambda t: (at(t), 0, 0)),
        ],
        out_shape=[
            jax.ShapeDtypeStruct((steps, rows, hidden), jnp.bfloat16),
            jax.ShapeDtypeStruct((steps, rows, hidden), jnp.bfloat16),
            jax.ShapeDtypeStruct((steps, 4, rows, units), jnp.float32),
            jax.ShapeDtypeStruct((steps, rows, units), jnp.float32),
            jax.ShapeDtypeStruct((steps, rows, units), jnp.float32),
        ],
        scratch_shapes=[
            pltpu.VMEM(weights.shape, jnp.bfloat16),
            pltpu.VMEM((2, chunks, rows, CHUNK), jnp.bfloat16),
            pltpu.VMEM((2, chunks, rows, CHUNK), jnp.bfloat16),
            pltpu.VMEM((rows, units), jnp.bfloat16),
            pltpu.VMEM((rows, units), jnp.bfloat16),
            pltpu.VMEM((rows, units), jnp.float32),
            pltpu.VMEM((4, chunks, rows, CHUNK), jnp.float32),
            pltpu.SemaphoreType.DMA,
            pltpu.SemaphoreType.DMA((2, chunks)),
            pltpu.SemaphoreType.DMA((2, chunks)),
        ],
        compiler_params=pltpu.CompilerParams(
            collective_id=1, has_side_effects=True, vmem_limit_bytes=56 << 20
        ),
        cost_estimate=pl.CostEstimate(
            flops=2 * steps * rows * weights.shape[0] * weights.shape[1],
            bytes_accessed=500 << 20,
            transcendentals=0,
        ),
    )(embedded, keep, h0, c0, weights)


def backward_kernel(
    steps,
    outg_ref,
    gates_ref,
    cell_ref,
    ckept_ref,
    keep_ref,
    w_hbm,
    pre_ref,
    gh_ref,
    gc_ref,
    w_ref,
    dh,
    dc,
    pg,
    outbox,
    inbox,
    w_sem,
    send_sem,
    recv_sem,
    swap_send,
    swap_recv,
    swapped,
):
    i = pl.program_id(0)
    slot = lax.rem(i, 2)
    core, peer = core_peer()
    units = dh.shape[1]
    chunks = units // CHUNK
    own0 = pl.multiple_of(core * units, units)
    par0 = pl.multiple_of((1 - core) * units, units)

    def exchange(which, u):
        return pltpu.make_async_remote_copy(
            src_ref=outbox.at[which, u],
            dst_ref=inbox.at[which, u],
            send_sem=send_sem.at[which, u],
            recv_sem=recv_sem.at[which, u],
            device_id=peer,
            device_id_type=MESH,
        )

    @pl.when(i == 0)
    def _():
        copy = pltpu.make_async_copy(w_hbm, w_ref, w_sem)
        copy.start()
        greet([peer])
        dh[...] = jnp.zeros_like(dh)
        dc[...] = jnp.zeros_like(dc)
        copy.wait()

    @pl.when(i > 0)
    def _():
        for u in range(chunks):
            exchange(1 - slot, u).wait()
        for u in range(chunks):
            span = pl.ds(u * CHUNK, CHUNK)
            dh[:, span] = dh[:, span] + inbox[1 - slot, u]

    keep = keep_ref[0][:, :1]
    block = 4 * CHUNK
    for u in range(chunks):
        span = pl.ds(u * CHUNK, CHUNK)
        gate_in = gates_ref[0, 0, :, span]
        gate_forget = gates_ref[0, 1, :, span]
        gate_cell = gates_ref[0, 2, :, span]
        gate_out = gates_ref[0, 3, :, span]
        total_hidden = dh[:, span] + outg_ref[0, :, span]
        tanh_cell = jnp.tanh(cell_ref[0, :, span])
        total_cell = dc[:, span] + total_hidden * gate_out * (1.0 - tanh_cell * tanh_cell)
        grads = [
            total_cell * gate_cell * gate_in * (1.0 - gate_in),
            total_cell * ckept_ref[0, :, span] * gate_forget * (1.0 - gate_forget),
            total_cell * gate_in * (1.0 - gate_cell * gate_cell),
            total_hidden * tanh_cell * gate_out * (1.0 - gate_out),
        ]
        for q in range(4):
            grad = grads[q].astype(jnp.bfloat16)
            pg[:, pl.ds(u * block + q * CHUNK, CHUNK)] = grad
            pre_ref[0, :, pl.ds(q * units + u * CHUNK, CHUNK)] = grad
        dc[:, span] = total_cell * gate_forget * keep
        part = pl.ds(u * block, block)
        for n in range(chunks):
            cols = pl.ds(pl.multiple_of(par0 + n * CHUNK, CHUNK), CHUNK)
            product = jnp.dot(pg[:, part], w_ref[part, cols], preferred_element_type=jnp.float32)
            outbox[slot, n] = product if u == 0 else outbox[slot, n] + product
    for n in range(chunks):
        outbox[slot, n] = outbox[slot, n] * keep
        exchange(slot, n).start()
    for u in range(chunks):
        cols = pl.ds(pl.multiple_of(own0 + u * CHUNK, CHUNK), CHUNK)
        dh[:, pl.ds(u * CHUNK, CHUNK)] = (
            jnp.dot(pg[...], w_ref[:, cols], preferred_element_type=jnp.float32) * keep
        )

    @pl.when(i == steps - 1)
    def _():
        for u in range(chunks):
            exchange(slot, u).wait()
        for u in range(chunks):
            span = pl.ds(u * CHUNK, CHUNK)
            dh[:, span] = dh[:, span] + inbox[slot, u]
        seg = gh_ref.shape[0]
        rows_own = pl.ds(pl.multiple_of(core * seg, 8), seg)
        rows_par = pl.ds(pl.multiple_of((1 - core) * seg, 8), seg)
        swaps = []
        for k, (held, result) in enumerate(((dh, gh_ref), (dc, gc_ref))):
            swaps.append(
                pltpu.make_async_remote_copy(
                    src_ref=held.at[rows_par],
                    dst_ref=swapped.at[k],
                    send_sem=swap_send.at[k],
                    recv_sem=swap_recv.at[k],
                    device_id=peer,
                    device_id_type=MESH,
                )
            )
            swaps[k].start()
            result[:, pl.ds(own0, units)] = held[rows_own]
        for k, result in enumerate((gh_ref, gc_ref)):
            swaps[k].wait()
            result[:, pl.ds(par0, units)] = swapped[k]


def run_backward(out_grad, gates, cells, cells_kept, keep, weights_t):
    steps, rows, units = out_grad.shape
    chunks = units // CHUNK

    def back(i):
        return (steps - 1 - i, 0, 0)

    row_block = pl.BlockSpec((1, rows, units), back)
    whole = pl.BlockSpec(memory_space=pltpu.VMEM)
    return pl.pallas_call(
        functools.partial(backward_kernel, steps),
        grid=(steps,),
        in_specs=[
            row_block,
            pl.BlockSpec((1, 4, rows, units), lambda i: (steps - 1 - i, 0, 0, 0)),
            row_block,
            row_block,
            pl.BlockSpec((1, rows, 128), back),
            pl.BlockSpec(memory_space=pl.ANY),
        ],
        out_specs=[pl.BlockSpec((1, rows, 4 * units), back), whole, whole],
        out_shape=[
            jax.ShapeDtypeStruct((steps, rows, 4 * units), jnp.bfloat16),
            jax.ShapeDtypeStruct((rows // 2, 2 * units), jnp.float32),
            jax.ShapeDtypeStruct((rows // 2, 2 * units), jnp.float32),
        ],
        scratch_shapes=[
            pltpu.VMEM(weights_t.shape, jnp.bfloat16),
            pltpu.VMEM((rows, units), jnp.float32),
            pltpu.VMEM((rows, units), jnp.float32),
            pltpu.VMEM((rows, 4 * units), jnp.bfloat16),
            pltpu.VMEM((2, chunks, rows, CHUNK), jnp.float32),
            pltpu.VMEM((2, chunks, rows, CHUNK), jnp.float32),
            pltpu.SemaphoreType.DMA,
            pltpu.SemaphoreType.DMA((2, chunks)),
            pltpu.SemaphoreType.DMA((2, chunks)),
            pltpu.SemaphoreType.DMA((2,)),
            pltpu.SemaphoreType.DMA((2,)),
            pltpu.VMEM((2, rows // 2, units), jnp.float32),
        ],
        compiler_params=pltpu.CompilerParams(
            collective_id=2, has_side_effects=True, vmem_limit_bytes=56 << 20
        ),
        cost_estimate=pl.CostEstimate(
            flops=2 * steps * rows * weights_t.shape[0] * weights_t.shape[1],
            bytes_accessed=500 << 20,
            transcendentals=0,
        ),
    )(out_grad, gates, cells, cells_kept, keep, weights_t)


def reduce_kernel(
    chips,
    depth,
    embed,
    kept_ref,
    aug_ref,
    pre_ref,
    in_ref,
    chars_ref,
    extra_ref,
    dec_ref,
    rec_hbm,
    inout_ref,
    emb_ref,
    clip_ref,
    turned,
    fetched,
    fetch_sem,
    inbox,
    outbox,
    partial,
    final,
    in_all,
    in_box,
    in_final,
    in_swap,
    emb_box,
    emb_mine,
    emb_part,
    emb_final,
    ssq,
    norm_box,
    y_send,
    y_recv,
    part_recv,
    final_recv,
    part_send,
    final_send,
    write_sem,
    in_send,
    in_recv,
    emb_send,
    emb_recv,
    misc_recv,
    misc_send,
    norm_send,
    norm_recv,
):
    model = lax.axis_index("dir")
    group = lax.axis_index("group")
    z = lax.axis_index("dp")
    core = lax.rem(group, 2)
    chip = group // 2
    peers = 2 * chips
    middle = depth // 2
    rows_out = kept_ref.shape[1] // peers
    wide = pre_ref.shape[1]
    tall = turned.shape[0]
    lot = tall // 16
    batches = rows_out // tall
    groups = rows_out // 16
    per_pass = lot // peers
    upper = depth - 1 > middle
    is_middle = z == middle
    low = z < middle
    has_away = jnp.logical_or(jnp.logical_and(low, z > 0), jnp.logical_and(z > middle, z < depth - 1))
    toward = jnp.where(low, z + 1, jnp.maximum(z - 1, 0))
    away = jnp.where(low, jnp.maximum(z - 1, 0), jnp.minimum(z + 1, depth - 1))

    def in_group(index):
        return (model, index, z)

    def in_line(index):
        return (model, group, index)

    def owner_of(slot):
        if slot == 0:
            return group
        if slot == 1:
            return group + 1 - 2 * core
        step = (slot - 2) // 2 + 1
        side = core if slot % 2 == 0 else 1 - core
        return 2 * lax.rem(chip + step, chips) + side

    def slot_there(slot):
        if slot == 1:
            return 1
        step = (slot - 2) // 2 + 1
        return 2 + 2 * (chips - step - 1) + slot % 2

    order = list(range(2, peers)) + [1, 0]
    barrier = pltpu.get_barrier_semaphore()
    for slot in range(1, peers):
        pl.semaphore_signal(barrier, inc=1, device_id=in_group(owner_of(slot)), device_id_type=MESH)

    @pl.when(z > 0)
    def _():
        pl.semaphore_signal(
            barrier, inc=1, device_id=in_line(jnp.maximum(z - 1, 0)), device_id_type=MESH
        )

    @pl.when(z < depth - 1)
    def _():
        pl.semaphore_signal(
            barrier, inc=1, device_id=in_line(jnp.minimum(z + 1, depth - 1)), device_id_type=MESH
        )

    pl.semaphore_wait(
        barrier,
        peers - 1 + jnp.where(z > 0, 1, 0) + jnp.where(z < depth - 1, 1, 0),
    )
    ssq[...] = jnp.zeros_like(ssq)

    def remote(src, dst, send, recv, device):
        return pltpu.make_async_remote_copy(
            src_ref=src,
            dst_ref=dst,
            send_sem=send,
            recv_sem=recv,
            device_id=device,
            device_id_type=MESH,
        )

    def squares(value):
        square = value * value
        total = square[:, :128]
        for lane in range(128, value.shape[1], 128):
            total = total + square[:, lane : lane + 128]
        rows = total[:16]
        for row in range(16, value.shape[0], 16):
            rows = rows + total[row : row + 16]
        ssq[...] = ssq[...] + rows

    def send_partial(mine, part, fin, sems):
        @pl.when(jnp.logical_not(is_middle))
        def _():
            @pl.when(has_away)
            def _():
                remote(mine, part, sems["ps"], sems["pr"], in_line(away)).wait_recv()
                mine[...] = (
                    mine[...].astype(jnp.float32) + part[...].astype(jnp.float32)
                ).astype(mine.dtype)

            if upper:

                @pl.when(z == middle + 1)
                def _():
                    remote(mine, fin, sems["ps"], sems["fr"], in_line(toward)).start()

            @pl.when(z != middle + 1)
            def _():
                remote(mine, part, sems["ps"], sems["pr"], in_line(toward)).start()

        @pl.when(is_middle)
        def _():
            remote(mine, part, sems["ps"], sems["pr"], in_line(toward)).wait_recv()
            total = mine[...].astype(jnp.float32) + part[...].astype(jnp.float32)
            if upper:
                remote(mine, fin, sems["ps"], sems["fr"], in_line(toward)).wait_recv()
                total = total + fin[...].astype(jnp.float32)
            fin[...] = total.astype(fin.dtype)
            remote(fin, fin, sems["f0"], sems["fr"], in_line(middle - 1)).start()
            if upper:
                remote(fin, fin, sems["f1"], sems["fr"], in_line(middle + 1)).start()

    def pass_final(fin, sems):
        @pl.when(jnp.logical_not(is_middle))
        def _():
            remote(fin, fin, sems["f0"], sems["fr"], in_line(toward)).wait_recv()

            @pl.when(has_away)
            def _():
                remote(fin, fin, sems["f0"], sems["fr"], in_line(away)).start()

    def wait_line(mine, fin, sems):
        @pl.when(is_middle)
        def _():
            remote(fin, fin, sems["f0"], sems["fr"], in_line(toward)).wait_send()
            if upper:
                remote(fin, fin, sems["f1"], sems["fr"], in_line(toward)).wait_send()

        @pl.when(jnp.logical_not(is_middle))
        def _():
            remote(mine, fin, sems["ps"], sems["fr"], in_line(toward)).wait_send()

            @pl.when(has_away)
            def _():
                remote(fin, fin, sems["f0"], sems["fr"], in_line(away)).wait_send()

    def line_sems(unit):
        return {
            "pr": part_recv.at[unit],
            "fr": final_recv.at[unit],
            "ps": part_send.at[unit],
            "f0": final_send.at[0, unit],
            "f1": final_send.at[1, unit],
        }

    extra_rows = 4 // chips
    emb_sems = line_sems(2 * (groups + extra_rows))

    def send_block(slot, parity, index, row):
        return remote(
            outbox.at[slot - 1, parity, index],
            inbox.at[slot_there(slot), row],
            y_send.at[slot - 1, parity, index],
            y_recv.at[slot_there(slot) - 1, row],
            in_group(owner_of(slot)),
        )

    span = 1024

    def product(dest):
        def columns(j, carry):
            cols = pl.ds(pl.multiple_of(j * span, span), span)
            dest[:, :, cols] = (
                jnp.dot(turned[...], pre_ref[:, cols], preferred_element_type=jnp.float32)
                .astype(jnp.bfloat16)
                .reshape(lot, 16, span)
            )
            return carry

        lax.fori_loop(0, wide // span, columns, 0)

    def fetch(turn, b):
        start = owner_of(order[turn]) * rows_out + b * tall
        return pltpu.make_async_copy(
            kept_ref.at[:, pl.ds(pl.multiple_of(start, tall), tall)],
            fetched.at[turn % 2],
            fetch_sem.at[turn % 2],
        )

    def block(turn, b, parity):
        slot = order[turn]
        if turn + 1 < peers:
            fetch(turn + 1, b).start()
        else:

            @pl.when(b + 1 < batches)
            def _():
                fetch(0, b + 1).start()

        fetch(turn, b).wait()
        turned[...] = jnp.transpose(fetched[turn % 2])
        if slot == 0:
            product(inbox.at[0, pl.ds(b * lot, lot)])
        else:

            @pl.when(b >= 2)
            def _():
                for index in range(lot):
                    send_block(slot, parity, index, 0).wait_send()

            product(outbox.at[slot - 1, parity])

    def send(row):
        parity, index = lax.rem(row // lot, 2), lax.rem(row, lot)
        if chips > 1:

            @pl.when(row > 0)
            def _():
                send_block(2, parity, index, row).start()

        for slot in list(range(3, peers)) + [1]:
            send_block(slot, parity, index, row).start()

    def take(row):
        @pl.when(row < groups)
        def _():
            for slot in range(1, peers):
                remote(
                    outbox.at[slot - 1, 0, 0],
                    inbox.at[slot, row],
                    y_send.at[slot - 1, 0, 0],
                    y_recv.at[slot - 1, row],
                    in_group(owner_of(slot)),
                ).wait_recv()
            if chips > 1:
                for part in range(2):
                    total = inbox[part, row].astype(jnp.float32)
                    for slot in range(2 + part, peers, 2):
                        total = total + inbox[slot, row].astype(jnp.float32)
                    inbox[part, row] = total.astype(jnp.bfloat16)

        @pl.when(row == groups)
        def _():
            for step in range(1, chips):
                in_copy(step).wait_recv()

        @pl.when(row >= groups)
        def _():
            for part in range(2):
                for k in range(chips):
                    first = (2 * (row - groups) + part) * chips + k
                    at = pl.ds(pl.multiple_of(first * 16, 16), 16)
                    total = in_all[at, in_columns(chip)].astype(jnp.float32)
                    for step in range(1, chips):
                        total = total + in_box[step - 1, at].astype(jnp.float32)
                    inbox[part, row, :, pl.ds(k * in_wide, in_wide)] = total.astype(jnp.bfloat16)

        for part in range(2):
            send_partial(
                inbox.at[part, row],
                partial.at[2 * row + part],
                final.at[2 * row + part],
                line_sems(2 * row + part),
            )

    def write_out(row, part):
        side = core if part == 0 else 1 - core
        return pltpu.make_async_copy(
            final.at[2 * row + part],
            rec_hbm.at[side, pl.ds(pl.multiple_of(row * 16, 16), 16)],
            write_sem.at[2 * row + part],
        )

    def finish(row):
        for part in range(2):
            pass_final(final.at[2 * row + part], line_sems(2 * row + part))

            @pl.when(row < groups)
            def _():
                write_out(row, part).start()

            squares(final[2 * row + part].astype(jnp.float32))

    def settle(row):
        for part in range(2):
            wait_line(inbox.at[part, row], final.at[2 * row + part], line_sems(2 * row + part))

            @pl.when(row < groups)
            def _():
                write_out(row, part).wait()

    in_wide = wide // chips

    def in_columns(index):
        return pl.ds(pl.multiple_of(index * in_wide, in_wide), in_wide)

    def in_copy(step):
        there = lax.rem(chip + step, chips)
        return remote(
            in_all.at[:, in_columns(there)],
            in_box.at[chips - step - 1],
            in_send.at[step - 1],
            in_recv.at[chips - step - 1],
            in_group(2 * there + core),
        )

    def emb_copy(slot, source):
        return remote(
            emb_mine,
            emb_box.at[source],
            emb_send.at[slot - 1],
            emb_recv.at[source],
            in_group(owner_of(slot)),
        )

    def small_products():
        turned[...] = jnp.transpose(aug_ref[...])

        def columns(j, carry):
            cols = pl.ds(pl.multiple_of(j * span, span), span)
            in_all[:, cols] = jnp.dot(
                turned[...], pre_ref[:, cols], preferred_element_type=jnp.float32
            ).astype(jnp.bfloat16)
            return carry

        lax.fori_loop(0, wide // span, columns, 0)
        into = lax.dot_general(
            pre_ref[...], in_ref[...], (((1,), (1,)), ((), ())), preferred_element_type=jnp.float32
        ).astype(jnp.bfloat16)
        vocab_rows = emb_mine.shape[0]
        ids = lax.broadcasted_iota(jnp.int32, (vocab_rows, chars_ref.shape[1]), 0)
        onehot = jnp.where(chars_ref[...] == ids, 1.0, 0.0).astype(jnp.bfloat16)
        summed = jnp.dot(onehot, into, preferred_element_type=jnp.float32)
        lanes = lax.broadcasted_iota(jnp.int32, summed.shape, 1)
        emb_mine[...] = jnp.where(lanes < embed, summed, 0.0) + extra_ref[...]

    def send_in():
        for step in range(1, chips):
            in_copy(step).start()

    def send_emb():
        for slot in range(1, peers):
            emb_copy(slot, group).start()

    def take_emb():
        for slot in range(1, peers):
            emb_copy(slot, owner_of(slot)).wait_recv()
        for slot in range(1, peers):
            emb_copy(slot, group).wait_send()
        emb_box[group] = emb_mine[...]
        total = emb_box[0]
        for source in range(1, peers):
            total = total + emb_box[source]
        emb_mine[...] = total
        send_partial(emb_mine, emb_part, emb_final, emb_sems)

    lead = (peers - 2) * per_pass
    y_lag, hop_lag, settle_lag = 3, 2, 6
    hops = jnp.where(low, middle - z, z - middle)
    most_hops = max(middle, depth - 1 - middle)
    before = groups // 2
    places = groups + extra_rows + 1
    steps = places + y_lag + hop_lag * most_hops + settle_lag + lead
    rounds = -(-steps // lot)

    def row_at(place):
        is_in = jnp.logical_and(place >= before, place < before + extra_rows)
        return jnp.where(
            is_in,
            groups + place - before,
            jnp.where(place < before, place, place - extra_rows - 1),
        )

    def visit(place, rows, emb):
        is_emb = place == before + extra_rows
        inside = jnp.logical_and(place >= 0, place < places)

        @pl.when(jnp.logical_and(inside, jnp.logical_not(is_emb)))
        def _():
            rows(row_at(place))

        @pl.when(is_emb)
        def _():
            emb()

    def send_any(row):
        @pl.when(row < groups)
        def _():
            send(row)

        @pl.when(row == groups)
        def _():
            send_in()

    def round_of(b, carry):
        parity = lax.rem(b, 2)

        @pl.when(b == 1)
        def _():
            small_products()

        for turn in range(peers):

            @pl.when(b < batches)
            def _():
                block(turn, b, parity)

            if turn == 0 and chips > 1:

                @pl.when(b == 0)
                def _():
                    send_block(2, 0, 0, 0).start()

            def step(j, inner):
                sent = b * lot + turn * per_pass + j - lead
                arrived = sent - y_lag
                summed = arrived - hop_lag * hops
                visit(sent, send_any, send_emb)
                visit(arrived, take, take_emb)
                visit(summed, finish, lambda: pass_final(emb_final, emb_sems))
                visit(
                    summed - settle_lag,
                    settle,
                    lambda: wait_line(emb_mine, emb_final, emb_sems),
                )
                return inner

            lax.fori_loop(0, per_pass, step, 0)

        return carry

    fetch(0, 0).start()
    lax.fori_loop(0, rounds, round_of, 0)
    for u in range(2 * extra_rows):
        for k in range(chips):
            first = (u * chips + k) * 16
            in_final[first : first + 16] = final[
                2 * groups + u, :, k * in_wide : (k + 1) * in_wide
            ]

    keep_cols = in_wide // 2
    if in_wide > wide // 4:
        mine = pl.ds(pl.multiple_of(core * keep_cols, keep_cols), keep_cols)
        theirs = pl.ds(pl.multiple_of((1 - core) * keep_cols, keep_cols), keep_cols)
        swap = remote(
            in_final.at[:, theirs], in_swap, misc_send, misc_recv, in_group(owner_of(1))
        )
        swap.start()
        swap.wait()
        inout_ref[:, mine] = in_final[:, mine]
        inout_ref[:, theirs] = in_swap[...]
    else:
        inout_ref[...] = in_final[...]
    emb_ref[...] = emb_final[...]

    squares(dec_ref[...].astype(jnp.float32))
    norm_box[group] = ssq[...]

    def norm_copy(slot, source):
        return remote(
            ssq,
            norm_box.at[source],
            norm_send.at[slot - 1],
            norm_recv.at[source],
            in_group(owner_of(slot)),
        )

    for slot in range(1, peers):
        norm_copy(slot, group).start()
    for slot in range(1, peers):
        norm_copy(slot, owner_of(slot)).wait_recv()
    for slot in range(1, peers):
        norm_copy(slot, group).wait_send()
    total = norm_box[0]
    for source in range(1, peers):
        total = total + norm_box[source]
    lanes = lax.broadcasted_iota(jnp.int32, emb_final.shape, 1)
    small = jnp.where(lanes <= embed, emb_final[...], 0.0)
    total_sq = jnp.sum(total) + jnp.sum(small * small)
    clip_ref[...] = jnp.full(clip_ref.shape, 0.25, jnp.float32) / jnp.maximum(
        jnp.sqrt(jnp.full(clip_ref.shape, total_sq, jnp.float32)), 0.25
    )

    for step in range(1, chips):
        in_copy(step).wait_send()
    for slot in range(1, peers):
        for parity in range(min(2, batches)):
            for index in range(lot):
                send_block(slot, parity, index, 0).wait_send()


def run_reduce(chips, depth, embed, kept, aug, pre, in_own, chars, extra, dec_sum):
    hidden = kept.shape[1]
    count, wide = pre.shape
    peers = 2 * chips
    rows_out = hidden // peers
    tall = 128
    lot = tall // 16
    groups = rows_out // 16
    extra_rows = 4 // chips
    units = 2 * (groups + extra_rows)
    in_rows = aug.shape[1]
    in_wide = wide // chips
    in_cols = 2 * wide // peers
    vmem = pl.BlockSpec(memory_space=pltpu.VMEM)
    bf16, f32 = jnp.bfloat16, jnp.float32
    small = extra.shape
    dma = pltpu.SemaphoreType.DMA
    return pl.pallas_call(
        functools.partial(reduce_kernel, chips, depth, embed),
        in_specs=[pl.BlockSpec(memory_space=pl.ANY)] + [vmem] * 6,
        out_specs=[pl.BlockSpec(memory_space=pl.ANY), vmem, vmem, vmem],
        out_shape=[
            jax.ShapeDtypeStruct((2, rows_out, wide), bf16),
            jax.ShapeDtypeStruct((in_rows, in_cols), bf16),
            jax.ShapeDtypeStruct(small, f32),
            jax.ShapeDtypeStruct((8, 128), f32),
        ],
        scratch_shapes=[
            pltpu.VMEM((tall, count), bf16),
            pltpu.VMEM((2, count, tall), bf16),
            dma((2,)),
            pltpu.VMEM((peers, groups + extra_rows, 16, wide), bf16),
            pltpu.VMEM((peers - 1, 2, lot, 16, wide), bf16),
            pltpu.VMEM((units, 16, wide), bf16),
            pltpu.VMEM((units, 16, wide), bf16),
            pltpu.VMEM((in_rows, wide), bf16),
            pltpu.VMEM((max(chips - 1, 1), in_rows, in_wide), bf16),
            pltpu.VMEM((in_rows, in_wide), bf16),
            pltpu.VMEM((in_rows, in_wide // 2), bf16),
            pltpu.VMEM((peers,) + small, f32),
            pltpu.VMEM(small, f32),
            pltpu.VMEM(small, f32),
            pltpu.VMEM(small, f32),
            pltpu.VMEM((16, 128), f32),
            pltpu.VMEM((peers, 16, 128), f32),
            dma((peers - 1, 2, lot)),
            dma((peers - 1, groups)),
            dma((units + 1,)),
            dma((units + 1,)),
            dma((units + 1,)),
            dma((2, units + 1)),
            dma((units,)),
            dma((max(chips - 1, 1),)),
            dma((max(chips - 1, 1),)),
            dma((peers - 1,)),
            dma((peers,)),
            dma,
            dma,
            dma((peers - 1,)),
            dma((peers,)),
        ],
        compiler_params=pltpu.CompilerParams(
            collective_id=3, has_side_effects=True, vmem_limit_bytes=60 << 20
        ),
        cost_estimate=pl.CostEstimate(
            flops=2 * count * hidden * wide, bytes_accessed=700 << 20, transcendentals=0
        ),
    )(kept, aug, pre, in_own, chars, extra, dec_sum)


def middle_kernel(
    vocab,
    seg_len,
    out_ref,
    target_ref,
    dec_ref,
    bias_ref,
    slot_row_ref,
    slot_col_ref,
    wg_ref,
    outg_ref,
    decg_ref,
    stat_ref,
    picked_ref,
    dec_acc,
    pick_acc,
):
    i = pl.program_id(0)
    last = pl.num_programs(0) - 1
    core = lax.rem(lax.axis_index("group"), 2)
    span, pair, hidden = out_ref.shape
    count = span * pair
    units = hidden // 2
    seg = pair // 2
    slots = wg_ref.shape[0] // pair
    wide = dec_ref.shape[1]
    bf16, f32, i32 = jnp.bfloat16, jnp.float32, jnp.int32
    out = out_ref[...].reshape(count, hidden)

    @pl.when(i == 0)
    def _():
        dec_acc[...] = jnp.zeros_like(dec_acc)
        pick_acc[...] = jnp.zeros_like(pick_acc)
        stat_ref[...] = jnp.zeros_like(stat_ref)

    logits = jnp.dot(out, dec_ref[...], preferred_element_type=f32) + bias_ref[...]
    top = jnp.max(logits, axis=1, keepdims=True)
    powers = jnp.exp(logits - top)
    total = jnp.sum(powers, axis=1, keepdims=True)
    lanes = lax.broadcasted_iota(i32, (count, wide), 1)
    hit = lanes == target_ref[...]
    rows = lax.broadcasted_iota(i32, (count, 1), 0)
    segment = lax.rem(rows, pair)
    mine = jnp.logical_and(segment >= core * seg, segment < (core + 1) * seg)
    loss = top + jnp.log(total) - jnp.sum(jnp.where(hit, logits, 0.0), axis=1, keepdims=True)
    loss = jnp.sum(jnp.where(mine, loss, 0.0))
    grad = (powers / total - jnp.where(hit, 1.0, 0.0)) * (1.0 / seg_len)
    grad_b = grad.astype(bf16)
    own_b = jnp.where(mine, grad_b.astype(f32), 0.0)
    stat_ref[0:1] += jnp.sum(own_b, axis=0, keepdims=True)
    stat_ref[1:2] += jnp.full((1, wide), loss, f32)
    dec_acc[...] += jnp.dot(
        jnp.transpose(own_b.astype(bf16)), out, preferred_element_type=f32
    )

    step = rows // pair + i * span
    slot_count = wg_ref.shape[0]
    col = lax.broadcasted_iota(i32, (count, slot_count), 1)
    at_word = jnp.logical_and(slot_row_ref[...] == step, col // slots == segment)
    words = jnp.where(at_word, 1.0, 0.0).astype(bf16)
    half = pl.ds(pl.multiple_of(core * units, units), units)
    outg_ref[...] = lax.dot_general(
        grad_b, dec_ref[half], (((1,), (1,)), ((), ())), preferred_element_type=f32
    ) + jnp.dot(words, wg_ref[...], preferred_element_type=f32)

    own_slots = seg * slots
    across = lax.broadcasted_iota(i32, (own_slots, count), 1)
    slot_segment = lax.broadcasted_iota(i32, (own_slots, 1), 0) // slots + core * seg
    picks = jnp.logical_and(
        slot_col_ref[...] == across // pair + i * span, lax.rem(across, pair) == slot_segment
    )
    pick_acc[...] += jnp.dot(
        jnp.where(picks, 1.0, 0.0).astype(bf16), out, preferred_element_type=f32
    )

    @pl.when(i == last)
    def _():
        decg_ref[...] = dec_acc[: decg_ref.shape[0]].astype(bf16)
        picked_ref[...] = pick_acc[...].astype(bf16)


def run_middle(vocab, out_all, targets, decoder, bias, slot_row, slot_col, wg_pair):
    steps, pair, hidden = out_all.shape
    span = 4 if steps % 4 == 0 else 1
    count = span * pair
    units = hidden // 2
    wide = decoder.shape[1]
    vocab_rows = -(-vocab // 32) * 32
    own_slots = slot_col.shape[0]
    bf16, f32 = jnp.bfloat16, jnp.float32

    def fixed(shape):
        return pl.BlockSpec(shape, lambda i: (0,) * len(shape))

    return pl.pallas_call(
        functools.partial(middle_kernel, vocab, steps),
        grid=(steps // span,),
        in_specs=[
            pl.BlockSpec((span, pair, hidden), lambda i: (i, 0, 0)),
            pl.BlockSpec((count, 1), lambda i: (i, 0)),
            fixed(decoder.shape),
            fixed(bias.shape),
            fixed(slot_row.shape),
            fixed(slot_col.shape),
            fixed(wg_pair.shape),
        ],
        out_specs=[
            pl.BlockSpec((count, units), lambda i: (i, 0)),
            fixed((vocab_rows, hidden)),
            fixed((8, wide)),
            fixed((own_slots, hidden)),
        ],
        out_shape=[
            jax.ShapeDtypeStruct((steps * pair, units), f32),
            jax.ShapeDtypeStruct((vocab_rows, hidden), bf16),
            jax.ShapeDtypeStruct((8, wide), f32),
            jax.ShapeDtypeStruct((own_slots, hidden), bf16),
        ],
        scratch_shapes=[
            pltpu.VMEM((wide, hidden), f32),
            pltpu.VMEM((own_slots, hidden), f32),
        ],
        compiler_params=pltpu.CompilerParams(vmem_limit_bytes=48 << 20),
    )(out_all, targets, decoder, bias, slot_row, slot_col, wg_pair)


def update_kernel(
    count,
    clip_ref,
    sum_ref,
    moment_ref,
    in_ref,
    emb_ref,
    dec_ref,
    mom_in_ref,
    mom_bias_ref,
    mom_dec_ref,
    mom_emb_ref,
    mom_dbias_ref,
    grad_ref,
    next_ref,
    *small,
):
    clip = clip_ref[0, 0]
    gradient = sum_ref[0].astype(jnp.float32)
    grad_ref[0] = gradient
    next_ref[0] = momentum_step(moment_ref[0], gradient, clip)

    index = (pl.program_id(0) * pl.num_programs(1) + pl.program_id(1)) * pl.num_programs(2)
    index = index + pl.program_id(2)
    embed = mom_in_ref.shape[0]
    vocab = mom_emb_ref.shape[0]

    def turned():
        return jnp.transpose(emb_ref[...])

    results = [
        (lambda: in_ref[...].astype(jnp.float32)[:embed], mom_in_ref),
        (lambda: in_ref[...].astype(jnp.float32)[embed : embed + 1], mom_bias_ref),
        (lambda: dec_ref[...].astype(jnp.float32)[:vocab], mom_dec_ref),
        (lambda: emb_ref[:vocab, :embed], mom_emb_ref),
        (lambda: turned()[embed : embed + 1, :vocab], mom_dbias_ref),
    ]

    @pl.when(index == 0)
    def _():
        small[0][...] = turned()[embed + 1 : embed + 2, :128] / count

    def one(k, value_of, moment):
        @pl.when(index == k + 1)
        def _():
            value = value_of().reshape(moment.shape)
            small[1 + 2 * k][...] = value
            small[2 + 2 * k][...] = momentum_step(moment[...], value, clip)

    for k, (value_of, moment) in enumerate(results):
        one(k, value_of, moment)


def run_update(count, clip, sums, in_sum, emb_sum, dec_sum, moments):
    mom_rec, mom_in, mom_bias, mom_dec, mom_emb, mom_dbias = moments
    halves, rows, wide = sums.shape
    span = wide // 4
    tall = rows
    block = pl.BlockSpec((1, tall, span), lambda q, s, r: (0, r, 2 * q + s))
    f32 = jnp.float32

    def fixed(shape):
        return pl.BlockSpec(shape, lambda q, s, r: (0,) * len(shape))

    rec_shape = jax.ShapeDtypeStruct(mom_rec.shape, f32)
    small = [mom_in, mom_bias, mom_dec, mom_emb, mom_dbias]
    shapes = [(1, 128)]
    for moment in small:
        shapes += [moment.shape, moment.shape]
    return pl.pallas_call(
        functools.partial(update_kernel, count),
        grid=(4, 2, 1),
        in_specs=[
            pl.BlockSpec(memory_space=pltpu.SMEM),
            pl.BlockSpec((1, tall, span), lambda q, s, r: (s, r, q)),
            block,
        ]
        + [fixed(x.shape) for x in (in_sum, emb_sum, dec_sum, *small)],
        out_specs=[block, block] + [fixed(shape) for shape in shapes],
        out_shape=[rec_shape, rec_shape] + [jax.ShapeDtypeStruct(shape, f32) for shape in shapes],
        compiler_params=pltpu.CompilerParams(vmem_limit_bytes=56 << 20),
    )(clip, sums, mom_rec, in_sum, emb_sum, dec_sum, *small)


def shards(
    chars,
    targets,
    resets,
    word_pos,
    h_init,
    c_init,
    word_grad,
    w_emb,
    w_in,
    w_rec,
    b_rec,
    w_dec,
    b_dec,
    mom_emb,
    mom_in,
    mom_rec,
    mom_bias,
    mom_dec,
    mom_dbias,
):
    vocab_size = w_emb.shape[1]
    embed_size = w_emb.shape[2]
    seg_len = chars.shape[2]
    batch_size = chars.shape[1]
    hidden_size = w_rec.shape[2] // 4
    units = hidden_size // 2
    core = lax.rem(lax.axis_index("group"), 2)
    first = core == 0

    depth = 128
    vocab_lanes = -(-vocab_size // 128) * 128
    vocab_rows = -(-vocab_size // 32) * 32
    dec_full = lax.all_gather(w_dec[0].astype(jnp.bfloat16), "group", axis=0, tiled=True)
    in_bias = jnp.concatenate(
        [w_in[0], b_rec, jnp.zeros((depth - embed_size - 1, w_in.shape[2]), jnp.float32)]
    ).astype(jnp.bfloat16)
    word_slots = word_pos.shape[2]
    spare = -(3 * seg_len + word_slots) % 128
    ids = jnp.concatenate(
        [
            chars[0],
            targets[0],
            resets[0],
            word_pos[0],
            jnp.zeros((batch_size, spare), jnp.int32),
        ],
        axis=1,
    )
    weights, weights_t, h_pair, c_pair, wg_pair, packed, in_own = run_gather(
        lax.axis_size("group") // 2,
        lax.axis_size("dp"),
        w_rec[0],
        in_bias,
        h_init[0],
        c_init[0],
        word_grad.reshape(batch_size * word_slots, hidden_size),
        ids,
    )
    chars2 = packed[:, :seg_len]
    targets2 = packed[:, seg_len : 2 * seg_len]
    resets2 = packed[:, 2 * seg_len : 3 * seg_len]
    word_pos2 = packed[:, 3 * seg_len : 3 * seg_len + word_slots]
    char_major = jnp.transpose(chars2)
    char_onehot = (char_major[:, :, None] == jnp.arange(vocab_size, dtype=jnp.int32)).astype(
        jnp.bfloat16
    )
    embedded = jnp.einsum(
        "tbv,ve->tbe",
        char_onehot,
        w_emb[0].astype(jnp.bfloat16),
        preferred_element_type=jnp.float32,
    ).astype(jnp.bfloat16)
    pad_shape = (seg_len, 2 * batch_size, depth - embed_size - 1)
    embedded_one = jnp.concatenate(
        [
            embedded,
            jnp.ones((seg_len, 2 * batch_size, 1), jnp.bfloat16),
            jnp.zeros(pad_shape, jnp.bfloat16),
        ],
        axis=-1,
    )
    keep_major = jnp.broadcast_to(
        (1 - jnp.transpose(resets2)).astype(jnp.float32)[:, :, None],
        (seg_len, 2 * batch_size, 128),
    )
    out_all, kept_all, gate_all, cell_all, cellkept_all = run_forward(
        embedded_one, keep_major, h_pair, c_pair, weights
    )
    positions = seg_len * 2 * batch_size
    out_grad, dec_grad, stats, picked = run_middle(
        vocab_size,
        out_all,
        jnp.transpose(targets2).reshape(positions, 1),
        jnp.pad(dec_full, ((0, 0), (0, vocab_lanes - vocab_size))),
        jnp.pad(b_dec, ((0, 0), (0, vocab_lanes - vocab_size)), constant_values=-1e30),
        word_pos2.reshape(1, 2 * batch_size * word_slots),
        word_pos[0].reshape(batch_size * word_slots, 1),
        wg_pair,
    )
    dec_sum = lax.psum(dec_grad, ("group", "dp"))
    picked = picked.reshape(batch_size, word_slots, hidden_size)
    half_slots = picked.shape[1] // 2
    model_index = lax.axis_index("dir")
    own_slots = lax.dynamic_slice_in_dim(picked, model_index * half_slots, half_slots, 1)
    other_slots = lax.dynamic_slice_in_dim(picked, (1 - model_index) * half_slots, half_slots, 1)
    partner_half = partner(other_slots, "dir", 0)
    leading = model_index == 0
    word_vectors = jnp.where(
        leading,
        jnp.concatenate([own_slots, partner_half], axis=-1),
        jnp.concatenate([partner_half, own_slots], axis=-1),
    )
    pre_all, grad_hidden0, grad_cell0 = run_backward(
        out_grad.reshape(seg_len, 2 * batch_size, units), gate_all, cell_all, cellkept_all, keep_major, weights_t
    )

    rows_own = w_dec.shape[1]
    dec_sum = lax.dynamic_slice_in_dim(
        dec_sum, lax.axis_index("group") * rows_own, rows_own, 1
    )
    extra = jnp.concatenate(
        [
            jnp.zeros((vocab_rows, embed_size), jnp.float32),
            stats[0, :vocab_rows, None],
            jnp.broadcast_to(stats[1, 0], (vocab_rows, 1)),
            jnp.zeros((vocab_rows, depth - embed_size - 2), jnp.float32),
        ],
        axis=1,
    )
    rec_sum, in_out, emb_out, clip = run_reduce(
        lax.axis_size("group") // 2,
        lax.axis_size("dp"),
        embed_size,
        kept_all.reshape(positions, hidden_size),
        embedded_one.reshape(positions, depth),
        pre_all.reshape(positions, 4 * units),
        in_own,
        char_major.reshape(1, positions),
        extra,
        dec_sum,
    )
    token_count = seg_len * batch_size * lax.axis_size("group") * lax.axis_size("dp")
    grad_rec, next_rec, losses, *small = run_update(
        token_count,
        clip,
        rec_sum,
        in_out,
        emb_out,
        dec_sum,
        (
            mom_rec,
            jnp.transpose(mom_in, (1, 0, 2)),
            mom_bias,
            jnp.transpose(mom_dec, (2, 0, 1)),
            jnp.transpose(mom_emb, (1, 0, 2)),
            mom_dbias,
        ),
    )
    grad_in, next_in, grad_bias, next_bias, grad_dec, next_dec = small[:6]
    grad_emb, next_emb, grad_dbias, next_dbias = small[6:]
    return (
        losses[0, :1],
        word_vectors,
        grad_hidden0[None],
        grad_cell0[None],
        jnp.transpose(grad_emb, (1, 0, 2)),
        jnp.transpose(grad_in, (1, 0, 2)),
        grad_rec,
        grad_bias,
        jnp.transpose(grad_dec, (1, 2, 0)),
        grad_dbias,
        jnp.transpose(next_emb, (1, 0, 2)),
        jnp.transpose(next_in, (1, 0, 2)),
        next_rec,
        next_bias,
        jnp.transpose(next_dec, (1, 2, 0)),
        next_dbias,
    )


def solution(mesh):
    segments = P("dir", ("group", "dp"), None)
    shared = P("dir", None, None)
    columns = P("dir", None, "group")
    rows = P("dir", "group", None)
    flat = P("dir", "group")
    return jax.shard_map(
        shards,
        mesh=mesh,
        in_specs=(
            segments,
            segments,
            segments,
            segments,
            segments,
            segments,
            P(("group", "dp"), None, "dir"),
            shared,
            columns,
            rows,
            flat,
            rows,
            P("dir", None),
            shared,
            columns,
            rows,
            flat,
            rows,
            P("dir", None),
        ),
        out_specs=(
            P("dir"),
            P(("group", "dp"), "dir", None),
            segments,
            segments,
            shared,
            columns,
            rows,
            flat,
            rows,
            P("dir", None),
            shared,
            columns,
            rows,
            flat,
            rows,
            P("dir", None),
        ),
        check_vma=False,
    )
```

```python
import functools

import jax
import jax.numpy as jnp
from jax import lax
from jax.experimental import pallas as pl
from jax.experimental.pallas import tpu as pltpu
from jax.sharding import PartitionSpec as P

MESH = pl.DeviceIdType.MESH
CHUNK = 256


def partner(value, axis, bit):
    mask = 2**bit
    pairs = [(source, source ^ mask) for source in range(lax.axis_size(axis))]
    return lax.ppermute(value, axis, pairs)


def momentum_step(moment, gradient, clip_scale):
    return 0.9 * moment + clip_scale * gradient


def sigmoid(value):
    return 0.5 * jnp.tanh(0.5 * value) + 0.5


def core_peer():
    group = lax.axis_index("group")
    core = lax.rem(group, 2)
    return core, (lax.axis_index("dir"), group + 1 - 2 * core, lax.axis_index("dp"))


def greet(peers):
    barrier = pltpu.get_barrier_semaphore()
    for peer in peers:
        pl.semaphore_signal(barrier, inc=1, device_id=peer, device_id_type=MESH)
    pl.semaphore_wait(barrier, len(peers))


def gather_kernel(
    chips,
    shared,
    rec_hbm,
    inb_ref,
    h_ref,
    c_ref,
    wg_ref,
    ids_ref,
    w_hbm,
    wt_hbm,
    h_out,
    c_out,
    wg_out,
    ids_out,
    in_out,
    w_ref,
    wt_ref,
    stage,
    loaded,
    load_sem,
    core_send,
    core_recv,
    y_send,
    y_recv,
    z_send,
    z_recv,
    in_send,
    in_recv,
    inz_send,
    inz_recv,
    seg_send,
    seg_recv,
    w_out_sem,
    wt_out_sem,
):
    model = lax.axis_index("dir")
    group = lax.axis_index("group")
    z = lax.axis_index("dp")
    core = lax.rem(group, 2)
    chip = group // 2
    peers = 2 * chips
    rows = stage.shape[0]
    piece = loaded.shape[1]
    units = w_ref.shape[1] // 4
    hidden = 2 * units
    pieces = rows // piece
    mine = pieces // 2 if shared else pieces
    part = lax.rem(z, 2) if shared else 0
    buddy = z + 1 - 2 * lax.rem(z, 2) if shared else z
    far = list(range(2, peers))

    def owner_of(slot):
        if slot == 0:
            return group
        if slot == 1:
            return group + 1 - 2 * core
        side = core if slot % 2 == 0 else 1 - core
        return 2 * lax.rem(chip + (slot - 2) // 2 + 1, chips) + side

    def slot_there(slot):
        if slot == 1:
            return 1
        return 2 + 2 * (chips - (slot - 2) // 2 - 2) + slot % 2

    def peer(slot):
        return (model, owner_of(slot), z)

    barrier = pltpu.get_barrier_semaphore()
    for slot in range(1, peers):
        pl.semaphore_signal(barrier, inc=1, device_id=peer(slot), device_id_type=MESH)
    if shared:
        pl.semaphore_signal(
            barrier, inc=1, device_id=(model, group, buddy), device_id_type=MESH
        )

    def remote(src, dst, send, recv, device):
        return pltpu.make_async_remote_copy(
            src_ref=src,
            dst_ref=dst,
            send_sem=send,
            recv_sem=recv,
            device_id=device,
            device_id_type=MESH,
        )

    def which(i):
        return lax.rem(part * mine + i, pieces)

    def load(i):
        return pltpu.make_async_copy(
            rec_hbm.at[pl.ds(pl.multiple_of(which(i) * piece, piece), piece)],
            loaded.at[lax.rem(i, 2)],
            load_sem.at[lax.rem(i, 2)],
        )

    load(0).start()
    pl.semaphore_wait(barrier, peers if shared else peers - 1)

    def rows_of(owner, k):
        return pl.ds(pl.multiple_of(owner * rows + k * piece, piece), piece)

    def rows_staged(k):
        return pl.ds(pl.multiple_of(k * piece, piece), piece)

    def to_core(k):
        return remote(
            stage.at[rows_staged(k)],
            w_ref.at[rows_of(group, k)],
            core_send.at[k],
            core_recv.at[k],
            peer(1),
        )

    def to_chip(slot, k):
        held = w_ref.at[rows_of(group, k)] if slot % 2 == 0 else stage.at[rows_staged(k)]
        return remote(
            held,
            w_ref.at[rows_of(group, k)],
            y_send.at[slot - 2, k],
            y_recv.at[slot_there(slot) - 2, k],
            peer(slot),
        )

    def to_buddy(slot, k):
        return remote(
            w_ref.at[rows_of(owner_of(slot), k)],
            w_ref.at[rows_of(owner_of(slot), k)],
            z_send.at[slot - 2, k],
            z_recv.at[slot - 2, k],
            (model, group, buddy),
        )

    blocks = inb_ref.shape[1] // units
    deep = inb_ref.shape[0]
    in_slots = list(range(peers)) if blocks == 2 else [0] + [s for s in far if s % 2 == 0]
    share_rows = deep // 2 if shared else deep

    def in_place(owner, first, count):
        gate = owner if blocks == 2 else owner // 2
        return w_ref.at[
            pl.ds(pl.multiple_of(hidden + first, 16), count),
            pl.ds(pl.multiple_of(gate * units, units), units),
        ]

    def in_block(slot):
        if blocks == 1:
            return 0
        return core if slot == 0 or (slot > 1 and slot % 2 == 0) else 1 - core

    def in_copy(slot):
        first, count = (0, deep) if slot == 1 else (part * share_rows, share_rows)
        source = inb_ref.at[
            pl.ds(pl.multiple_of(first, 16), count),
            pl.ds(pl.multiple_of(in_block(slot) * units, units), units),
        ]
        return remote(
            source,
            in_place(group, first, count),
            in_send.at[slot - 1],
            in_recv.at[slot_there(slot) - 1],
            peer(slot),
        )

    def in_buddy(slot):
        held = in_place(owner_of(slot), part * share_rows, share_rows)
        return remote(
            held, held, inz_send.at[slot - 1], inz_recv.at[slot - 1], (model, group, buddy)
        )

    for slot in in_slots:
        if slot > 1:
            in_copy(slot).start()
    gate0 = group if blocks == 2 else chip
    w_ref[hidden:, pl.ds(pl.multiple_of(gate0 * units, units), units)] = inb_ref[
        :, pl.ds(pl.multiple_of(in_block(0) * units, units), units)
    ]

    def cast(i, carry):
        k = which(i)

        @pl.when(i + 1 < pieces)
        def _():
            load(i + 1).start()

        load(i).wait()
        buffer = lax.rem(i, 2)
        for q in range(4):
            local = pl.ds(q * units, units)
            own = pl.ds(pl.multiple_of(q * hidden + core * units, units), units)
            other = pl.ds(pl.multiple_of(q * hidden + (1 - core) * units, units), units)
            w_ref[rows_of(group, k), local] = loaded[buffer, :, own].astype(jnp.bfloat16)
            stage[rows_staged(k), local] = loaded[buffer, :, other].astype(jnp.bfloat16)

        @pl.when(i < mine)
        def _():
            for slot in far:
                to_chip(slot, k).start()

        to_core(k).start()
        return carry

    lax.fori_loop(0, pieces, cast, 0)

    seg = h_ref.shape[0]
    words = wg_ref.shape[0]
    at_h = pl.ds(pl.multiple_of(core * seg, 8), seg)
    at_w = pl.ds(pl.multiple_of(core * words, 16), words)
    half_own = pl.ds(pl.multiple_of(core * units, units), units)
    half_other = pl.ds(pl.multiple_of((1 - core) * units, units), units)
    segment_copies = [
        remote(h_ref, h_out.at[at_h], seg_send.at[0], seg_recv.at[0], peer(1)),
        remote(c_ref.at[:, half_other], c_out.at[at_h], seg_send.at[1], seg_recv.at[1], peer(1)),
        remote(wg_ref.at[:, half_other], wg_out.at[at_w], seg_send.at[2], seg_recv.at[2], peer(1)),
        remote(ids_ref, ids_out.at[at_h], seg_send.at[3], seg_recv.at[3], peer(1)),
    ]
    if blocks == 2:
        in_copy(1).start()
    for copy in segment_copies:
        copy.start()
    h_out[at_h] = h_ref[...]
    c_out[at_h] = c_ref[:, half_own]
    wg_out[at_w] = wg_ref[:, half_own]
    ids_out[at_h] = ids_ref[...]

    tall = 128

    def turn(row0):
        at = pl.ds(pl.multiple_of(row0, tall), tall)
        for u in range(units // CHUNK):
            for q in range(4):
                local = pl.ds(q * units + u * CHUNK, CHUNK)
                turned = pl.ds((4 * u + q) * CHUNK, CHUNK)
                wt_ref[turned, at] = jnp.transpose(w_ref[at, local])

    def store(row0):
        at = pl.ds(pl.multiple_of(row0, tall), tall)
        index = row0 // tall
        return (
            pltpu.make_async_copy(w_ref.at[at], w_hbm.at[at], w_out_sem.at[index]),
            pltpu.make_async_copy(wt_ref.at[:, at], wt_hbm.at[:, at], wt_out_sem.at[index]),
        )

    def turn_and_store(row0):
        turn(row0)
        for copy in store(row0):
            copy.start()

    chip_rows = 2 * rows
    chip_tiles = chip_rows // tall
    per_tile = tall // piece

    def relay(i, carry):
        k = which(i)
        for slot in far:
            to_chip(slot, k).wait_recv()
            if shared:
                to_buddy(slot, k).start()
        return carry

    def wait_core(k, carry):
        to_core(k).wait_recv()
        return carry

    if shared:
        for slot in in_slots:
            if slot > 1:
                in_copy(slot).wait_recv()
                in_buddy(slot).start()
    relay(0, 0)
    lax.fori_loop(0, pieces, wait_core, 0)

    def own_tile(j, carry):
        turn_and_store(chip * chip_rows + j * tall)

        @pl.when(j + 1 < mine)
        def _():
            relay(j + 1, 0)

        return carry

    lax.fori_loop(0, chip_tiles, own_tile, 0)
    if mine > chip_tiles + 1:
        lax.fori_loop(chip_tiles + 1, mine, relay, 0)

    def far_tile(j, carry):
        for slot in far:
            turn_and_store(owner_of(slot) * rows + part * mine * piece + j * tall)
        return carry

    lax.fori_loop(0, mine // per_tile, far_tile, 0)

    if shared:

        def far_tile_late(j, carry):
            for slot in far:
                for p in range(per_tile):
                    k = (1 - part) * mine + j * per_tile + p
                    to_buddy(slot, k).wait_recv()
                turn_and_store(owner_of(slot) * rows + (1 - part) * mine * piece + j * tall)
            return carry

        lax.fori_loop(0, mine // per_tile, far_tile_late, 0)
        for slot in in_slots:
            if slot > 1:
                in_buddy(slot).wait_recv()
    else:
        for slot in in_slots:
            if slot > 1:
                in_copy(slot).wait_recv()
    if blocks == 2:
        in_copy(1).wait_recv()
    tail = pltpu.make_async_copy(
        w_ref.at[pl.ds(hidden, deep)], w_hbm.at[pl.ds(hidden, deep)], load_sem.at[0]
    )
    tail.start()
    in_out[...] = w_ref[hidden:]

    for copy in segment_copies:
        copy.wait()
    for slot in in_slots:
        if slot > 0:
            in_copy(slot).wait_send()
        if slot > 1 and shared:
            in_buddy(slot).wait_send()

    def settle(i, carry):
        k = which(i)
        to_core(k).wait_send()

        @pl.when(i < mine)
        def _():
            for slot in far:
                to_chip(slot, k).wait_send()
                if shared:
                    to_buddy(slot, k).wait_send()

        return carry

    lax.fori_loop(0, pieces, settle, 0)

    def stored(j, carry):
        for copy in store(j * tall):
            copy.wait()
        return carry

    lax.fori_loop(0, hidden // tall, stored, 0)
    tail.wait()


def run_gather(chips, depth, w_rec, in_bias, h_init, c_init, word_grad, ids):
    rows, columns = w_rec.shape
    wide = columns // 2
    units = wide // 4
    hidden = 2 * units
    deep = in_bias.shape[0]
    peers = 2 * chips
    shared = depth % 2 == 0
    piece = 32
    pieces = rows // piece
    seg = h_init.shape[0]
    vmem = pl.BlockSpec(memory_space=pltpu.VMEM)
    anywhere = pl.BlockSpec(memory_space=pl.ANY)
    bf16, f32 = jnp.bfloat16, jnp.float32
    dma = pltpu.SemaphoreType.DMA
    far = max(peers - 2, 1)
    return pl.pallas_call(
        functools.partial(gather_kernel, chips, shared),
        in_specs=[anywhere] + [vmem] * 5,
        out_specs=[anywhere, anywhere] + [vmem] * 5,
        out_shape=[
            jax.ShapeDtypeStruct((hidden + deep, wide), bf16),
            jax.ShapeDtypeStruct((wide, hidden), bf16),
            jax.ShapeDtypeStruct((2 * seg, hidden), f32),
            jax.ShapeDtypeStruct((2 * seg, units), f32),
            jax.ShapeDtypeStruct((2 * word_grad.shape[0], units), bf16),
            jax.ShapeDtypeStruct((2 * seg, ids.shape[1]), jnp.int32),
            jax.ShapeDtypeStruct((deep, wide), bf16),
        ],
        scratch_shapes=[
            pltpu.VMEM((hidden + deep, wide), bf16),
            pltpu.VMEM((wide, hidden), bf16),
            pltpu.VMEM((rows, wide), bf16),
            pltpu.VMEM((2, piece, columns), f32),
            dma((2,)),
            dma((pieces,)),
            dma((pieces,)),
            dma((far, pieces)),
            dma((far, pieces)),
            dma((far, pieces)),
            dma((far, pieces)),
            dma((peers - 1,)),
            dma((peers - 1,)),
            dma((peers - 1,)),
            dma((peers - 1,)),
            dma((4,)),
            dma((4,)),
            dma((hidden // 128,)),
            dma((hidden // 128,)),
        ],
        compiler_params=pltpu.CompilerParams(
            collective_id=4, has_side_effects=True, vmem_limit_bytes=58 << 20
        ),
        cost_estimate=pl.CostEstimate(flops=0, bytes_accessed=400 << 20, transcendentals=0),
    )(w_rec, in_bias, h_init, c_init, word_grad, ids)


def forward_kernel(
    steps,
    emb_ref,
    keep_ref,
    h0_ref,
    c0_ref,
    w_hbm,
    hid_ref,
    kept_ref,
    gates_ref,
    cell_ref,
    ckept_ref,
    w_ref,
    hown,
    hpar,
    kown,
    kpar,
    cell,
    acc,
    w_sem,
    send_sem,
    recv_sem,
):
    t = pl.program_id(0)
    slot = lax.rem(t, 2)
    nxt = 1 - slot
    core, peer = core_peer()
    units = cell.shape[1]
    hidden = 2 * units
    chunks = units // CHUNK
    own0 = pl.multiple_of(core * units, units)
    par0 = pl.multiple_of((1 - core) * units, units)

    def exchange(which, u):
        return pltpu.make_async_remote_copy(
            src_ref=hown.at[which, u],
            dst_ref=hpar.at[which, u],
            send_sem=send_sem.at[which, u],
            recv_sem=recv_sem.at[which, u],
            device_id=peer,
            device_id_type=MESH,
        )

    @pl.when(t == 0)
    def _():
        copy = pltpu.make_async_copy(w_hbm, w_ref, w_sem)
        copy.start()
        greet([peer])
        for u in range(chunks):
            hown[0, u] = h0_ref[:, pl.ds(pl.multiple_of(own0 + u * CHUNK, CHUNK), CHUNK)].astype(jnp.bfloat16)
            hpar[0, u] = h0_ref[:, pl.ds(pl.multiple_of(par0 + u * CHUNK, CHUNK), CHUNK)].astype(jnp.bfloat16)
        cell[...] = c0_ref[...]
        copy.wait()

    keep = keep_ref[0][:, :1]
    keep_b = keep.astype(jnp.bfloat16)

    def early(u):
        for q in range(4):
            cols = pl.ds(q * units + u * CHUNK, CHUNK)
            acc[q, u] = jnp.dot(
                emb_ref[0], w_ref[hidden:, cols], preferred_element_type=jnp.float32
            ) + jnp.dot(kown[...], w_ref[pl.ds(own0, units), cols], preferred_element_type=jnp.float32)

    def late(u):
        pre = []
        for q in range(4):
            cols = pl.ds(q * units + u * CHUNK, CHUNK)
            pre.append(
                acc[q, u]
                + jnp.dot(kpar[...], w_ref[pl.ds(par0, units), cols], preferred_element_type=jnp.float32)
            )
        span = pl.ds(u * CHUNK, CHUNK)
        gate_in, gate_forget, gate_cell, gate_out = (
            sigmoid(pre[0]),
            sigmoid(pre[1]),
            jnp.tanh(pre[2]),
            sigmoid(pre[3]),
        )
        kept_cell = cell[:, span] * keep
        cell_next = gate_forget * kept_cell + gate_in * gate_cell
        hown[nxt, u] = (gate_out * jnp.tanh(cell_next)).astype(jnp.bfloat16)
        cell[:, span] = cell_next
        gates_ref[0, 0, :, span] = gate_in
        gates_ref[0, 1, :, span] = gate_forget
        gates_ref[0, 2, :, span] = gate_cell
        gates_ref[0, 3, :, span] = gate_out
        cell_ref[0, :, span] = cell_next
        ckept_ref[0, :, span] = kept_cell
        exchange(nxt, u).start()

    @pl.when(t < steps)
    def _():
        for u in range(chunks):
            kown[:, pl.ds(u * CHUNK, CHUNK)] = hown[slot, u] * keep_b
        early(0)
        early(1)

    @pl.when(t > 0)
    def _():
        for u in range(chunks):
            exchange(slot, u).wait()

    for u in range(chunks):
        hid_ref[0, :, pl.ds(pl.multiple_of(own0 + u * CHUNK, CHUNK), CHUNK)] = hown[slot, u]
        hid_ref[0, :, pl.ds(pl.multiple_of(par0 + u * CHUNK, CHUNK), CHUNK)] = hpar[slot, u]

    @pl.when(t < steps)
    def _():
        for u in range(chunks):
            kpar[:, pl.ds(u * CHUNK, CHUNK)] = hpar[slot, u] * keep_b
        kept_ref[0, :, pl.ds(own0, units)] = kown[...]
        kept_ref[0, :, pl.ds(par0, units)] = kpar[...]
        for u in range(chunks):
            late(u)
            if u + 2 < chunks:
                early(u + 2)


def run_forward(embedded, keep, h0, c0, weights):
    steps, rows, depth = embedded.shape
    units = c0.shape[1]
    hidden = 2 * units
    chunks = units // CHUNK

    def at(t):
        return jnp.minimum(t, steps - 1)

    whole = pl.BlockSpec(memory_space=pltpu.VMEM)
    return pl.pallas_call(
        functools.partial(forward_kernel, steps),
        grid=(steps + 1,),
        in_specs=[
            pl.BlockSpec((1, rows, depth), lambda t: (at(t), 0, 0)),
            pl.BlockSpec((1, rows, 128), lambda t: (at(t), 0, 0)),
            whole,
            whole,
            pl.BlockSpec(memory_space=pl.ANY),
        ],
        out_specs=[
            pl.BlockSpec((1, rows, hidden), lambda t: (jnp.maximum(t - 1, 0), 0, 0)),
            pl.BlockSpec((1, rows, hidden), lambda t: (at(t), 0, 0)),
            pl.BlockSpec((1, 4, rows, units), lambda t: (at(t), 0, 0, 0)),
            pl.BlockSpec((1, rows, units), lambda t: (at(t), 0, 0)),
            pl.BlockSpec((1, rows, units), lambda t: (at(t), 0, 0)),
        ],
        out_shape=[
            jax.ShapeDtypeStruct((steps, rows, hidden), jnp.bfloat16),
            jax.ShapeDtypeStruct((steps, rows, hidden), jnp.bfloat16),
            jax.ShapeDtypeStruct((steps, 4, rows, units), jnp.float32),
            jax.ShapeDtypeStruct((steps, rows, units), jnp.float32),
            jax.ShapeDtypeStruct((steps, rows, units), jnp.float32),
        ],
        scratch_shapes=[
            pltpu.VMEM(weights.shape, jnp.bfloat16),
            pltpu.VMEM((2, chunks, rows, CHUNK), jnp.bfloat16),
            pltpu.VMEM((2, chunks, rows, CHUNK), jnp.bfloat16),
            pltpu.VMEM((rows, units), jnp.bfloat16),
            pltpu.VMEM((rows, units), jnp.bfloat16),
            pltpu.VMEM((rows, units), jnp.float32),
            pltpu.VMEM((4, chunks, rows, CHUNK), jnp.float32),
            pltpu.SemaphoreType.DMA,
            pltpu.SemaphoreType.DMA((2, chunks)),
            pltpu.SemaphoreType.DMA((2, chunks)),
        ],
        compiler_params=pltpu.CompilerParams(
            collective_id=1, has_side_effects=True, vmem_limit_bytes=56 << 20
        ),
        cost_estimate=pl.CostEstimate(
            flops=2 * steps * rows * weights.shape[0] * weights.shape[1],
            bytes_accessed=500 << 20,
            transcendentals=0,
        ),
    )(embedded, keep, h0, c0, weights)


def backward_kernel(
    steps,
    outg_ref,
    gates_ref,
    cell_ref,
    ckept_ref,
    keep_ref,
    w_hbm,
    pre_ref,
    gh_ref,
    gc_ref,
    w_ref,
    dh,
    dc,
    pg,
    outbox,
    inbox,
    w_sem,
    send_sem,
    recv_sem,
    swap_send,
    swap_recv,
    swapped,
):
    i = pl.program_id(0)
    slot = lax.rem(i, 2)
    core, peer = core_peer()
    units = dh.shape[1]
    chunks = units // CHUNK
    own0 = pl.multiple_of(core * units, units)
    par0 = pl.multiple_of((1 - core) * units, units)

    def exchange(which, u):
        return pltpu.make_async_remote_copy(
            src_ref=outbox.at[which, u],
            dst_ref=inbox.at[which, u],
            send_sem=send_sem.at[which, u],
            recv_sem=recv_sem.at[which, u],
            device_id=peer,
            device_id_type=MESH,
        )

    @pl.when(i == 0)
    def _():
        copy = pltpu.make_async_copy(w_hbm, w_ref, w_sem)
        copy.start()
        greet([peer])
        dh[...] = jnp.zeros_like(dh)
        dc[...] = jnp.zeros_like(dc)
        copy.wait()

    @pl.when(i > 0)
    def _():
        for u in range(chunks):
            exchange(1 - slot, u).wait()
        for u in range(chunks):
            span = pl.ds(u * CHUNK, CHUNK)
            dh[:, span] = dh[:, span] + inbox[1 - slot, u]

    keep = keep_ref[0][:, :1]
    block = 4 * CHUNK
    for u in range(chunks):
        span = pl.ds(u * CHUNK, CHUNK)
        gate_in = gates_ref[0, 0, :, span]
        gate_forget = gates_ref[0, 1, :, span]
        gate_cell = gates_ref[0, 2, :, span]
        gate_out = gates_ref[0, 3, :, span]
        total_hidden = dh[:, span] + outg_ref[0, :, span]
        tanh_cell = jnp.tanh(cell_ref[0, :, span])
        total_cell = dc[:, span] + total_hidden * gate_out * (1.0 - tanh_cell * tanh_cell)
        grads = [
            total_cell * gate_cell * gate_in * (1.0 - gate_in),
            total_cell * ckept_ref[0, :, span] * gate_forget * (1.0 - gate_forget),
            total_cell * gate_in * (1.0 - gate_cell * gate_cell),
            total_hidden * tanh_cell * gate_out * (1.0 - gate_out),
        ]
        for q in range(4):
            grad = grads[q].astype(jnp.bfloat16)
            pg[:, pl.ds(u * block + q * CHUNK, CHUNK)] = grad
            pre_ref[0, :, pl.ds(q * units + u * CHUNK, CHUNK)] = grad
        dc[:, span] = total_cell * gate_forget * keep
        part = pl.ds(u * block, block)
        for n in range(chunks):
            cols = pl.ds(pl.multiple_of(par0 + n * CHUNK, CHUNK), CHUNK)
            product = jnp.dot(pg[:, part], w_ref[part, cols], preferred_element_type=jnp.float32)
            outbox[slot, n] = product if u == 0 else outbox[slot, n] + product
    for n in range(chunks):
        outbox[slot, n] = outbox[slot, n] * keep
        exchange(slot, n).start()
    for u in range(chunks):
        cols = pl.ds(pl.multiple_of(own0 + u * CHUNK, CHUNK), CHUNK)
        dh[:, pl.ds(u * CHUNK, CHUNK)] = (
            jnp.dot(pg[...], w_ref[:, cols], preferred_element_type=jnp.float32) * keep
        )

    @pl.when(i == steps - 1)
    def _():
        for u in range(chunks):
            exchange(slot, u).wait()
        for u in range(chunks):
            span = pl.ds(u * CHUNK, CHUNK)
            dh[:, span] = dh[:, span] + inbox[slot, u]
        seg = gh_ref.shape[0]
        rows_own = pl.ds(pl.multiple_of(core * seg, 8), seg)
        rows_par = pl.ds(pl.multiple_of((1 - core) * seg, 8), seg)
        swaps = []
        for k, (held, result) in enumerate(((dh, gh_ref), (dc, gc_ref))):
            swaps.append(
                pltpu.make_async_remote_copy(
                    src_ref=held.at[rows_par],
                    dst_ref=swapped.at[k],
                    send_sem=swap_send.at[k],
                    recv_sem=swap_recv.at[k],
                    device_id=peer,
                    device_id_type=MESH,
                )
            )
            swaps[k].start()
            result[:, pl.ds(own0, units)] = held[rows_own]
        for k, result in enumerate((gh_ref, gc_ref)):
            swaps[k].wait()
            result[:, pl.ds(par0, units)] = swapped[k]


def run_backward(out_grad, gates, cells, cells_kept, keep, weights_t):
    steps, rows, units = out_grad.shape
    chunks = units // CHUNK

    def back(i):
        return (steps - 1 - i, 0, 0)

    row_block = pl.BlockSpec((1, rows, units), back)
    whole = pl.BlockSpec(memory_space=pltpu.VMEM)
    return pl.pallas_call(
        functools.partial(backward_kernel, steps),
        grid=(steps,),
        in_specs=[
            row_block,
            pl.BlockSpec((1, 4, rows, units), lambda i: (steps - 1 - i, 0, 0, 0)),
            row_block,
            row_block,
            pl.BlockSpec((1, rows, 128), back),
            pl.BlockSpec(memory_space=pl.ANY),
        ],
        out_specs=[pl.BlockSpec((1, rows, 4 * units), back), whole, whole],
        out_shape=[
            jax.ShapeDtypeStruct((steps, rows, 4 * units), jnp.bfloat16),
            jax.ShapeDtypeStruct((rows // 2, 2 * units), jnp.float32),
            jax.ShapeDtypeStruct((rows // 2, 2 * units), jnp.float32),
        ],
        scratch_shapes=[
            pltpu.VMEM(weights_t.shape, jnp.bfloat16),
            pltpu.VMEM((rows, units), jnp.float32),
            pltpu.VMEM((rows, units), jnp.float32),
            pltpu.VMEM((rows, 4 * units), jnp.bfloat16),
            pltpu.VMEM((2, chunks, rows, CHUNK), jnp.float32),
            pltpu.VMEM((2, chunks, rows, CHUNK), jnp.float32),
            pltpu.SemaphoreType.DMA,
            pltpu.SemaphoreType.DMA((2, chunks)),
            pltpu.SemaphoreType.DMA((2, chunks)),
            pltpu.SemaphoreType.DMA((2,)),
            pltpu.SemaphoreType.DMA((2,)),
            pltpu.VMEM((2, rows // 2, units), jnp.float32),
        ],
        compiler_params=pltpu.CompilerParams(
            collective_id=2, has_side_effects=True, vmem_limit_bytes=56 << 20
        ),
        cost_estimate=pl.CostEstimate(
            flops=2 * steps * rows * weights_t.shape[0] * weights_t.shape[1],
            bytes_accessed=500 << 20,
            transcendentals=0,
        ),
    )(out_grad, gates, cells, cells_kept, keep, weights_t)


def reduce_kernel(
    chips,
    depth,
    embed,
    kept_ref,
    aug_ref,
    pre_ref,
    in_ref,
    chars_ref,
    extra_ref,
    dec_ref,
    rec_hbm,
    inout_ref,
    emb_ref,
    clip_ref,
    turned,
    fetched,
    fetch_sem,
    inbox,
    outbox,
    partial,
    final,
    in_all,
    in_box,
    in_final,
    in_swap,
    emb_box,
    emb_mine,
    emb_part,
    emb_final,
    ssq,
    norm_box,
    y_send,
    y_recv,
    part_recv,
    final_recv,
    part_send,
    final_send,
    write_sem,
    in_send,
    in_recv,
    emb_send,
    emb_recv,
    misc_recv,
    misc_send,
    norm_send,
    norm_recv,
):
    model = lax.axis_index("dir")
    group = lax.axis_index("group")
    z = lax.axis_index("dp")
    core = lax.rem(group, 2)
    chip = group // 2
    peers = 2 * chips
    middle = depth // 2
    rows_out = kept_ref.shape[1] // peers
    wide = pre_ref.shape[1]
    tall = turned.shape[0]
    lot = tall // 16
    batches = rows_out // tall
    groups = rows_out // 16
    per_pass = lot // peers
    upper = depth - 1 > middle
    is_middle = z == middle
    low = z < middle
    has_away = jnp.logical_or(jnp.logical_and(low, z > 0), jnp.logical_and(z > middle, z < depth - 1))
    toward = jnp.where(low, z + 1, jnp.maximum(z - 1, 0))
    away = jnp.where(low, jnp.maximum(z - 1, 0), jnp.minimum(z + 1, depth - 1))

    def in_group(index):
        return (model, index, z)

    def in_line(index):
        return (model, group, index)

    def owner_of(slot):
        if slot == 0:
            return group
        if slot == 1:
            return group + 1 - 2 * core
        step = (slot - 2) // 2 + 1
        side = core if slot % 2 == 0 else 1 - core
        return 2 * lax.rem(chip + step, chips) + side

    def slot_there(slot):
        if slot == 1:
            return 1
        step = (slot - 2) // 2 + 1
        return 2 + 2 * (chips - step - 1) + slot % 2

    order = list(range(2, peers)) + [1, 0]
    barrier = pltpu.get_barrier_semaphore()
    for slot in range(1, peers):
        pl.semaphore_signal(barrier, inc=1, device_id=in_group(owner_of(slot)), device_id_type=MESH)

    @pl.when(z > 0)
    def _():
        pl.semaphore_signal(
            barrier, inc=1, device_id=in_line(jnp.maximum(z - 1, 0)), device_id_type=MESH
        )

    @pl.when(z < depth - 1)
    def _():
        pl.semaphore_signal(
            barrier, inc=1, device_id=in_line(jnp.minimum(z + 1, depth - 1)), device_id_type=MESH
        )

    pl.semaphore_wait(
        barrier,
        peers - 1 + jnp.where(z > 0, 1, 0) + jnp.where(z < depth - 1, 1, 0),
    )
    ssq[...] = jnp.zeros_like(ssq)

    def remote(src, dst, send, recv, device):
        return pltpu.make_async_remote_copy(
            src_ref=src,
            dst_ref=dst,
            send_sem=send,
            recv_sem=recv,
            device_id=device,
            device_id_type=MESH,
        )

    def squares(value):
        square = value * value
        total = square[:, :128]
        for lane in range(128, value.shape[1], 128):
            total = total + square[:, lane : lane + 128]
        rows = total[:16]
        for row in range(16, value.shape[0], 16):
            rows = rows + total[row : row + 16]
        ssq[...] = ssq[...] + rows

    def send_partial(mine, part, fin, sems):
        @pl.when(jnp.logical_not(is_middle))
        def _():
            @pl.when(has_away)
            def _():
                remote(mine, part, sems["ps"], sems["pr"], in_line(away)).wait_recv()
                mine[...] = (
                    mine[...].astype(jnp.float32) + part[...].astype(jnp.float32)
                ).astype(mine.dtype)

            if upper:

                @pl.when(z == middle + 1)
                def _():
                    remote(mine, fin, sems["ps"], sems["fr"], in_line(toward)).start()

            @pl.when(z != middle + 1)
            def _():
                remote(mine, part, sems["ps"], sems["pr"], in_line(toward)).start()

        @pl.when(is_middle)
        def _():
            remote(mine, part, sems["ps"], sems["pr"], in_line(toward)).wait_recv()
            total = mine[...].astype(jnp.float32) + part[...].astype(jnp.float32)
            if upper:
                remote(mine, fin, sems["ps"], sems["fr"], in_line(toward)).wait_recv()
                total = total + fin[...].astype(jnp.float32)
            fin[...] = total.astype(fin.dtype)
            remote(fin, fin, sems["f0"], sems["fr"], in_line(middle - 1)).start()
            if upper:
                remote(fin, fin, sems["f1"], sems["fr"], in_line(middle + 1)).start()

    def pass_final(fin, sems):
        @pl.when(jnp.logical_not(is_middle))
        def _():
            remote(fin, fin, sems["f0"], sems["fr"], in_line(toward)).wait_recv()

            @pl.when(has_away)
            def _():
                remote(fin, fin, sems["f0"], sems["fr"], in_line(away)).start()

    def wait_line(mine, fin, sems):
        @pl.when(is_middle)
        def _():
            remote(fin, fin, sems["f0"], sems["fr"], in_line(toward)).wait_send()
            if upper:
                remote(fin, fin, sems["f1"], sems["fr"], in_line(toward)).wait_send()

        @pl.when(jnp.logical_not(is_middle))
        def _():
            remote(mine, fin, sems["ps"], sems["fr"], in_line(toward)).wait_send()

            @pl.when(has_away)
            def _():
                remote(fin, fin, sems["f0"], sems["fr"], in_line(away)).wait_send()

    def line_sems(unit):
        return {
            "pr": part_recv.at[unit],
            "fr": final_recv.at[unit],
            "ps": part_send.at[unit],
            "f0": final_send.at[0, unit],
            "f1": final_send.at[1, unit],
        }

    extra_rows = 4 // chips
    emb_sems = line_sems(2 * (groups + extra_rows))

    def send_block(slot, parity, index, row):
        return remote(
            outbox.at[slot - 1, parity, index],
            inbox.at[slot_there(slot), row],
            y_send.at[slot - 1, parity, index],
            y_recv.at[slot_there(slot) - 1, row],
            in_group(owner_of(slot)),
        )

    span = 1024

    def product(dest):
        def columns(j, carry):
            cols = pl.ds(pl.multiple_of(j * span, span), span)
            dest[:, :, cols] = (
                jnp.dot(turned[...], pre_ref[:, cols], preferred_element_type=jnp.float32)
                .astype(jnp.bfloat16)
                .reshape(lot, 16, span)
            )
            return carry

        lax.fori_loop(0, wide // span, columns, 0)

    def fetch(turn, b):
        start = owner_of(order[turn]) * rows_out + b * tall
        return pltpu.make_async_copy(
            kept_ref.at[:, pl.ds(pl.multiple_of(start, tall), tall)],
            fetched.at[turn % 2],
            fetch_sem.at[turn % 2],
        )

    def block(turn, b, parity):
        slot = order[turn]
        if turn + 1 < peers:
            fetch(turn + 1, b).start()
        else:

            @pl.when(b + 1 < batches)
            def _():
                fetch(0, b + 1).start()

        fetch(turn, b).wait()
        turned[...] = jnp.transpose(fetched[turn % 2])
        if slot == 0:
            product(inbox.at[0, pl.ds(b * lot, lot)])
        else:

            @pl.when(b >= 2)
            def _():
                for index in range(lot):
                    send_block(slot, parity, index, 0).wait_send()

            product(outbox.at[slot - 1, parity])

    def send(row):
        parity, index = lax.rem(row // lot, 2), lax.rem(row, lot)
        if chips > 1:

            @pl.when(row > 0)
            def _():
                send_block(2, parity, index, row).start()

        for slot in list(range(3, peers)) + [1]:
            send_block(slot, parity, index, row).start()

    def take(row):
        @pl.when(row < groups)
        def _():
            for slot in range(1, peers):
                remote(
                    outbox.at[slot - 1, 0, 0],
                    inbox.at[slot, row],
                    y_send.at[slot - 1, 0, 0],
                    y_recv.at[slot - 1, row],
                    in_group(owner_of(slot)),
                ).wait_recv()
            if chips > 1:
                for part in range(2):
                    total = inbox[part, row].astype(jnp.float32)
                    for slot in range(2 + part, peers, 2):
                        total = total + inbox[slot, row].astype(jnp.float32)
                    inbox[part, row] = total.astype(jnp.bfloat16)

        @pl.when(row == groups)
        def _():
            for step in range(1, chips):
                in_copy(step).wait_recv()

        @pl.when(row >= groups)
        def _():
            for part in range(2):
                for k in range(chips):
                    first = (2 * (row - groups) + part) * chips + k
                    at = pl.ds(pl.multiple_of(first * 16, 16), 16)
                    total = in_all[at, in_columns(chip)].astype(jnp.float32)
                    for step in range(1, chips):
                        total = total + in_box[step - 1, at].astype(jnp.float32)
                    inbox[part, row, :, pl.ds(k * in_wide, in_wide)] = total.astype(jnp.bfloat16)

        for part in range(2):
            send_partial(
                inbox.at[part, row],
                partial.at[2 * row + part],
                final.at[2 * row + part],
                line_sems(2 * row + part),
            )

    def write_out(row, part):
        side = core if part == 0 else 1 - core
        return pltpu.make_async_copy(
            final.at[2 * row + part],
            rec_hbm.at[side, pl.ds(pl.multiple_of(row * 16, 16), 16)],
            write_sem.at[2 * row + part],
        )

    def finish(row):
        for part in range(2):
            pass_final(final.at[2 * row + part], line_sems(2 * row + part))

            @pl.when(row < groups)
            def _():
                write_out(row, part).start()

            squares(final[2 * row + part].astype(jnp.float32))

    def settle(row):
        for part in range(2):
            wait_line(inbox.at[part, row], final.at[2 * row + part], line_sems(2 * row + part))

            @pl.when(row < groups)
            def _():
                write_out(row, part).wait()

    in_wide = wide // chips

    def in_columns(index):
        return pl.ds(pl.multiple_of(index * in_wide, in_wide), in_wide)

    def in_copy(step):
        there = lax.rem(chip + step, chips)
        return remote(
            in_all.at[:, in_columns(there)],
            in_box.at[chips - step - 1],
            in_send.at[step - 1],
            in_recv.at[chips - step - 1],
            in_group(2 * there + core),
        )

    def emb_copy(slot, source):
        return remote(
            emb_mine,
            emb_box.at[source],
            emb_send.at[slot - 1],
            emb_recv.at[source],
            in_group(owner_of(slot)),
        )

    def small_products():
        turned[...] = jnp.transpose(aug_ref[...])

        def columns(j, carry):
            cols = pl.ds(pl.multiple_of(j * span, span), span)
            in_all[:, cols] = jnp.dot(
                turned[...], pre_ref[:, cols], preferred_element_type=jnp.float32
            ).astype(jnp.bfloat16)
            return carry

        lax.fori_loop(0, wide // span, columns, 0)
        into = lax.dot_general(
            pre_ref[...], in_ref[...], (((1,), (1,)), ((), ())), preferred_element_type=jnp.float32
        ).astype(jnp.bfloat16)
        vocab_rows = emb_mine.shape[0]
        ids = lax.broadcasted_iota(jnp.int32, (vocab_rows, chars_ref.shape[1]), 0)
        onehot = jnp.where(chars_ref[...] == ids, 1.0, 0.0).astype(jnp.bfloat16)
        summed = jnp.dot(onehot, into, preferred_element_type=jnp.float32)
        lanes = lax.broadcasted_iota(jnp.int32, summed.shape, 1)
        emb_mine[...] = jnp.where(lanes < embed, summed, 0.0) + extra_ref[...]

    def send_in():
        for step in range(1, chips):
            in_copy(step).start()

    def send_emb():
        for slot in range(1, peers):
            emb_copy(slot, group).start()

    def take_emb():
        for slot in range(1, peers):
            emb_copy(slot, owner_of(slot)).wait_recv()
        for slot in range(1, peers):
            emb_copy(slot, group).wait_send()
        emb_box[group] = emb_mine[...]
        total = emb_box[0]
        for source in range(1, peers):
            total = total + emb_box[source]
        emb_mine[...] = total
        send_partial(emb_mine, emb_part, emb_final, emb_sems)

    lead = (peers - 2) * per_pass
    y_lag, hop_lag, settle_lag = 3, 1, 6
    hops = jnp.where(low, middle - z, z - middle)
    most_hops = max(middle, depth - 1 - middle)
    before = groups // 2
    places = groups + extra_rows + 1
    steps = places + y_lag + hop_lag * most_hops + settle_lag + lead
    rounds = -(-steps // lot)

    def row_at(place):
        is_in = jnp.logical_and(place >= before, place < before + extra_rows)
        return jnp.where(
            is_in,
            groups + place - before,
            jnp.where(place < before, place, place - extra_rows - 1),
        )

    def visit(place, rows, emb):
        is_emb = place == before + extra_rows
        inside = jnp.logical_and(place >= 0, place < places)

        @pl.when(jnp.logical_and(inside, jnp.logical_not(is_emb)))
        def _():
            rows(row_at(place))

        @pl.when(is_emb)
        def _():
            emb()

    def send_any(row):
        @pl.when(row < groups)
        def _():
            send(row)

        @pl.when(row == groups)
        def _():
            send_in()

    def round_of(b, carry):
        parity = lax.rem(b, 2)

        @pl.when(b == 1)
        def _():
            small_products()

        for turn in range(peers):

            @pl.when(b < batches)
            def _():
                block(turn, b, parity)

            if turn == 0 and chips > 1:

                @pl.when(b == 0)
                def _():
                    send_block(2, 0, 0, 0).start()

            def step(j, inner):
                sent = b * lot + turn * per_pass + j - lead
                arrived = sent - y_lag
                summed = arrived - hop_lag * hops
                visit(sent, send_any, send_emb)
                visit(arrived, take, take_emb)
                visit(summed, finish, lambda: pass_final(emb_final, emb_sems))
                visit(
                    summed - settle_lag,
                    settle,
                    lambda: wait_line(emb_mine, emb_final, emb_sems),
                )
                return inner

            lax.fori_loop(0, per_pass, step, 0)

        return carry

    fetch(0, 0).start()
    lax.fori_loop(0, rounds, round_of, 0)
    for u in range(2 * extra_rows):
        for k in range(chips):
            first = (u * chips + k) * 16
            in_final[first : first + 16] = final[
                2 * groups + u, :, k * in_wide : (k + 1) * in_wide
            ]

    keep_cols = in_wide // 2
    if in_wide > wide // 4:
        mine = pl.ds(pl.multiple_of(core * keep_cols, keep_cols), keep_cols)
        theirs = pl.ds(pl.multiple_of((1 - core) * keep_cols, keep_cols), keep_cols)
        swap = remote(
            in_final.at[:, theirs], in_swap, misc_send, misc_recv, in_group(owner_of(1))
        )
        swap.start()
        swap.wait()
        inout_ref[:, mine] = in_final[:, mine]
        inout_ref[:, theirs] = in_swap[...]
    else:
        inout_ref[...] = in_final[...]
    emb_ref[...] = emb_final[...]

    squares(dec_ref[...].astype(jnp.float32))
    norm_box[group] = ssq[...]

    def norm_copy(slot, source):
        return remote(
            ssq,
            norm_box.at[source],
            norm_send.at[slot - 1],
            norm_recv.at[source],
            in_group(owner_of(slot)),
        )

    for slot in range(1, peers):
        norm_copy(slot, group).start()
    for slot in range(1, peers):
        norm_copy(slot, owner_of(slot)).wait_recv()
    for slot in range(1, peers):
        norm_copy(slot, group).wait_send()
    total = norm_box[0]
    for source in range(1, peers):
        total = total + norm_box[source]
    lanes = lax.broadcasted_iota(jnp.int32, emb_final.shape, 1)
    small = jnp.where(lanes <= embed, emb_final[...], 0.0)
    total_sq = jnp.sum(total) + jnp.sum(small * small)
    clip_ref[...] = jnp.full(clip_ref.shape, 0.25, jnp.float32) / jnp.maximum(
        jnp.sqrt(jnp.full(clip_ref.shape, total_sq, jnp.float32)), 0.25
    )

    for step in range(1, chips):
        in_copy(step).wait_send()
    for slot in range(1, peers):
        for parity in range(min(2, batches)):
            for index in range(lot):
                send_block(slot, parity, index, 0).wait_send()


def run_reduce(chips, depth, embed, kept, aug, pre, in_own, chars, extra, dec_sum):
    hidden = kept.shape[1]
    count, wide = pre.shape
    peers = 2 * chips
    rows_out = hidden // peers
    tall = 128
    lot = tall // 16
    groups = rows_out // 16
    extra_rows = 4 // chips
    units = 2 * (groups + extra_rows)
    in_rows = aug.shape[1]
    in_wide = wide // chips
    in_cols = 2 * wide // peers
    vmem = pl.BlockSpec(memory_space=pltpu.VMEM)
    bf16, f32 = jnp.bfloat16, jnp.float32
    small = extra.shape
    dma = pltpu.SemaphoreType.DMA
    return pl.pallas_call(
        functools.partial(reduce_kernel, chips, depth, embed),
        in_specs=[pl.BlockSpec(memory_space=pl.ANY)] + [vmem] * 6,
        out_specs=[pl.BlockSpec(memory_space=pl.ANY), vmem, vmem, vmem],
        out_shape=[
            jax.ShapeDtypeStruct((2, rows_out, wide), bf16),
            jax.ShapeDtypeStruct((in_rows, in_cols), bf16),
            jax.ShapeDtypeStruct(small, f32),
            jax.ShapeDtypeStruct((8, 128), f32),
        ],
        scratch_shapes=[
            pltpu.VMEM((tall, count), bf16),
            pltpu.VMEM((2, count, tall), bf16),
            dma((2,)),
            pltpu.VMEM((peers, groups + extra_rows, 16, wide), bf16),
            pltpu.VMEM((peers - 1, 2, lot, 16, wide), bf16),
            pltpu.VMEM((units, 16, wide), bf16),
            pltpu.VMEM((units, 16, wide), bf16),
            pltpu.VMEM((in_rows, wide), bf16),
            pltpu.VMEM((max(chips - 1, 1), in_rows, in_wide), bf16),
            pltpu.VMEM((in_rows, in_wide), bf16),
            pltpu.VMEM((in_rows, in_wide // 2), bf16),
            pltpu.VMEM((peers,) + small, f32),
            pltpu.VMEM(small, f32),
            pltpu.VMEM(small, f32),
            pltpu.VMEM(small, f32),
            pltpu.VMEM((16, 128), f32),
            pltpu.VMEM((peers, 16, 128), f32),
            dma((peers - 1, 2, lot)),
            dma((peers - 1, groups)),
            dma((units + 1,)),
            dma((units + 1,)),
            dma((units + 1,)),
            dma((2, units + 1)),
            dma((units,)),
            dma((max(chips - 1, 1),)),
            dma((max(chips - 1, 1),)),
            dma((peers - 1,)),
            dma((peers,)),
            dma,
            dma,
            dma((peers - 1,)),
            dma((peers,)),
        ],
        compiler_params=pltpu.CompilerParams(
            collective_id=3, has_side_effects=True, vmem_limit_bytes=60 << 20
        ),
        cost_estimate=pl.CostEstimate(
            flops=2 * count * hidden * wide, bytes_accessed=700 << 20, transcendentals=0
        ),
    )(kept, aug, pre, in_own, chars, extra, dec_sum)


def middle_kernel(
    vocab,
    seg_len,
    out_ref,
    target_ref,
    dec_ref,
    bias_ref,
    slot_row_ref,
    slot_col_ref,
    wg_ref,
    outg_ref,
    decg_ref,
    stat_ref,
    picked_ref,
    dec_acc,
    pick_acc,
):
    i = pl.program_id(0)
    last = pl.num_programs(0) - 1
    core = lax.rem(lax.axis_index("group"), 2)
    span, pair, hidden = out_ref.shape
    count = span * pair
    units = hidden // 2
    seg = pair // 2
    slots = wg_ref.shape[0] // pair
    wide = dec_ref.shape[1]
    bf16, f32, i32 = jnp.bfloat16, jnp.float32, jnp.int32
    out = out_ref[...].reshape(count, hidden)

    @pl.when(i == 0)
    def _():
        dec_acc[...] = jnp.zeros_like(dec_acc)
        pick_acc[...] = jnp.zeros_like(pick_acc)
        stat_ref[...] = jnp.zeros_like(stat_ref)

    logits = jnp.dot(out, dec_ref[...], preferred_element_type=f32) + bias_ref[...]
    top = jnp.max(logits, axis=1, keepdims=True)
    powers = jnp.exp(logits - top)
    total = jnp.sum(powers, axis=1, keepdims=True)
    lanes = lax.broadcasted_iota(i32, (count, wide), 1)
    hit = lanes == target_ref[...]
    rows = lax.broadcasted_iota(i32, (count, 1), 0)
    segment = lax.rem(rows, pair)
    mine = jnp.logical_and(segment >= core * seg, segment < (core + 1) * seg)
    loss = top + jnp.log(total) - jnp.sum(jnp.where(hit, logits, 0.0), axis=1, keepdims=True)
    loss = jnp.sum(jnp.where(mine, loss, 0.0))
    grad = (powers / total - jnp.where(hit, 1.0, 0.0)) * (1.0 / seg_len)
    grad_b = grad.astype(bf16)
    own_b = jnp.where(mine, grad_b.astype(f32), 0.0)
    stat_ref[0:1] += jnp.sum(own_b, axis=0, keepdims=True)
    stat_ref[1:2] += jnp.full((1, wide), loss, f32)
    dec_acc[...] += jnp.dot(
        jnp.transpose(own_b.astype(bf16)), out, preferred_element_type=f32
    )

    step = rows // pair + i * span
    slot_count = wg_ref.shape[0]
    col = lax.broadcasted_iota(i32, (count, slot_count), 1)
    at_word = jnp.logical_and(slot_row_ref[...] == step, col // slots == segment)
    words = jnp.where(at_word, 1.0, 0.0).astype(bf16)
    half = pl.ds(pl.multiple_of(core * units, units), units)
    outg_ref[...] = lax.dot_general(
        grad_b, dec_ref[half], (((1,), (1,)), ((), ())), preferred_element_type=f32
    ) + jnp.dot(words, wg_ref[...], preferred_element_type=f32)

    own_slots = seg * slots
    across = lax.broadcasted_iota(i32, (own_slots, count), 1)
    slot_segment = lax.broadcasted_iota(i32, (own_slots, 1), 0) // slots + core * seg
    picks = jnp.logical_and(
        slot_col_ref[...] == across // pair + i * span, lax.rem(across, pair) == slot_segment
    )
    pick_acc[...] += jnp.dot(
        jnp.where(picks, 1.0, 0.0).astype(bf16), out, preferred_element_type=f32
    )

    @pl.when(i == last)
    def _():
        decg_ref[...] = dec_acc[: decg_ref.shape[0]].astype(bf16)
        picked_ref[...] = pick_acc[...].astype(bf16)


def run_middle(vocab, out_all, targets, decoder, bias, slot_row, slot_col, wg_pair):
    steps, pair, hidden = out_all.shape
    span = 4 if steps % 4 == 0 else 1
    count = span * pair
    units = hidden // 2
    wide = decoder.shape[1]
    vocab_rows = -(-vocab // 32) * 32
    own_slots = slot_col.shape[0]
    bf16, f32 = jnp.bfloat16, jnp.float32

    def fixed(shape):
        return pl.BlockSpec(shape, lambda i: (0,) * len(shape))

    return pl.pallas_call(
        functools.partial(middle_kernel, vocab, steps),
        grid=(steps // span,),
        in_specs=[
            pl.BlockSpec((span, pair, hidden), lambda i: (i, 0, 0)),
            pl.BlockSpec((count, 1), lambda i: (i, 0)),
            fixed(decoder.shape),
            fixed(bias.shape),
            fixed(slot_row.shape),
            fixed(slot_col.shape),
            fixed(wg_pair.shape),
        ],
        out_specs=[
            pl.BlockSpec((count, units), lambda i: (i, 0)),
            fixed((vocab_rows, hidden)),
            fixed((8, wide)),
            fixed((own_slots, hidden)),
        ],
        out_shape=[
            jax.ShapeDtypeStruct((steps * pair, units), f32),
            jax.ShapeDtypeStruct((vocab_rows, hidden), bf16),
            jax.ShapeDtypeStruct((8, wide), f32),
            jax.ShapeDtypeStruct((own_slots, hidden), bf16),
        ],
        scratch_shapes=[
            pltpu.VMEM((wide, hidden), f32),
            pltpu.VMEM((own_slots, hidden), f32),
        ],
        compiler_params=pltpu.CompilerParams(vmem_limit_bytes=48 << 20),
    )(out_all, targets, decoder, bias, slot_row, slot_col, wg_pair)


def update_kernel(
    count,
    clip_ref,
    sum_ref,
    moment_ref,
    in_ref,
    emb_ref,
    dec_ref,
    mom_in_ref,
    mom_bias_ref,
    mom_dec_ref,
    mom_emb_ref,
    mom_dbias_ref,
    grad_ref,
    next_ref,
    *small,
):
    clip = clip_ref[0, 0]
    gradient = sum_ref[0].astype(jnp.float32)
    grad_ref[0] = gradient
    next_ref[0] = momentum_step(moment_ref[0], gradient, clip)

    index = (pl.program_id(0) * pl.num_programs(1) + pl.program_id(1)) * pl.num_programs(2)
    index = index + pl.program_id(2)
    embed = mom_in_ref.shape[0]
    vocab = mom_emb_ref.shape[0]

    def turned():
        return jnp.transpose(emb_ref[...])

    results = [
        (lambda: in_ref[...].astype(jnp.float32)[:embed], mom_in_ref),
        (lambda: in_ref[...].astype(jnp.float32)[embed : embed + 1], mom_bias_ref),
        (lambda: dec_ref[...].astype(jnp.float32)[:vocab], mom_dec_ref),
        (lambda: emb_ref[:vocab, :embed], mom_emb_ref),
        (lambda: turned()[embed : embed + 1, :vocab], mom_dbias_ref),
    ]

    @pl.when(index == 0)
    def _():
        small[0][...] = turned()[embed + 1 : embed + 2, :128] / count

    def one(k, value_of, moment):
        @pl.when(index == k + 1)
        def _():
            value = value_of().reshape(moment.shape)
            small[1 + 2 * k][...] = value
            small[2 + 2 * k][...] = momentum_step(moment[...], value, clip)

    for k, (value_of, moment) in enumerate(results):
        one(k, value_of, moment)


def run_update(count, clip, sums, in_sum, emb_sum, dec_sum, moments):
    mom_rec, mom_in, mom_bias, mom_dec, mom_emb, mom_dbias = moments
    halves, rows, wide = sums.shape
    span = wide // 4
    tall = rows
    block = pl.BlockSpec((1, tall, span), lambda q, s, r: (0, r, 2 * q + s))
    f32 = jnp.float32

    def fixed(shape):
        return pl.BlockSpec(shape, lambda q, s, r: (0,) * len(shape))

    rec_shape = jax.ShapeDtypeStruct(mom_rec.shape, f32)
    small = [mom_in, mom_bias, mom_dec, mom_emb, mom_dbias]
    shapes = [(1, 128)]
    for moment in small:
        shapes += [moment.shape, moment.shape]
    return pl.pallas_call(
        functools.partial(update_kernel, count),
        grid=(4, 2, 1),
        in_specs=[
            pl.BlockSpec(memory_space=pltpu.SMEM),
            pl.BlockSpec((1, tall, span), lambda q, s, r: (s, r, q)),
            block,
        ]
        + [fixed(x.shape) for x in (in_sum, emb_sum, dec_sum, *small)],
        out_specs=[block, block] + [fixed(shape) for shape in shapes],
        out_shape=[rec_shape, rec_shape] + [jax.ShapeDtypeStruct(shape, f32) for shape in shapes],
        compiler_params=pltpu.CompilerParams(vmem_limit_bytes=56 << 20),
    )(clip, sums, mom_rec, in_sum, emb_sum, dec_sum, *small)


def shards(
    chars,
    targets,
    resets,
    word_pos,
    h_init,
    c_init,
    word_grad,
    w_emb,
    w_in,
    w_rec,
    b_rec,
    w_dec,
    b_dec,
    mom_emb,
    mom_in,
    mom_rec,
    mom_bias,
    mom_dec,
    mom_dbias,
):
    vocab_size = w_emb.shape[1]
    embed_size = w_emb.shape[2]
    seg_len = chars.shape[2]
    batch_size = chars.shape[1]
    hidden_size = w_rec.shape[2] // 4
    units = hidden_size // 2
    core = lax.rem(lax.axis_index("group"), 2)
    first = core == 0

    depth = 128
    vocab_lanes = -(-vocab_size // 128) * 128
    vocab_rows = -(-vocab_size // 32) * 32
    dec_own = jnp.pad(w_dec[0].astype(jnp.bfloat16), ((0, 0), (0, vocab_lanes - vocab_size)))
    dec_full = lax.all_gather(dec_own, "group", axis=0, tiled=True)
    in_bias = jnp.concatenate(
        [w_in[0], b_rec, jnp.zeros((depth - embed_size - 1, w_in.shape[2]), jnp.float32)]
    ).astype(jnp.bfloat16)
    word_slots = word_pos.shape[2]
    spare = -(3 * seg_len + word_slots) % 128
    ids = jnp.concatenate(
        [
            chars[0],
            targets[0],
            resets[0],
            word_pos[0],
            jnp.zeros((batch_size, spare), jnp.int32),
        ],
        axis=1,
    )
    weights, weights_t, h_pair, c_pair, wg_pair, packed, in_own = run_gather(
        lax.axis_size("group") // 2,
        lax.axis_size("dp"),
        w_rec[0],
        in_bias,
        h_init[0],
        c_init[0],
        word_grad.reshape(batch_size * word_slots, hidden_size),
        ids,
    )
    chars2 = packed[:, :seg_len]
    targets2 = packed[:, seg_len : 2 * seg_len]
    resets2 = packed[:, 2 * seg_len : 3 * seg_len]
    word_pos2 = packed[:, 3 * seg_len : 3 * seg_len + word_slots]
    char_major = jnp.transpose(chars2)
    char_onehot = (char_major[:, :, None] == jnp.arange(vocab_size, dtype=jnp.int32)).astype(
        jnp.bfloat16
    )
    embedded = jnp.einsum(
        "tbv,ve->tbe",
        char_onehot,
        w_emb[0].astype(jnp.bfloat16),
        preferred_element_type=jnp.float32,
    ).astype(jnp.bfloat16)
    pad_shape = (seg_len, 2 * batch_size, depth - embed_size - 1)
    embedded_one = jnp.concatenate(
        [
            embedded,
            jnp.ones((seg_len, 2 * batch_size, 1), jnp.bfloat16),
            jnp.zeros(pad_shape, jnp.bfloat16),
        ],
        axis=-1,
    )
    keep_major = jnp.broadcast_to(
        (1 - jnp.transpose(resets2)).astype(jnp.float32)[:, :, None],
        (seg_len, 2 * batch_size, 128),
    )
    out_all, kept_all, gate_all, cell_all, cellkept_all = run_forward(
        embedded_one, keep_major, h_pair, c_pair, weights
    )
    positions = seg_len * 2 * batch_size
    out_grad, dec_grad, stats, picked = run_middle(
        vocab_size,
        out_all,
        jnp.transpose(targets2).reshape(positions, 1),
        dec_full,
        jnp.pad(b_dec, ((0, 0), (0, vocab_lanes - vocab_size)), constant_values=-1e30),
        word_pos2.reshape(1, 2 * batch_size * word_slots),
        word_pos[0].reshape(batch_size * word_slots, 1),
        wg_pair,
    )
    dec_sum = lax.psum(dec_grad, ("group", "dp"))
    picked = picked.reshape(batch_size, word_slots, hidden_size)
    half_slots = picked.shape[1] // 2
    model_index = lax.axis_index("dir")
    own_slots = lax.dynamic_slice_in_dim(picked, model_index * half_slots, half_slots, 1)
    other_slots = lax.dynamic_slice_in_dim(picked, (1 - model_index) * half_slots, half_slots, 1)
    partner_half = partner(other_slots, "dir", 0)
    leading = model_index == 0
    word_vectors = jnp.where(
        leading,
        jnp.concatenate([own_slots, partner_half], axis=-1),
        jnp.concatenate([partner_half, own_slots], axis=-1),
    )
    pre_all, grad_hidden0, grad_cell0 = run_backward(
        out_grad.reshape(seg_len, 2 * batch_size, units), gate_all, cell_all, cellkept_all, keep_major, weights_t
    )

    rows_own = w_dec.shape[1]
    dec_sum = lax.dynamic_slice_in_dim(
        dec_sum, lax.axis_index("group") * rows_own, rows_own, 1
    )
    extra = jnp.concatenate(
        [
            jnp.zeros((vocab_rows, embed_size), jnp.float32),
            stats[0, :vocab_rows, None],
            jnp.broadcast_to(stats[1, 0], (vocab_rows, 1)),
            jnp.zeros((vocab_rows, depth - embed_size - 2), jnp.float32),
        ],
        axis=1,
    )
    rec_sum, in_out, emb_out, clip = run_reduce(
        lax.axis_size("group") // 2,
        lax.axis_size("dp"),
        embed_size,
        kept_all.reshape(positions, hidden_size),
        embedded_one.reshape(positions, depth),
        pre_all.reshape(positions, 4 * units),
        in_own,
        char_major.reshape(1, positions),
        extra,
        dec_sum,
    )
    token_count = seg_len * batch_size * lax.axis_size("group") * lax.axis_size("dp")
    grad_rec, next_rec, losses, *small = run_update(
        token_count,
        clip,
        rec_sum,
        in_out,
        emb_out,
        dec_sum,
        (
            mom_rec,
            jnp.transpose(mom_in, (1, 0, 2)),
            mom_bias,
            jnp.transpose(mom_dec, (2, 0, 1)),
            jnp.transpose(mom_emb, (1, 0, 2)),
            mom_dbias,
        ),
    )
    grad_in, next_in, grad_bias, next_bias, grad_dec, next_dec = small[:6]
    grad_emb, next_emb, grad_dbias, next_dbias = small[6:]
    return (
        losses[0, :1],
        word_vectors,
        grad_hidden0[None],
        grad_cell0[None],
        jnp.transpose(grad_emb, (1, 0, 2)),
        jnp.transpose(grad_in, (1, 0, 2)),
        grad_rec,
        grad_bias,
        jnp.transpose(grad_dec, (1, 2, 0)),
        grad_dbias,
        jnp.transpose(next_emb, (1, 0, 2)),
        jnp.transpose(next_in, (1, 0, 2)),
        next_rec,
        next_bias,
        jnp.transpose(next_dec, (1, 2, 0)),
        next_dbias,
    )


def solution(mesh):
    segments = P("dir", ("group", "dp"), None)
    shared = P("dir", None, None)
    columns = P("dir", None, "group")
    rows = P("dir", "group", None)
    flat = P("dir", "group")
    return jax.shard_map(
        shards,
        mesh=mesh,
        in_specs=(
            segments,
            segments,
            segments,
            segments,
            segments,
            segments,
            P(("group", "dp"), None, "dir"),
            shared,
            columns,
            rows,
            flat,
            rows,
            P("dir", None),
            shared,
            columns,
            rows,
            flat,
            rows,
            P("dir", None),
        ),
        out_specs=(
            P("dir"),
            P(("group", "dp"), "dir", None),
            segments,
            segments,
            shared,
            columns,
            rows,
            flat,
            rows,
            P("dir", None),
            shared,
            columns,
            rows,
            flat,
            rows,
            P("dir", None),
        ),
        check_vma=False,
    )
```
